32 devices in a mesh: dp: 16 (over z, x, core), tensor: 2 (over y).
Axes of the slice: x: 2, y: 2, z: 4, core: 2. Of those that a mesh axis runs over, the one named last changes fastest.
Arguments:
- tokens: bfloat16 [4096, 1536], P('dp'), may hold values from -6 to 6
- cotangent: bfloat16 [4096, 1536], P('dp'), may hold values from -6 to 6
- document_numbers: int32 [4096], P('dp'), may hold values from 0 to 3, as said below
- valid: int32 [4096], P('dp'), may hold values from 0 to 1, as said below
- routes: int32 [4096, 8], P('dp'), may hold values from 0 to 15, all different within a row; in each aligned block of 256 rows (0 to 255, 256 to 511, ...) at most 160 rows name the same one
- gain_attn: float32 [1536], replicated, may hold values from 0.5 to 1.5
- gain_moe: float32 [1536], replicated, may hold values from 0.5 to 1.5
- w_query: bfloat16 [1536, 1536], P(None, 'tensor'), may hold values from -0.3125 to 0.3125
- key_weight: bfloat16 [1536, 512], P(None, 'tensor'), may hold values from -0.15625 to 0.15625
- value_weight: bfloat16 [1536, 512], P(None, 'tensor'), may hold values from -0.15625 to 0.15625
- w_out: bfloat16 [1536, 1536], P('tensor'), may hold values from -0.875 to 0.875
- w_router: bfloat16 [1536, 16], replicated, may hold values from -0.078125 to 0.078125
- w_gate: bfloat16 [16, 1536, 512], P(None, None, 'tensor'), may hold values from -0.15625 to 0.15625
- w_up: bfloat16 [16, 1536, 512], P(None, None, 'tensor'), may hold values from -0.15625 to 0.15625
- w_down: bfloat16 [16, 512, 1536], P(None, 'tensor'), may hold values from -2 to 2
Outputs:
- output: bfloat16 [4096, 1536], P('dp')
- d_tokens: bfloat16 [4096, 1536], P('dp')
- d_gain_attn: float32 [1536], P('dp')
- d_gain_moe: float32 [1536], P('dp')
- d_query: float32 [1536, 1536], P('dp', 'tensor')
- d_key: float32 [1536, 512], P('dp', 'tensor')
- d_value: float32 [1536, 512], P('dp', 'tensor')
- d_out: float32 [1536, 1536], P('tensor', 'dp')
- d_router: float32 [1536, 16], P('dp')
- d_gate: float32 [16, 1536, 512], P(None, 'dp', 'tensor')
- d_up: float32 [16, 1536, 512], P(None, 'dp', 'tensor')
- d_down: float32 [16, 512, 1536], P(None, 'tensor', 'dp')
The draws below stay inside these ranges and needn't reach their ends.
Inputs may be any that keep to these rules, and one draw needn't show every extreme that they name: `document_numbers`: within each packed row of 2048 tokens the ids never fall; id 3 marks exactly the tokens where valid is 0. `valid`: padding stands only at the end of a packed row, and every row has some. `routes`: each row names 8 different experts. Among the 256 rows of one index of dp no expert is named more than 160 times, a bound that some block reaches.
All inputs are finite; a program needn't handle non-finite values.
Results may differ from the reference program's by a relative error of at most 0.024.
Values may be sent and summed in bfloat16 or wider, within the bound.
A program may use at most 320 MiB of HBM per device.

```python
import math
from functools import partial
import jax
import jax.numpy as jnp
import numpy as np
from jax import lax

MODEL_WIDTH = 1536
QUERY_HEADS = 24
KEY_VALUE_HEADS = 8
HEAD_SIZE = 64
FF = 512
TOP = 8
EXPERTS = 16
TOK_DEV = 256
ROW_LENGTH = 2048
WINDOW = 1024
CAP = 160
TOKEN_COUNT = 4096


def document_bounds(key):
    packed_rows = TOKEN_COUNT // ROW_LENGTH
    first_key, second_key, third_key = jax.random.split(key, 3)
    first_cut = jax.random.randint(first_key, (packed_rows, 1), 1, TOK_DEV // 2 + 1)
    second_cut = jax.random.randint(second_key, (packed_rows, 1), ROW_LENGTH - TOK_DEV // 2, ROW_LENGTH - TOK_DEV // 4)
    padding = jax.random.randint(third_key, (packed_rows, 1), 1, TOK_DEV // 8 + 1)
    places = jnp.arange(ROW_LENGTH, dtype=jnp.int32)[None, :]
    return (first_cut, second_cut, ROW_LENGTH - padding, places)


def draw_document_numbers(key, part):
    first_cut, second_cut, pad_start, places = document_bounds(key)
    ids = (places >= first_cut).astype(jnp.int32) + (places >= second_cut).astype(jnp.int32) + (places >= pad_start).astype(jnp.int32)
    return ids.reshape(-1)


def draw_valid(key, part):
    first_cut, second_cut, pad_start, places = document_bounds(key)
    return (places < pad_start).astype(jnp.int32).reshape(-1)


def raised(drawn, own_key, source, target, shards_of, factor):
    def block_of(position):
        return (jnp.arange(drawn.shape[position]) // (drawn.shape[position] // shards_of)).reshape((-1,) + (1,) * (drawn.ndim - 1 - position))

    first = jax.random.permutation(own_key, shards_of)[block_of(target)]
    far = (block_of(target) + shards_of // 2) % shards_of
    return jnp.where((block_of(source) == first) | (block_of(source) == far), factor * drawn, drawn)


def block_scale(stream_key, extent, cuts, least, largest):
    factor_of, own = 1.0, jax.random.fold_in(stream_key, 6)
    for position, parts in cuts:
        steps = jnp.exp(jax.random.uniform(jax.random.fold_in(own, position), (parts,), jnp.float32, least / len(cuts), largest / len(cuts)))
        factor_of = factor_of * jnp.repeat(steps, extent[position] // parts).reshape([-1 if axis == position else 1 for axis in range(len(extent))])
    return factor_of


def shared_out(stream_key, own, number, rows, count, top, reach, skew):
    ranking = jax.random.permutation(stream_key, count)
    heavy_load, common = load_shares(count, rows * top, reach, skew, True), load_shares(count, rows * top, reach, skew, False)
    places = jnp.arange(count)

    def named(tallies, offset_by):
        used = int((tallies > 0).sum())
        fixed = max(1, used // 4)
        shifted = fixed + (places - fixed + offset_by * (used - fixed)) % max(1, count - fixed)
        return jnp.zeros((count,), jnp.int32).at[ranking[jnp.where(places < fixed, places, shifted)]].set(jnp.asarray(tallies, jnp.int32))

    tallies = jnp.where(number % 4 == 0, named(heavy_load, number // 4), named(common, number - number // 4 - 1))
    mixed = jax.random.permutation(jax.random.fold_in(own, 3), count)
    donor, taker = mixed[0:count // 2 * 2:2], mixed[1:count // 2 * 2:2]
    room = jnp.minimum(tallies[donor] - 1, reach - tallies[taker]) // 2
    room = jnp.where((donor == ranking[0]) | (taker == ranking[0]) | (tallies[taker] == 0), 0, jnp.maximum(room, 0))
    shifted = jax.random.randint(jax.random.fold_in(own, 4), (count // 2,), 0, 1 << 20) % (room + 1)
    tallies = tallies.at[donor].add(-shifted).at[taker].add(shifted)
    members = jnp.searchsorted(jnp.cumsum(tallies), jnp.arange(rows * top), side="right").astype(jnp.int32)
    listing = members.reshape(top, rows).T
    listing = listing[jax.random.permutation(jax.random.fold_in(own, 1), rows)]
    offset_by = jax.random.randint(jax.random.fold_in(own, 2), (rows, 1), 0, top)
    return jnp.take_along_axis(listing, (jnp.arange(top)[None, :] + offset_by) % top, axis=1)


def load_shares(count, total, most, slope, full):
    portions = [(1 << 20) // math.isqrt(standing ** slope) + 1 for standing in range(1, count + 1)]
    largest = most if full else min(most, max(-(-total // count), total * portions[0] // sum(portions)))
    least = 1 if total - largest >= count - 1 else 0
    given, surplus = [largest] + [least] * (count - 1), total - largest - least * (count - 1)
    while surplus > 0:
        free = [i for i in range(1, count) if given[i] < largest] or [i for i in range(1, count) if given[i] < most]
        pool, remaining = sum([portions[i] for i in free]), surplus
        for i in free:
            addition = min(most - given[i], max(1, remaining * portions[i] // pool), surplus)
            given[i] = given[i] + addition
            surplus = surplus - addition
    return np.array(given)


def scatter_about(stream_key, extent, deviation, bound, shards=(), kind=jnp.bfloat16):
    array = deviation * jax.random.normal(stream_key, extent, jnp.float32)
    if shards:
        array = array * block_scale(stream_key, extent, shards, -0.22, 0.18)
    return jnp.clip(array, -bound, bound).astype(kind)


def bell_draw_with(rng, extent, deviation, most, cuts, heavy, kind=jnp.bfloat16):
    drawn = deviation * jax.random.normal(rng, extent, jnp.float32)
    if cuts:
        drawn = drawn * block_scale(rng, extent, cuts, -0.22, 0.18)
    return jnp.clip(raised(drawn, jax.random.fold_in(rng, 3), *heavy), -most, most).astype(kind)


def setup_inputs(seed: int = 0) -> dict:
    arg_keys = jax.random.split(jax.random.key(seed), 16)
    tokens = bell_draw_with(arg_keys[0], (TOKEN_COUNT, MODEL_WIDTH), 1.0, 6.0, ((0, 16),), (0, 1, 16, 2.0))
    cotangent = bell_draw_with(arg_keys[1], (TOKEN_COUNT, MODEL_WIDTH), 1.0, 6.0, ((0, 16),), (0, 1, 16, 2.0))
    document_numbers = draw_document_numbers(jax.random.fold_in(arg_keys[15], 71), 0)
    valid = draw_valid(jax.random.fold_in(arg_keys[15], 71), 0)
    routes_keys = jax.random.split(jax.random.fold_in(arg_keys[4], 1), TOKEN_COUNT // TOK_DEV)
    routes_turns = jax.random.permutation(jax.random.fold_in(arg_keys[4], 3), TOKEN_COUNT // TOK_DEV)
    routes = jax.vmap(lambda own, number: shared_out(jax.random.fold_in(arg_keys[4], 2), own, number, TOK_DEV, EXPERTS, TOP, CAP, 1))(routes_keys, routes_turns).reshape((TOKEN_COUNT, TOP))
    gain_attn = jnp.clip(1.0 + 0.1 * jax.random.normal(arg_keys[5], (MODEL_WIDTH,), jnp.float32), 0.5, 1.5)
    gain_moe = jnp.clip(1.0 + 0.1 * jax.random.normal(arg_keys[6], (MODEL_WIDTH,), jnp.float32), 0.5, 1.5)
    w_query = scatter_about(arg_keys[7], (MODEL_WIDTH, QUERY_HEADS * HEAD_SIZE), (MODEL_WIDTH // 4) ** -0.5, 0.3125, ((1, 2),))
    key_weight = scatter_about(arg_keys[8], (MODEL_WIDTH, KEY_VALUE_HEADS * HEAD_SIZE), MODEL_WIDTH ** -0.5, 0.15625, ((1, 2),))
    value_weight = scatter_about(arg_keys[9], (MODEL_WIDTH, KEY_VALUE_HEADS * HEAD_SIZE), MODEL_WIDTH ** -0.5, 0.15625, ((1, 2),))
    w_out = scatter_about(arg_keys[10], (QUERY_HEADS * HEAD_SIZE, MODEL_WIDTH), (max(1, QUERY_HEADS * HEAD_SIZE // 32)) ** -0.5, 0.875, ((0, 2),))
    w_router = scatter_about(arg_keys[11], (MODEL_WIDTH, EXPERTS), (4 * MODEL_WIDTH) ** -0.5, 0.078125)
    w_gate = scatter_about(arg_keys[12], (EXPERTS, MODEL_WIDTH, FF), MODEL_WIDTH ** -0.5, 0.15625, ((2, 2),))
    w_up = scatter_about(arg_keys[13], (EXPERTS, MODEL_WIDTH, FF), MODEL_WIDTH ** -0.5, 0.15625, ((2, 2),))
    w_down = scatter_about(arg_keys[14], (EXPERTS, FF, MODEL_WIDTH), (max(1, FF // 64)) ** -0.5, 2.0, ((1, 2),))
    return {"tokens": tokens, "cotangent": cotangent, "document_numbers": document_numbers, "valid": valid, "routes": routes, "gain_attn": gain_attn, "gain_moe": gain_moe, "w_query": w_query, "key_weight": key_weight, "value_weight": value_weight, "w_out": w_out, "w_router": w_router, "w_gate": w_gate, "w_up": w_up, "w_down": w_down}


@jax.custom_vjp
def reduced_precision(v):
    return lax.optimization_barrier(v.astype(jnp.bfloat16)).astype(jnp.float32)

@jax.custom_vjp
def reduced_precision_backward(v):
    return v

def low_keep(v):
    return (reduced_precision(v), None)

def low_pass(kept, grad):
    return (grad,)

def back_keep(v):
    return (v, None)

def back_low(kept, grad):
    return (reduced_precision(grad),)
reduced_precision.defvjp(low_keep, low_pass)
reduced_precision_backward.defvjp(back_keep, back_low)
norm_eps = 1e-06
rope_base = 10000.0
masked_score = -1e+30

def matrix_product(left, right):
    return jnp.dot(left, right, precision=lax.Precision.HIGHEST)

def rms_scale(value_rows, gain):
    inverse = lax.rsqrt(lax.optimization_barrier(jnp.mean(value_rows * value_rows, axis=-1, keepdims=True)) + norm_eps)
    return value_rows * inverse * gain

def rotary_apply(value_rows, cosine_table, sine_table):
    half = value_rows.shape[-1] // 2
    first = value_rows[..., :half]
    second = value_rows[..., half:]
    return jnp.concatenate([first * cosine_table - second * sine_table, second * cosine_table + first * sine_table], axis=-1)

def silu(value_rows):
    return value_rows * jax.nn.sigmoid(value_rows)

def route_tables(routes, experts, capacity):
    flat_routes = routes.reshape(-1)
    total = flat_routes.shape[0]
    order = jnp.argsort(flat_routes, stable=True).astype(jnp.int32)
    sorted_experts = flat_routes[order]
    matches = (flat_routes[:, None] == jnp.arange(experts, dtype=jnp.int32)[None, :]).astype(jnp.int32)
    counts = lax.optimization_barrier(jnp.sum(matches, axis=0, dtype=jnp.int32))
    starts = jnp.cumsum(counts, dtype=jnp.int32) - counts
    ranks = jnp.arange(total, dtype=jnp.int32) - starts[sorted_experts]
    route_slot = jnp.zeros((total,), jnp.int32).at[order].set(sorted_experts * capacity + ranks)
    slot_route = jnp.zeros((experts * capacity,), jnp.int32).at[route_slot].set(jnp.arange(total, dtype=jnp.int32))
    slot_alive = jnp.zeros((experts * capacity,), jnp.int32).at[route_slot].set(1)
    return (route_slot, slot_route, slot_alive)

def attend_packed_row(operands):
    query_rows, key_rows, value_rows, segments = operands
    rows_per_block = min(512, ROW_LENGTH)
    key_places = jnp.arange(ROW_LENGTH, dtype=jnp.int32)

    def one_block(start):
        query_tile_block = lax.dynamic_slice_in_dim(query_rows, start, rows_per_block, 0)
        query_segments = lax.dynamic_slice_in_dim(segments, start, rows_per_block, 0)
        query_places = start + jnp.arange(rows_per_block, dtype=jnp.int32)
        grouped_heads = query_tile_block.reshape(rows_per_block, KEY_VALUE_HEADS, QUERY_HEADS // KEY_VALUE_HEADS, HEAD_SIZE)
        raw_scores = jnp.einsum('bkgd,lkd->kgbl', grouped_heads, key_rows, precision=lax.Precision.HIGHEST)
        distance = query_places[:, None] - key_places[None, :]
        allowed = (query_segments[:, None] == segments[None, :]) & (distance >= 0) & (distance < WINDOW)
        scores = reduced_precision_backward(jnp.where(allowed, raw_scores * HEAD_SIZE ** (-0.5), masked_score))
        row_max = lax.optimization_barrier(jnp.max(scores, axis=-1, keepdims=True))
        exp_scores = jnp.exp(scores - row_max)
        probs = exp_scores / lax.optimization_barrier(jnp.sum(exp_scores, axis=-1, keepdims=True))
        mixed_heads = jnp.einsum('kgbl,lkd->bkgd', reduced_precision(probs), value_rows, precision=lax.Precision.HIGHEST)
        return mixed_heads.reshape(rows_per_block, QUERY_HEADS * HEAD_SIZE)
    starts = jnp.arange(0, ROW_LENGTH, rows_per_block, dtype=jnp.int32)
    pieces = lax.map(jax.checkpoint(one_block), starts)
    return pieces.reshape(ROW_LENGTH, QUERY_HEADS * HEAD_SIZE)

def expert_block(w_gate, w_up, w_down, operands):
    normed_input, routes, gates = operands
    route_slot, slot_route, slot_alive = route_tables(routes, EXPERTS, CAP)
    slot_token = slot_route // TOP
    rows = normed_input[slot_token] * slot_alive.astype(jnp.float32)[:, None]
    rows = rows.reshape(EXPERTS, CAP, MODEL_WIDTH)
    gate_lin = reduced_precision_backward(jnp.einsum('ecd,edf->ecf', rows, w_gate, precision=lax.Precision.HIGHEST))
    up_lin = reduced_precision_backward(jnp.einsum('ecd,edf->ecf', rows, w_up, precision=lax.Precision.HIGHEST))
    hidden = reduced_precision(silu(gate_lin) * up_lin)
    expert_out = reduced_precision_backward(jnp.einsum('ecf,efd->ecd', hidden, w_down, precision=lax.Precision.HIGHEST))
    routed = expert_out.reshape(EXPERTS * CAP, MODEL_WIDTH)[route_slot].reshape(TOK_DEV, TOP, MODEL_WIDTH)
    return lax.optimization_barrier(jnp.sum(gates[:, :, None] * routed, axis=1))

def forward(tokens, gain_attn, gain_moe, w_query, key_weight, value_weight, w_out, w_router, w_gate, w_up, w_down, routes, document_numbers):
    packed_rows = TOKEN_COUNT // ROW_LENGTH
    blocks = TOKEN_COUNT // TOK_DEV
    normed_input = reduced_precision(rms_scale(tokens, gain_attn))
    places = jnp.arange(TOKEN_COUNT, dtype=jnp.int32) % ROW_LENGTH
    half = HEAD_SIZE // 2
    freqs = rope_base ** (-2.0 * jnp.arange(half, dtype=jnp.float32) / HEAD_SIZE)
    angle = places.astype(jnp.float32)[:, None] * freqs[None, :]
    cosine_table = jnp.cos(angle)[:, None, :]
    sine_table = jnp.sin(angle)[:, None, :]
    query_rows = reduced_precision(rotary_apply(reduced_precision_backward(matrix_product(normed_input, w_query)).reshape(TOKEN_COUNT, QUERY_HEADS, HEAD_SIZE), cosine_table, sine_table))
    key_rows = reduced_precision(rotary_apply(reduced_precision_backward(matrix_product(normed_input, key_weight)).reshape(TOKEN_COUNT, KEY_VALUE_HEADS, HEAD_SIZE), cosine_table, sine_table))
    value_rows = reduced_precision(reduced_precision_backward(matrix_product(normed_input, value_weight))).reshape(TOKEN_COUNT, KEY_VALUE_HEADS, HEAD_SIZE)
    mixed_heads = lax.map(attend_packed_row, (query_rows.reshape(packed_rows, ROW_LENGTH, QUERY_HEADS, HEAD_SIZE), key_rows.reshape(packed_rows, ROW_LENGTH, KEY_VALUE_HEADS, HEAD_SIZE), value_rows.reshape(packed_rows, ROW_LENGTH, KEY_VALUE_HEADS, HEAD_SIZE), document_numbers.reshape(packed_rows, ROW_LENGTH)))
    mixed_heads = reduced_precision_backward(reduced_precision(mixed_heads.reshape(TOKEN_COUNT, QUERY_HEADS * HEAD_SIZE)))
    middle = tokens + reduced_precision_backward(matrix_product(mixed_heads, w_out))
    normed_two = reduced_precision(rms_scale(middle, gain_moe))
    logits = reduced_precision_backward(matrix_product(normed_two, w_router))
    row_max = lax.optimization_barrier(jnp.max(logits, axis=-1, keepdims=True))
    exp_logits = jnp.exp(logits - row_max)
    router = exp_logits / lax.optimization_barrier(jnp.sum(exp_logits, axis=-1, keepdims=True))
    gates = jnp.take_along_axis(router, routes, axis=1)
    moe = lax.map(jax.checkpoint(partial(expert_block, w_gate, w_up, w_down)), (normed_two.reshape(blocks, TOK_DEV, MODEL_WIDTH), routes.reshape(blocks, TOK_DEV, TOP), gates.reshape(blocks, TOK_DEV, TOP)))
    return middle + moe.reshape(TOKEN_COUNT, MODEL_WIDTH)

def reference(tokens, cotangent, document_numbers, valid, routes, gain_attn, gain_moe, w_query, key_weight, value_weight, w_out, w_router, w_gate, w_up, w_down):

    def closed(tokens_f, gain_one, gain_two, query_f, key_f, value_f, out_f, router_f, gate_f, up_f, down_f):
        return forward(tokens_f, gain_one, gain_two, query_f, key_f, value_f, out_f, router_f, gate_f, up_f, down_f, routes, document_numbers)
    output, pullback = jax.vjp(closed, tokens.astype(jnp.float32), gain_attn.astype(jnp.float32), gain_moe.astype(jnp.float32), w_query.astype(jnp.float32), key_weight.astype(jnp.float32), value_weight.astype(jnp.float32), w_out.astype(jnp.float32), w_router.astype(jnp.float32), w_gate.astype(jnp.float32), w_up.astype(jnp.float32), w_down.astype(jnp.float32))
    masked = cotangent.astype(jnp.float32) * valid.astype(jnp.float32)[:, None]
    grads = pullback(masked)
    return (output.astype(jnp.bfloat16), grads[0].astype(jnp.bfloat16), grads[1], grads[2], grads[3], grads[4], grads[5], grads[6], grads[7], grads[8], grads[9], grads[10])
```

```python
import jax
import jax.numpy as jnp
from jax import lax
from jax.sharding import PartitionSpec as P

HEAD_SIZE = 64
EXPERTS = 16
ROW_LENGTH = 2048
WINDOW = 1024


norm_eps = 1e-06
rope_base = 10000.0
masked_score = -1e30


def passed_along(block, axis, distance):
    devices = range(lax.axis_size(axis))
    route = [(i - distance, i) for i in devices if i - distance in devices]
    return lax.ppermute(block, axis, route)


def rms_forward(value_rows, gain):
    inverse = lax.rsqrt(jnp.mean(value_rows * value_rows, axis=-1, keepdims=True) + norm_eps)
    return (value_rows * inverse * gain, inverse)


def rms_backward(grad, value_rows, inverse, gain):
    scaled = grad * gain
    inner = jnp.mean(scaled * value_rows, axis=-1, keepdims=True)
    d_values = inverse * scaled - value_rows * inverse * inverse * inverse * inner
    return (d_values, jnp.sum(grad * value_rows * inverse, axis=0))


def rotary_apply(value_rows, cosine_table, sine_table):
    half = value_rows.shape[-1] // 2
    first = value_rows[..., :half]
    second = value_rows[..., half:]
    return jnp.concatenate(
        [first * cosine_table - second * sine_table, second * cosine_table + first * sine_table],
        axis=-1,
    )


def silu(value_rows):
    return value_rows * jax.nn.sigmoid(value_rows)


def member_groups(axis):
    size = lax.axis_size(axis)
    return [[r * EXPERTS + m for m in range(EXPERTS)] for r in range(size // EXPERTS)]


def cross_groups(axis):
    size = lax.axis_size(axis)
    return [[r * EXPERTS + m for r in range(size // EXPERTS)] for m in range(EXPERTS)]


def gathered(block):
    return lax.all_gather(
        block, "dp", axis=0, tiled=True, axis_index_groups=member_groups("dp")
    )


def spread_rows(grad):
    size = lax.axis_size("dp")
    if size > EXPERTS:
        grad = lax.psum_scatter(
            grad, "dp", scatter_dimension=0, tiled=True, axis_index_groups=cross_groups("dp")
        )
    grad = grad.astype(jnp.bfloat16)
    rows = grad.shape[0] // EXPERTS
    grad = grad.reshape(EXPERTS, rows, grad.shape[1])
    return lax.all_to_all(
        grad, "dp", 0, 0, tiled=True, axis_index_groups=member_groups("dp")
    )


def window_piece(key_rows, value_rows, tags, distance):
    return passed_along((key_rows, value_rows, tags), "dp", distance)


def returned_piece(key_part, value_part, distance):
    return (
        passed_along(key_part.astype(jnp.bfloat16), "dp", -distance).astype(key_part.dtype),
        passed_along(value_part.astype(jnp.bfloat16), "dp", -distance).astype(value_part.dtype),
    )


def per_device(
    tokens,
    cotangent,
    document_numbers,
    valid,
    routes,
    gain_attn,
    gain_moe,
    w_query,
    key_weight,
    value_weight,
    w_out,
    w_router,
    w_gate,
    w_up,
    w_down,
):
    f32 = jnp.float32
    bf16 = jnp.bfloat16
    rows_dev = tokens.shape[0]
    width = tokens.shape[1]
    q_heads = w_query.shape[1] // HEAD_SIZE
    kv_heads = key_weight.shape[1] // HEAD_SIZE
    group = q_heads // kv_heads
    reach = (WINDOW + rows_dev - 1) // rows_dev
    scale = HEAD_SIZE ** (-0.5)
    device = lax.axis_index("dp")
    token_places = device * rows_dev + jnp.arange(rows_dev, dtype=jnp.int32)
    positions = token_places % ROW_LENGTH
    source = tokens.astype(f32)
    normed_f, inverse_one = rms_forward(source, gain_attn)
    normed_input = normed_f.astype(bf16)
    query_lin = jnp.dot(normed_input, w_query, preferred_element_type=f32)
    key_lin = jnp.dot(normed_input, key_weight, preferred_element_type=f32)
    value_lin = jnp.dot(normed_input, value_weight, preferred_element_type=f32)
    half = HEAD_SIZE // 2
    freqs = rope_base ** (-2.0 * jnp.arange(half, dtype=f32) / HEAD_SIZE)
    angle = positions.astype(f32)[:, None] * freqs[None, :]
    cosine_table = jnp.cos(angle)[:, None, :]
    sine_table = jnp.sin(angle)[:, None, :]
    query_rows = rotary_apply(
        query_lin.reshape(rows_dev, q_heads, HEAD_SIZE), cosine_table, sine_table
    ).astype(bf16)
    key_rows = rotary_apply(
        key_lin.reshape(rows_dev, kv_heads, HEAD_SIZE), cosine_table, sine_table
    ).astype(bf16)
    value_rows = value_lin.astype(bf16).reshape(rows_dev, kv_heads, HEAD_SIZE)
    tags = document_numbers.astype(bf16)
    key_list = []
    value_list = []
    tag_list = []
    for distance in range(reach, 0, -1):
        far_keys, far_values, far_tags = window_piece(key_rows, value_rows, tags, distance)
        key_list.append(far_keys)
        value_list.append(far_values)
        tag_list.append(far_tags)
    all_keys = jnp.concatenate(key_list + [key_rows], axis=0)
    all_values = jnp.concatenate(value_list + [value_rows], axis=0)
    all_tags = jnp.concatenate(tag_list + [tags], axis=0).astype(jnp.int32)
    key_places = (device - reach) * rows_dev + jnp.arange(all_keys.shape[0], dtype=jnp.int32)
    distance_grid = token_places[:, None] - key_places[None, :]
    allowed = (
        (token_places[:, None] // ROW_LENGTH == key_places[None, :] // ROW_LENGTH)
        & (document_numbers[:, None] == all_tags[None, :])
        & (distance_grid >= 0)
        & (distance_grid < WINDOW)
    )
    grouped_heads = query_rows.reshape(rows_dev, kv_heads, group, HEAD_SIZE)
    raw_scores = jnp.einsum("tkgd,skd->kgts", grouped_heads, all_keys, preferred_element_type=f32)
    scores = jnp.where(allowed, raw_scores * scale, masked_score)
    row_max = jnp.max(scores, axis=-1, keepdims=True)
    exp_scores = jnp.exp(scores - row_max)
    row_total = jnp.sum(exp_scores, axis=-1, keepdims=True)
    probs = exp_scores / row_total
    log_total = row_max + jnp.log(row_total)
    mixed_heads = jnp.einsum(
        "kgts,skd->tkgd", probs.astype(bf16), all_values, preferred_element_type=f32
    )
    mixed_b = mixed_heads.reshape(rows_dev, q_heads * HEAD_SIZE).astype(bf16)
    attn_part = jnp.dot(mixed_b, w_out, preferred_element_type=f32)
    middle = source + lax.psum(attn_part.astype(jnp.bfloat16), "tensor").astype(jnp.float32)
    normed_two_f, inverse_two = rms_forward(middle, gain_moe)
    normed_two = normed_two_f.astype(bf16)
    logits = jnp.dot(normed_two, w_router, preferred_element_type=f32)
    logit_max = jnp.max(logits, axis=-1, keepdims=True)
    exp_logits = jnp.exp(logits - logit_max)
    router = exp_logits / jnp.sum(exp_logits, axis=-1, keepdims=True)
    picked = (routes[:, :, None] == jnp.arange(EXPERTS, dtype=jnp.int32)[None, None, :]).astype(f32)
    gate_table = jnp.sum(picked * router[:, None, :], axis=1)
    grad_b = cotangent * valid.astype(bf16)[:, None]
    grad_out = grad_b.astype(f32)
    gate_lin = jnp.einsum("td,edf->etf", normed_two, w_gate, preferred_element_type=f32)
    up_lin = jnp.einsum("td,edf->etf", normed_two, w_up, preferred_element_type=f32)
    pulled = jnp.einsum("td,efd->etf", grad_b, w_down, preferred_element_type=f32)
    column = gate_table.T[:, :, None]
    gate_sigmoid = jax.nn.sigmoid(gate_lin)
    activated = gate_lin * gate_sigmoid
    hidden = activated * up_lin
    prob_grad_part = jnp.sum(hidden * pulled, axis=-1).T
    scaled_hidden = (column * hidden).astype(bf16)
    moe_part = jnp.einsum("etf,efd->td", scaled_hidden, w_down, preferred_element_type=f32)
    hidden_grad = column * pulled
    gate_grad = (
        hidden_grad * up_lin * gate_sigmoid * (1.0 + gate_lin * (1.0 - gate_sigmoid))
    ).astype(bf16)
    up_grad = (hidden_grad * activated).astype(bf16)
    token_grad_part = jnp.einsum("etf,edf->td", gate_grad, w_gate, preferred_element_type=f32)
    token_grad_part = token_grad_part + jnp.einsum(
        "etf,edf->td", up_grad, w_up, preferred_element_type=f32
    )
    moe = lax.psum(moe_part.astype(jnp.bfloat16), "tensor").astype(jnp.float32)
    output = (middle + moe).astype(bf16)
    expert = lax.rem(device, EXPERTS)
    all_h2 = gathered(normed_two)
    all_dy = gathered(grad_b)
    all_gates = gathered(gate_table)
    own_column = lax.dynamic_index_in_dim(all_gates, expert, 1, keepdims=True)
    own_gate = lax.dynamic_index_in_dim(w_gate, expert, 0, keepdims=False)
    own_up = lax.dynamic_index_in_dim(w_up, expert, 0, keepdims=False)
    own_down = lax.dynamic_index_in_dim(w_down, expert, 0, keepdims=False)
    g_all = jnp.dot(all_h2, own_gate, preferred_element_type=f32)
    u_all = jnp.dot(all_h2, own_up, preferred_element_type=f32)
    p_all = jnp.einsum("td,fd->tf", all_dy, own_down, preferred_element_type=f32)
    s_all = jax.nn.sigmoid(g_all)
    a_all = g_all * s_all
    hc_all = (own_column * a_all * u_all).astype(bf16)
    hg_all = own_column * p_all
    dg_all = (hg_all * u_all * s_all * (1.0 + g_all * (1.0 - s_all))).astype(bf16)
    du_all = (hg_all * a_all).astype(bf16)
    sum_down = spread_rows(jnp.einsum("td,tf->df", all_dy, hc_all, preferred_element_type=f32))
    sum_gate = spread_rows(jnp.einsum("td,tf->df", all_h2, dg_all, preferred_element_type=f32))
    sum_up = spread_rows(jnp.einsum("td,tf->df", all_h2, du_all, preferred_element_type=f32))
    sum_down = jnp.swapaxes(sum_down, 1, 2).astype(f32)
    sum_gate = sum_gate.astype(f32)
    sum_up = sum_up.astype(f32)
    gate_grad_all, token_grad = (
        lax.psum(prob_grad_part, "tensor"),
        lax.psum(token_grad_part.astype(jnp.bfloat16), "tensor").astype(jnp.float32),
    )
    prob_grad = jnp.where(jnp.sum(picked, axis=1) > 0, gate_grad_all, 0.0)
    logit_grad = router * (prob_grad - jnp.sum(prob_grad * router, axis=-1, keepdims=True))
    logit_grad_b = logit_grad.astype(bf16)
    d_router = jnp.einsum("td,te->de", normed_two, logit_grad_b, preferred_element_type=f32)
    normed_two_grad = token_grad + jnp.einsum(
        "te,de->td", logit_grad_b, w_router, preferred_element_type=f32
    )
    middle_norm_grad, d_gain_moe = rms_backward(normed_two_grad, middle, inverse_two, gain_moe)
    middle_grad = grad_out + middle_norm_grad
    attn_grad = middle_grad.astype(bf16)
    d_out = jnp.einsum("ta,td->ad", mixed_b, attn_grad, preferred_element_type=f32)
    mixed_grad = jnp.einsum("td,ad->ta", attn_grad, w_out, preferred_element_type=f32).astype(bf16)
    mixed_grad = mixed_grad.reshape(rows_dev, kv_heads, group, HEAD_SIZE)
    raw_again = jnp.einsum("tkgd,skd->kgts", grouped_heads, all_keys, preferred_element_type=f32)
    weights = jnp.exp(jnp.where(allowed, raw_again * scale, masked_score) - log_total)
    probs_grad = jnp.einsum("tkgd,skd->kgts", mixed_grad, all_values, preferred_element_type=f32)
    inner = jnp.sum(probs_grad * weights, axis=-1, keepdims=True)
    score_grad = (weights * (probs_grad - inner)).astype(bf16)
    query_grad = (
        jnp.einsum("kgts,skd->tkgd", score_grad, all_keys, preferred_element_type=f32) * scale
    )
    key_grad = (
        jnp.einsum("kgts,tkgd->skd", score_grad, grouped_heads, preferred_element_type=f32) * scale
    )
    value_grad = jnp.einsum(
        "kgts,tkgd->skd", weights.astype(bf16), mixed_grad, preferred_element_type=f32
    )
    own_start = reach * rows_dev
    key_total = key_grad[own_start : own_start + rows_dev]
    value_total = value_grad[own_start : own_start + rows_dev]
    for distance in range(1, reach + 1):
        begin = (reach - distance) * rows_dev
        key_back, value_back = returned_piece(
            key_grad[begin : begin + rows_dev], value_grad[begin : begin + rows_dev], distance
        )
        key_total = key_total + key_back
        value_total = value_total + value_back
    query_lin_grad = (
        rotary_apply(query_grad.reshape(rows_dev, q_heads, HEAD_SIZE), cosine_table, -sine_table)
        .astype(bf16)
        .reshape(rows_dev, q_heads * HEAD_SIZE)
    )
    key_lin_grad = (
        rotary_apply(key_total, cosine_table, -sine_table)
        .astype(bf16)
        .reshape(rows_dev, kv_heads * HEAD_SIZE)
    )
    value_lin_grad = value_total.astype(bf16).reshape(rows_dev, kv_heads * HEAD_SIZE)
    d_query = jnp.einsum("td,ta->da", normed_input, query_lin_grad, preferred_element_type=f32)
    d_key = jnp.einsum("td,ta->da", normed_input, key_lin_grad, preferred_element_type=f32)
    d_value = jnp.einsum("td,ta->da", normed_input, value_lin_grad, preferred_element_type=f32)
    normed_grad_part = jnp.einsum("ta,da->td", query_lin_grad, w_query, preferred_element_type=f32)
    normed_grad_part = normed_grad_part + jnp.einsum(
        "ta,da->td", key_lin_grad, key_weight, preferred_element_type=f32
    )
    normed_grad_part = normed_grad_part + jnp.einsum(
        "ta,da->td", value_lin_grad, value_weight, preferred_element_type=f32
    )
    normed_grad = lax.psum(normed_grad_part.astype(jnp.bfloat16), "tensor").astype(jnp.float32)
    token_norm_grad, d_gain_attn = rms_backward(normed_grad, source, inverse_one, gain_attn)
    d_tokens = (middle_grad + token_norm_grad).astype(bf16)
    dense = jnp.concatenate([d_query, d_key, d_value, d_out.T], axis=1).astype(bf16)
    dense = lax.psum_scatter(dense, "dp", scatter_dimension=0, tiled=True).astype(f32)
    q_width, kv_width = q_heads * HEAD_SIZE, kv_heads * HEAD_SIZE
    sum_query = dense[:, :q_width]
    sum_key = dense[:, q_width : q_width + kv_width]
    sum_value = dense[:, q_width + kv_width : q_width + 2 * kv_width]
    sum_out = dense[:, q_width + 2 * kv_width :].T
    small = jnp.concatenate([d_router, d_gain_attn[:, None], d_gain_moe[:, None]], axis=1)
    small = lax.psum_scatter(small, "dp", scatter_dimension=0, tiled=True)
    sum_router = small[:, :EXPERTS]
    sum_gain_attn = small[:, EXPERTS]
    sum_gain_moe = small[:, EXPERTS + 1]
    return (
        output,
        d_tokens,
        sum_gain_attn,
        sum_gain_moe,
        sum_query,
        sum_key,
        sum_value,
        sum_out,
        sum_router,
        sum_gate,
        sum_up,
        sum_down,
    )


def solution(mesh):
    in_specs = (
        P("dp", None),
        P("dp", None),
        P("dp"),
        P("dp"),
        P("dp", None),
        P(),
        P(),
        P(None, "tensor"),
        P(None, "tensor"),
        P(None, "tensor"),
        P("tensor", None),
        P(),
        P(None, None, "tensor"),
        P(None, None, "tensor"),
        P(None, "tensor", None),
    )
    out_specs = (
        P("dp", None),
        P("dp", None),
        P("dp"),
        P("dp"),
        P("dp", "tensor"),
        P("dp", "tensor"),
        P("dp", "tensor"),
        P("tensor", "dp"),
        P("dp", None),
        P(None, "dp", "tensor"),
        P(None, "dp", "tensor"),
        P(None, "tensor", "dp"),
    )
    return jax.shard_map(
        per_device, mesh=mesh, in_specs=in_specs, out_specs=out_specs, check_vma=False
    )
```

```python
import jax
import jax.numpy as jnp
from jax import lax
from jax.experimental import pallas as pl
from jax.experimental.pallas import tpu as pltpu
from jax.sharding import PartitionSpec as P

HEAD_SIZE = 64
EXPERTS = 16
ROW_LENGTH = 2048
WINDOW = 1024


norm_eps = 1e-06
rope_base = 10000.0
masked_score = -1e30


MESH = pl.DeviceIdType.MESH
f32 = jnp.float32
bf16 = jnp.bfloat16
LINE = 4
VMEM_LIMIT = 60 * 2**20
def dot_nn(a,b): return lax.dot_general(a,b,(((1,),(0,)),((),())),preferred_element_type=f32)
def dot_nt(a,b): return lax.dot_general(a,b,(((1,),(1,)),((),())),preferred_element_type=f32)

def place():
    dp=lax.axis_index("dp"); t=lax.axis_index("tensor")
    m=lax.rem(dp,EXPERTS); base=dp-m
    a=m//4; b=lax.rem(m//2,2); c=lax.rem(m,2)
    return base,a,b,c,t

def near(a,j):
    low=(a<2).astype(jnp.int32)
    z=a*low+(3-a)*(1-low)
    o=j+z*((j==0)*1-(j==1)*1)
    return o*low+(3-o)*(1-low)

class Gather:
    def __init__(self, buf, sems, halves):
        self.buf=buf; self.recv,self.up,self.dn,self.bx,self.cx=sems
        self.halves=halves
        self.rows=buf.shape[1]//halves
        self.base,self.a,self.b,self.c,self.t=place()
    def slot(self,a,b,c): return a*4+b*2+c
    def ref(self,s,h): return self.buf.at[s,pl.ds(h*self.rows,self.rows)]
    def copy(self,s,h,sem,a,b,c):
        return pltpu.make_async_remote_copy(src_ref=self.ref(s,h),dst_ref=self.ref(s,h),send_sem=sem,recv_sem=self.recv.at[s,h],
            device_id=(self.base+self.slot(a,b,c),self.t),device_id_type=MESH)
    def wait_recv(self,s,h):
        self.copy(s,h,self.cx.at[0,h],self.a,self.b,1-self.c).wait_recv()
    def event(self,j,h):
        a,b,c=self.a,self.b,self.c
        z=near(a,j); s=self.slot(z,b,c)
        if not (isinstance(j,int) and j==0): self.wait_recv(s,h)
        @pl.when((z<=a)&(a<LINE-1))
        def _(): self.copy(s,h,self.up.at[j,h],a+1,b,c).start()
        @pl.when((z>=a)&(a>0))
        def _(): self.copy(s,h,self.dn.at[j,h],a-1,b,c).start()
        self.copy(s,h,self.bx.at[j,h],a,1-b,c).start()
        self.copy(s,h,self.cx.at[j,h],a,b,1-c).start()
    def xevent(self,j,h):
        a,b,c=self.a,self.b,self.c
        s=self.slot(near(a,j),1-b,c)
        self.wait_recv(s,h)
        self.copy(s,h,self.cx.at[LINE+j,h],a,b,1-c).start()
    def from_core(self,j,h):
        z=near(self.a,j)
        self.wait_recv(self.slot(z,self.b,1-self.c),h)
    def from_core_x(self,j,h):
        z=near(self.a,j)
        self.wait_recv(self.slot(z,1-self.b,1-self.c),h)
    def finish(self):
        a,b,c=self.a,self.b,self.c
        for j in range(LINE):
            z=near(a,j); s=self.slot(z,b,c)
            for h in range(self.halves):
                @pl.when((z<=a)&(a<LINE-1))
                def _(): self.copy(s,h,self.up.at[j,h],a+1,b,c).wait_send()
                @pl.when((z>=a)&(a>0))
                def _(): self.copy(s,h,self.dn.at[j,h],a-1,b,c).wait_send()
                self.copy(s,h,self.bx.at[j,h],a,1-b,c).wait_send()
                self.copy(s,h,self.cx.at[j,h],a,b,1-c).wait_send()
                self.copy(s,h,self.cx.at[LINE+j,h],a,b,1-c).wait_send()

def gather_sems(halves):
    return [pltpu.SemaphoreType.DMA((EXPERTS,halves)),pltpu.SemaphoreType.DMA((LINE,halves)),pltpu.SemaphoreType.DMA((LINE,halves)),
            pltpu.SemaphoreType.DMA((LINE,halves)),pltpu.SemaphoreType.DMA((2*LINE,halves))]

def enter(with_y):
    base,a,b,c,t=place()
    bar=pltpu.get_barrier_semaphore()
    def sig(a2,b2,c2,t2): pl.semaphore_signal(bar,inc=1,device_id=(base+a2*4+b2*2+c2,t2),device_id_type=MESH)
    @pl.when(a<LINE-1)
    def _(): sig(a+1,b,c,t)
    @pl.when(a>0)
    def _(): sig(a-1,b,c,t)
    sig(a,1-b,c,t); sig(a,b,1-c,t)
    n=2
    if with_y: sig(a,b,c,1-t); n=3
    ends=(a==0).astype(jnp.int32)+(a==LINE-1).astype(jnp.int32)
    pl.semaphore_wait(bar,n+2-ends)


def moe_kernel(
    h2_ref, dy_ref, cg_ref, ct_ref, middle_ref, wg_ref, wu_ref, wd_ref, dyall_ref,
    output_ref, dh2_ref, dprob_ref, grads_ref,
    h2all, ctall, gbuf, ubuf, dbuf, wgt, wut, wdo, dybuf, cat, acco, acch, accp, accg, accu, accd,
    ysend, yrecv, precv, wsem, lsem, dysem, yss, yrs, *sems,
):
    tokens = h2_ref.shape[0]
    gather = Gather(h2all, sems[:5], 2)
    gates = Gather(ctall, sems[5:], 1)
    base, a, b, c, t = place()
    me = a * 4 + b * 2 + c
    copies = [
        pltpu.make_async_copy(h2_ref, h2all.at[me], lsem.at[0]),
        pltpu.make_async_copy(ct_ref, ctall.at[me], lsem.at[1]),
    ]
    for copy in copies:
        copy.start()

    def weights(e, k):
        sides = ((wg_ref, gbuf), (wu_ref, ubuf), (wd_ref, dbuf))
        return [
            pltpu.make_async_copy(src.at[e], dst.at[k], wsem.at[i, k])
            for i, (src, dst) in enumerate(sides)
        ]

    for copy in weights(0, 0):
        copy.start()
    enter(True)
    for copy in copies:
        copy.wait()
    for h in range(2):
        gather.event(0, h)
    gates.event(0, 0)
    acco[...] = jnp.zeros_like(acco)
    acch[...] = jnp.zeros_like(acch)
    accp[...] = jnp.zeros_like(accp)
    accg[...] = jnp.zeros_like(accg)
    accu[...] = jnp.zeros_like(accu)
    accd[...] = jnp.zeros_like(accd)
    lanes = lax.broadcasted_iota(jnp.int32, (tokens, 128), 1)

    def one_expert(e, carry):
        k = lax.rem(e, 2)

        @pl.when(e < EXPERTS - 1)
        def _():
            for copy in weights(e + 1, 1 - k):
                copy.start()

        for copy in weights(e, k):
            copy.wait()

        @pl.when(e == me)
        def _():
            wgt[...] = gbuf[k].T
            wut[...] = ubuf[k].T
            wdo[...] = dbuf[k]

        own = h2all[me]
        g = dot_nn(own, gbuf[k])
        u = dot_nn(own, ubuf[k])
        p = dot_nt(dy_ref[...], dbuf[k])
        column = jnp.sum(jnp.where(lanes == e, cg_ref[...], 0.0), axis=1, keepdims=True)
        s = 1.0 / (1.0 + jnp.exp(-g))
        act = g * s
        hidden = act * u
        accp[...] += jnp.where(lanes == e, jnp.sum(hidden * p, axis=1, keepdims=True), 0.0)
        hc = (column * hidden).astype(bf16)
        hg = column * p
        dg = (hg * u * s * (1.0 + g * (1.0 - s))).astype(bf16)
        du = (hg * act).astype(bf16)
        acco[...] += dot_nn(hc, dbuf[k])
        acch[...] += dot_nt(dg, gbuf[k]) + dot_nt(du, ubuf[k])

        @pl.when(e == 5)
        def _():
            gather.event(1, 0)
            gather.xevent(0, 0)
            gates.event(1, 0)
            gates.xevent(0, 0)

        @pl.when(e == 9)
        def _():
            gather.event(1, 1)
            gather.xevent(0, 1)
            gates.event(2, 0)
            gates.xevent(1, 0)

        @pl.when(e == 13)
        def _():
            gather.event(2, 0)
            gather.xevent(1, 0)
            gates.event(3, 0)
            gates.xevent(2, 0)

        return carry

    lax.fori_loop(0, EXPERTS, one_expert, 0)

    other = (base + me, 1 - t)
    ysend[0] = acco[...].astype(bf16)
    ysend[1] = acch[...].astype(bf16)
    swaps = [
        pltpu.make_async_remote_copy(
            ysend.at[i], yrecv.at[i], yss.at[i], yrs.at[i], device_id=other, device_id_type=MESH
        )
        for i in range(2)
    ] + [
        pltpu.make_async_remote_copy(
            accp, precv, yss.at[2], yrs.at[2], device_id=other, device_id_type=MESH
        )
    ]
    swaps[1].start()
    swaps[2].start()
    swaps[0].start()
    gates.xevent(3, 0)

    def pair(k):
        j = k // 2
        side = lax.rem(b + lax.rem(k, 2), 2)
        return near(a, j) * 2 + side

    def dy_copy(k):
        slot = lax.rem(k, 2)
        return pltpu.make_async_copy(dyall_ref.at[pair(k)], dybuf.at[slot], dysem.at[slot])

    dy_copy(0).start()

    def one_pair(k, carry):
        @pl.when(k < 7)
        def _():
            dy_copy(k + 1).start()

        @pl.when(k == 1)
        def _():
            gather.event(2, 1)
            gather.xevent(1, 1)

        @pl.when(k == 3)
        def _():
            gather.event(3, 0)
            gather.xevent(2, 0)

        @pl.when(k == 4)
        def _():
            gather.event(3, 1)
            gather.xevent(2, 1)

        @pl.when(k == 6)
        def _():
            gather.xevent(3, 0)

        @pl.when(k == 7)
        def _():
            gather.xevent(3, 1)

        j = k // 2

        @pl.when(lax.rem(k, 2) == 0)
        def _():
            for h in range(2):
                gather.from_core(j, h)
            gates.from_core(j, 0)

        @pl.when(lax.rem(k, 2) == 1)
        def _():
            for h in range(2):
                gather.from_core_x(j, h)
            gates.from_core_x(j, 0)

        dy_copy(k).wait()
        at = pair(k)
        slot = lax.rem(k, 2)
        for q in range(2):
            h = h2all[2 * at + q]
            d = dybuf[slot, q * tokens : (q + 1) * tokens]
            g = dot_nt(wgt[...], h)
            u = dot_nt(wut[...], h)
            p = dot_nt(wdo[...], d)
            row = ctall[2 * at + q, pl.ds(me, 1), :]
            s = 1.0 / (1.0 + jnp.exp(-g))
            act = g * s
            hidden = act * u
            hg = row * p
            cols = slice(q * tokens, (q + 1) * tokens)
            cat[0, :, cols] = (row * hidden).astype(bf16)
            cat[1, :, cols] = (hg * u * s * (1.0 + g * (1.0 - s))).astype(bf16)
            cat[2, :, cols] = (hg * act).astype(bf16)
        both = h2all[pl.ds(2 * at, 2)].reshape(2 * tokens, h2all.shape[2])
        accd[...] += dot_nn(cat[0], dybuf[slot])
        accg[...] += dot_nn(cat[1], both)
        accu[...] += dot_nn(cat[2], both)
        return carry

    lax.fori_loop(0, 8, one_pair, 0)
    grads_ref[0] = accd[...].astype(bf16).T
    grads_ref[1] = accg[...].astype(bf16).T
    grads_ref[2] = accu[...].astype(bf16).T
    for copy in swaps:
        copy.wait()
    dprob_ref[...] = accp[...] + precv[...]
    dh2_ref[...] = ysend[1].astype(f32) + yrecv[1].astype(f32)
    total = ysend[0].astype(f32) + yrecv[0].astype(f32)
    output_ref[...] = (middle_ref[...] + total).astype(bf16)
    gather.finish()
    gates.finish()


def moe_call(h2, dy, cg, ct, middle, wg, wu, wd, dyall):
    tokens, width = h2.shape
    ff = wg.shape[2]
    vmem = pl.BlockSpec(memory_space=pltpu.VMEM)
    hbm = pl.BlockSpec(memory_space=pl.ANY)
    shape = jax.ShapeDtypeStruct
    dma = pltpu.SemaphoreType.DMA
    return pl.pallas_call(
        moe_kernel,
        out_shape=(
            shape((tokens, width), bf16),
            shape((tokens, width), f32),
            shape((tokens, 128), f32),
            shape((3, width, ff), bf16),
        ),
        in_specs=[hbm, vmem, vmem, hbm, vmem, hbm, hbm, hbm, hbm],
        out_specs=(vmem, vmem, vmem, vmem),
        scratch_shapes=[
            pltpu.VMEM((EXPERTS, tokens, width), bf16),
            pltpu.VMEM((EXPERTS, EXPERTS, tokens), f32),
            pltpu.VMEM((2, width, ff), bf16),
            pltpu.VMEM((2, width, ff), bf16),
            pltpu.VMEM((2, ff, width), bf16),
            pltpu.VMEM((ff, width), bf16),
            pltpu.VMEM((ff, width), bf16),
            pltpu.VMEM((ff, width), bf16),
            pltpu.VMEM((2, 2 * tokens, width), bf16),
            pltpu.VMEM((3, ff, 2 * tokens), bf16),
            pltpu.VMEM((tokens, width), f32),
            pltpu.VMEM((tokens, width), f32),
            pltpu.VMEM((tokens, 128), f32),
            pltpu.VMEM((ff, width), f32),
            pltpu.VMEM((ff, width), f32),
            pltpu.VMEM((ff, width), f32),
            pltpu.VMEM((2, tokens, width), bf16),
            pltpu.VMEM((2, tokens, width), bf16),
            pltpu.VMEM((tokens, 128), f32),
            dma((3, 2)),
            dma((2,)),
            dma((2,)),
            dma((3,)),
            dma((3,)),
        ]
        + gather_sems(2)
        + gather_sems(1),
        compiler_params=pltpu.CompilerParams(
            collective_id=0, has_side_effects=True, vmem_limit_bytes=VMEM_LIMIT
        ),
        name="moe",
    )(h2, dy, cg, ct, middle, wg, wu, wd, dyall)


def passed_along(block, axis, distance):
    devices = range(lax.axis_size(axis))
    route = [(i - distance, i) for i in devices if i - distance in devices]
    return lax.ppermute(block, axis, route)


def rms_forward(value_rows, gain):
    inverse = lax.rsqrt(jnp.mean(value_rows * value_rows, axis=-1, keepdims=True) + norm_eps)
    return (value_rows * inverse * gain, inverse)


def rms_backward(grad, value_rows, inverse, gain):
    scaled = grad * gain
    inner = jnp.mean(scaled * value_rows, axis=-1, keepdims=True)
    d_values = inverse * scaled - value_rows * inverse * inverse * inverse * inner
    return (d_values, jnp.sum(grad * value_rows * inverse, axis=0))


def rotary_apply(value_rows, cosine_table, sine_table):
    half = value_rows.shape[-1] // 2
    first = value_rows[..., :half]
    second = value_rows[..., half:]
    return jnp.concatenate(
        [first * cosine_table - second * sine_table, second * cosine_table + first * sine_table],
        axis=-1,
    )


def silu(value_rows):
    return value_rows * jax.nn.sigmoid(value_rows)


def member_groups(axis):
    size = lax.axis_size(axis)
    return [[r * EXPERTS + m for m in range(EXPERTS)] for r in range(size // EXPERTS)]


def cross_groups(axis):
    size = lax.axis_size(axis)
    return [[r * EXPERTS + m for r in range(size // EXPERTS)] for m in range(EXPERTS)]


def gathered(block):
    return lax.all_gather(
        block, "dp", axis=0, tiled=True, axis_index_groups=member_groups("dp")
    )


def spread_rows(grad):
    size = lax.axis_size("dp")
    if size > EXPERTS:
        grad = lax.psum_scatter(
            grad, "dp", scatter_dimension=0, tiled=True, axis_index_groups=cross_groups("dp")
        )
    grad = grad.astype(jnp.bfloat16)
    rows = grad.shape[0] // EXPERTS
    grad = grad.reshape(EXPERTS, rows, grad.shape[1])
    return lax.all_to_all(
        grad, "dp", 0, 0, tiled=True, axis_index_groups=member_groups("dp")
    )


def window_piece(key_rows, value_rows, tags, distance):
    return passed_along((key_rows, value_rows, tags), "dp", distance)


def returned_piece(key_part, value_part, distance):
    return (
        passed_along(key_part.astype(jnp.bfloat16), "dp", -distance).astype(key_part.dtype),
        passed_along(value_part.astype(jnp.bfloat16), "dp", -distance).astype(value_part.dtype),
    )


def per_device(
    tokens,
    cotangent,
    document_numbers,
    valid,
    routes,
    gain_attn,
    gain_moe,
    w_query,
    key_weight,
    value_weight,
    w_out,
    w_router,
    w_gate,
    w_up,
    w_down,
):
    rows_dev = tokens.shape[0]
    width = tokens.shape[1]
    q_heads = w_query.shape[1] // HEAD_SIZE
    kv_heads = key_weight.shape[1] // HEAD_SIZE
    group = q_heads // kv_heads
    reach = (WINDOW + rows_dev - 1) // rows_dev
    scale = HEAD_SIZE ** (-0.5)
    device = lax.axis_index("dp")
    token_places = device * rows_dev + jnp.arange(rows_dev, dtype=jnp.int32)
    positions = token_places % ROW_LENGTH
    source = tokens.astype(f32)
    normed_f, inverse_one = rms_forward(source, gain_attn)
    normed_input = normed_f.astype(bf16)
    query_lin = jnp.dot(normed_input, w_query, preferred_element_type=f32)
    key_lin = jnp.dot(normed_input, key_weight, preferred_element_type=f32)
    value_lin = jnp.dot(normed_input, value_weight, preferred_element_type=f32)
    half = HEAD_SIZE // 2
    freqs = rope_base ** (-2.0 * jnp.arange(half, dtype=f32) / HEAD_SIZE)
    angle = positions.astype(f32)[:, None] * freqs[None, :]
    cosine_table = jnp.cos(angle)[:, None, :]
    sine_table = jnp.sin(angle)[:, None, :]
    query_rows = rotary_apply(
        query_lin.reshape(rows_dev, q_heads, HEAD_SIZE), cosine_table, sine_table
    ).astype(bf16)
    key_rows = rotary_apply(
        key_lin.reshape(rows_dev, kv_heads, HEAD_SIZE), cosine_table, sine_table
    ).astype(bf16)
    value_rows = value_lin.astype(bf16).reshape(rows_dev, kv_heads, HEAD_SIZE)
    tags = document_numbers.astype(bf16)
    key_list = []
    value_list = []
    tag_list = []
    for distance in range(reach, 0, -1):
        far_keys, far_values, far_tags = window_piece(key_rows, value_rows, tags, distance)
        key_list.append(far_keys)
        value_list.append(far_values)
        tag_list.append(far_tags)
    all_keys = jnp.concatenate(key_list + [key_rows], axis=0)
    all_values = jnp.concatenate(value_list + [value_rows], axis=0)
    all_tags = jnp.concatenate(tag_list + [tags], axis=0).astype(jnp.int32)
    key_places = (device - reach) * rows_dev + jnp.arange(all_keys.shape[0], dtype=jnp.int32)
    distance_grid = token_places[:, None] - key_places[None, :]
    allowed = (
        (token_places[:, None] // ROW_LENGTH == key_places[None, :] // ROW_LENGTH)
        & (document_numbers[:, None] == all_tags[None, :])
        & (distance_grid >= 0)
        & (distance_grid < WINDOW)
    )
    grouped_heads = query_rows.reshape(rows_dev, kv_heads, group, HEAD_SIZE)
    raw_scores = jnp.einsum("tkgd,skd->kgts", grouped_heads, all_keys, preferred_element_type=f32)
    scores = jnp.where(allowed, raw_scores * scale, masked_score)
    row_max = jnp.max(scores, axis=-1, keepdims=True)
    exp_scores = jnp.exp(scores - row_max)
    row_total = jnp.sum(exp_scores, axis=-1, keepdims=True)
    probs = exp_scores / row_total
    log_total = row_max + jnp.log(row_total)
    mixed_heads = jnp.einsum(
        "kgts,skd->tkgd", probs.astype(bf16), all_values, preferred_element_type=f32
    )
    mixed_b = mixed_heads.reshape(rows_dev, q_heads * HEAD_SIZE).astype(bf16)
    attn_part = jnp.dot(mixed_b, w_out, preferred_element_type=f32)
    middle = source + lax.psum(attn_part.astype(jnp.bfloat16), "tensor").astype(jnp.float32)
    normed_two_f, inverse_two = rms_forward(middle, gain_moe)
    normed_two = normed_two_f.astype(bf16)
    logits = jnp.dot(normed_two, w_router, preferred_element_type=f32)
    logit_max = jnp.max(logits, axis=-1, keepdims=True)
    exp_logits = jnp.exp(logits - logit_max)
    router = exp_logits / jnp.sum(exp_logits, axis=-1, keepdims=True)
    picked = (routes[:, :, None] == jnp.arange(EXPERTS, dtype=jnp.int32)[None, None, :]).astype(f32)
    gate_table = jnp.sum(picked * router[:, None, :], axis=1)
    grad_b = cotangent * valid.astype(bf16)[:, None]
    grad_out = grad_b.astype(f32)
    all_dy = gathered(grad_b).reshape(EXPERTS // 2, 2 * rows_dev, width)
    padded = jnp.pad(gate_table, ((0, 0), (0, 128 - EXPERTS)))
    output, token_grad, gate_grad_all, grads = moe_call(
        normed_two, grad_b, padded, gate_table.T, middle, w_gate, w_up, w_down, all_dy
    )
    gate_grad_all = gate_grad_all[:, :EXPERTS]
    sum_down, sum_gate, sum_up = [spread_rows(grads[i]) for i in range(3)]
    sum_down = jnp.swapaxes(sum_down, 1, 2).astype(f32)
    sum_gate = sum_gate.astype(f32)
    sum_up = sum_up.astype(f32)
    prob_grad = jnp.where(jnp.sum(picked, axis=1) > 0, gate_grad_all, 0.0)
    logit_grad = router * (prob_grad - jnp.sum(prob_grad * router, axis=-1, keepdims=True))
    logit_grad_b = logit_grad.astype(bf16)
    d_router = jnp.einsum("td,te->de", normed_two, logit_grad_b, preferred_element_type=f32)
    normed_two_grad = token_grad + jnp.einsum(
        "te,de->td", logit_grad_b, w_router, preferred_element_type=f32
    )
    middle_norm_grad, d_gain_moe = rms_backward(normed_two_grad, middle, inverse_two, gain_moe)
    middle_grad = grad_out + middle_norm_grad
    attn_grad = middle_grad.astype(bf16)
    d_out = jnp.einsum("ta,td->ad", mixed_b, attn_grad, preferred_element_type=f32)
    mixed_grad = jnp.einsum("td,ad->ta", attn_grad, w_out, preferred_element_type=f32).astype(bf16)
    mixed_grad = mixed_grad.reshape(rows_dev, kv_heads, group, HEAD_SIZE)
    raw_again = jnp.einsum("tkgd,skd->kgts", grouped_heads, all_keys, preferred_element_type=f32)
    weights = jnp.exp(jnp.where(allowed, raw_again * scale, masked_score) - log_total)
    probs_grad = jnp.einsum("tkgd,skd->kgts", mixed_grad, all_values, preferred_element_type=f32)
    inner = jnp.sum(probs_grad * weights, axis=-1, keepdims=True)
    score_grad = (weights * (probs_grad - inner)).astype(bf16)
    query_grad = (
        jnp.einsum("kgts,skd->tkgd", score_grad, all_keys, preferred_element_type=f32) * scale
    )
    key_grad = (
        jnp.einsum("kgts,tkgd->skd", score_grad, grouped_heads, preferred_element_type=f32) * scale
    )
    value_grad = jnp.einsum(
        "kgts,tkgd->skd", weights.astype(bf16), mixed_grad, preferred_element_type=f32
    )
    own_start = reach * rows_dev
    key_total = key_grad[own_start : own_start + rows_dev]
    value_total = value_grad[own_start : own_start + rows_dev]
    for distance in range(1, reach + 1):
        begin = (reach - distance) * rows_dev
        key_back, value_back = returned_piece(
            key_grad[begin : begin + rows_dev], value_grad[begin : begin + rows_dev], distance
        )
        key_total = key_total + key_back
        value_total = value_total + value_back
    query_lin_grad = (
        rotary_apply(query_grad.reshape(rows_dev, q_heads, HEAD_SIZE), cosine_table, -sine_table)
        .astype(bf16)
        .reshape(rows_dev, q_heads * HEAD_SIZE)
    )
    key_lin_grad = (
        rotary_apply(key_total, cosine_table, -sine_table)
        .astype(bf16)
        .reshape(rows_dev, kv_heads * HEAD_SIZE)
    )
    value_lin_grad = value_total.astype(bf16).reshape(rows_dev, kv_heads * HEAD_SIZE)
    d_query = jnp.einsum("td,ta->da", normed_input, query_lin_grad, preferred_element_type=f32)
    d_key = jnp.einsum("td,ta->da", normed_input, key_lin_grad, preferred_element_type=f32)
    d_value = jnp.einsum("td,ta->da", normed_input, value_lin_grad, preferred_element_type=f32)
    normed_grad_part = jnp.einsum("ta,da->td", query_lin_grad, w_query, preferred_element_type=f32)
    normed_grad_part = normed_grad_part + jnp.einsum(
        "ta,da->td", key_lin_grad, key_weight, preferred_element_type=f32
    )
    normed_grad_part = normed_grad_part + jnp.einsum(
        "ta,da->td", value_lin_grad, value_weight, preferred_element_type=f32
    )
    normed_grad = lax.psum(normed_grad_part.astype(jnp.bfloat16), "tensor").astype(jnp.float32)
    token_norm_grad, d_gain_attn = rms_backward(normed_grad, source, inverse_one, gain_attn)
    d_tokens = (middle_grad + token_norm_grad).astype(bf16)
    dense = jnp.concatenate([d_query, d_key, d_value, d_out.T], axis=1).astype(bf16)
    dense = lax.psum_scatter(dense, "dp", scatter_dimension=0, tiled=True).astype(f32)
    q_width, kv_width = q_heads * HEAD_SIZE, kv_heads * HEAD_SIZE
    sum_query = dense[:, :q_width]
    sum_key = dense[:, q_width : q_width + kv_width]
    sum_value = dense[:, q_width + kv_width : q_width + 2 * kv_width]
    sum_out = dense[:, q_width + 2 * kv_width :].T
    small = jnp.concatenate([d_router, d_gain_attn[:, None], d_gain_moe[:, None]], axis=1)
    small = lax.psum_scatter(small, "dp", scatter_dimension=0, tiled=True)
    sum_router = small[:, :EXPERTS]
    sum_gain_attn = small[:, EXPERTS]
    sum_gain_moe = small[:, EXPERTS + 1]
    return (
        output,
        d_tokens,
        sum_gain_attn,
        sum_gain_moe,
        sum_query,
        sum_key,
        sum_value,
        sum_out,
        sum_router,
        sum_gate,
        sum_up,
        sum_down,
    )


def solution(mesh):
    in_specs = (
        P("dp", None),
        P("dp", None),
        P("dp"),
        P("dp"),
        P("dp", None),
        P(),
        P(),
        P(None, "tensor"),
        P(None, "tensor"),
        P(None, "tensor"),
        P("tensor", None),
        P(),
        P(None, None, "tensor"),
        P(None, None, "tensor"),
        P(None, "tensor", None),
    )
    out_specs = (
        P("dp", None),
        P("dp", None),
        P("dp"),
        P("dp"),
        P("dp", "tensor"),
        P("dp", "tensor"),
        P("dp", "tensor"),
        P("tensor", "dp"),
        P("dp", None),
        P(None, "dp", "tensor"),
        P(None, "dp", "tensor"),
        P(None, "tensor", "dp"),
    )
    return jax.shard_map(
        per_device, mesh=mesh, in_specs=in_specs, out_specs=out_specs, check_vma=False
    )
```

```python
import jax
import jax.numpy as jnp
from jax import lax
from jax.experimental import pallas as pl
from jax.experimental.pallas import tpu as pltpu
from jax.sharding import PartitionSpec as P

HEAD_SIZE = 64
EXPERTS = 16
ROW_LENGTH = 2048
WINDOW = 1024
norm_eps = 1e-06
rope_base = 10000.0
masked_score = -1e30
MESH = pl.DeviceIdType.MESH
f32 = jnp.float32
bf16 = jnp.bfloat16
LINE = 4
VMEM_LIMIT = 60 * 2**20


def dot_nn(a,b): return lax.dot_general(a,b,(((1,),(0,)),((),())),preferred_element_type=f32)
def dot_nt(a,b): return lax.dot_general(a,b,(((1,),(1,)),((),())),preferred_element_type=f32)

def place():
    dp=lax.axis_index("dp"); t=lax.axis_index("tensor")
    m=lax.rem(dp,EXPERTS); base=dp-m
    a=m//4; b=lax.rem(m//2,2); c=lax.rem(m,2)
    return base,a,b,c,t

def near(a,j):
    low=(a<2).astype(jnp.int32)
    z=a*low+(3-a)*(1-low)
    o=j+z*((j==0)*1-(j==1)*1)
    return o*low+(3-o)*(1-low)

class Gather:
    def __init__(self, buf, sems, halves):
        self.buf=buf; self.recv,self.up,self.dn,self.bx,self.cx=sems
        self.halves=halves
        self.rows=buf.shape[1]//halves
        self.base,self.a,self.b,self.c,self.t=place()
    def slot(self,a,b,c): return a*4+b*2+c
    def ref(self,s,h): return self.buf.at[s,pl.ds(h*self.rows,self.rows)]
    def copy(self,s,h,sem,a,b,c):
        return pltpu.make_async_remote_copy(src_ref=self.ref(s,h),dst_ref=self.ref(s,h),send_sem=sem,recv_sem=self.recv.at[s,h],
            device_id=(self.base+self.slot(a,b,c),self.t),device_id_type=MESH)
    def wait_recv(self,s,h):
        self.copy(s,h,self.cx.at[0,h],self.a,self.b,1-self.c).wait_recv()
    def event(self,j,h):
        a,b,c=self.a,self.b,self.c
        z=near(a,j); s=self.slot(z,b,c)
        if not (isinstance(j,int) and j==0): self.wait_recv(s,h)
        @pl.when((z<=a)&(a<LINE-1))
        def _(): self.copy(s,h,self.up.at[j,h],a+1,b,c).start()
        @pl.when((z>=a)&(a>0))
        def _(): self.copy(s,h,self.dn.at[j,h],a-1,b,c).start()
        self.copy(s,h,self.bx.at[j,h],a,1-b,c).start()
        self.copy(s,h,self.cx.at[j,h],a,b,1-c).start()
    def xevent(self,j,h):
        a,b,c=self.a,self.b,self.c
        s=self.slot(near(a,j),1-b,c)
        self.wait_recv(s,h)
        self.copy(s,h,self.cx.at[LINE+j,h],a,b,1-c).start()
    def from_core(self,j,h):
        z=near(self.a,j)
        self.wait_recv(self.slot(z,self.b,1-self.c),h)
    def from_core_x(self,j,h):
        z=near(self.a,j)
        self.wait_recv(self.slot(z,1-self.b,1-self.c),h)
    def finish(self):
        a,b,c=self.a,self.b,self.c
        for j in range(LINE):
            z=near(a,j); s=self.slot(z,b,c)
            for h in range(self.halves):
                @pl.when((z<=a)&(a<LINE-1))
                def _(): self.copy(s,h,self.up.at[j,h],a+1,b,c).wait_send()
                @pl.when((z>=a)&(a>0))
                def _(): self.copy(s,h,self.dn.at[j,h],a-1,b,c).wait_send()
                self.copy(s,h,self.bx.at[j,h],a,1-b,c).wait_send()
                self.copy(s,h,self.cx.at[j,h],a,b,1-c).wait_send()
                self.copy(s,h,self.cx.at[LINE+j,h],a,b,1-c).wait_send()

def gather_sems(halves):
    return [pltpu.SemaphoreType.DMA((EXPERTS,halves)),pltpu.SemaphoreType.DMA((LINE,halves)),pltpu.SemaphoreType.DMA((LINE,halves)),
            pltpu.SemaphoreType.DMA((LINE,halves)),pltpu.SemaphoreType.DMA((2*LINE,halves))]

def enter(with_y,more=0):
    base,a,b,c,t=place()
    bar=pltpu.get_barrier_semaphore()
    def sig(a2,b2,c2,t2): pl.semaphore_signal(bar,inc=1,device_id=(base+a2*4+b2*2+c2,t2),device_id_type=MESH)
    @pl.when(a<LINE-1)
    def _(): sig(a+1,b,c,t)
    @pl.when(a>0)
    def _(): sig(a-1,b,c,t)
    sig(a,1-b,c,t); sig(a,b,1-c,t)
    n=2
    if with_y: sig(a,b,c,1-t); n=3
    ends=(a==0).astype(jnp.int32)+(a==LINE-1).astype(jnp.int32)
    pl.semaphore_wait(bar,n+2-ends+more)


def swapped(block):
    lane = lax.broadcasted_iota(jnp.int32, block.shape, 1)
    low = lax.rem(lane, HEAD_SIZE) < HEAD_SIZE // 2
    return jnp.where(low, pltpu.roll(block, 128 - HEAD_SIZE // 2, 1), pltpu.roll(block, HEAD_SIZE // 2, 1))


def rotated(rows, cosine, sine):
    pieces = []
    for i in range(rows.shape[1] // 128):
        block = rows[:, 128 * i : 128 * (i + 1)]
        pieces.append(block * cosine + swapped(block) * sine)
    return jnp.concatenate(pieces, axis=1)


def attn_kernel(
    x_ref, cot_ref, valid_ref, docrow_ref, doccol_ref, routes_ref, gain1_ref, gain2_ref,
    wq_ref, wk_ref, wv_ref, wo_ref, wr_ref, cos_ref, sin_ref,
    h2_ref, middle_ref, router_ref, gates_ref, gatest_ref, q_ref, kv_ref, lse_ref, mixed_ref, mixedt_ref,
    dy_ref, dyall_ref,
    dyall, kvbuf, wq, wo, kheads, vt, qheads, bias, mixedt, ysend, yrecv,
    wsem, osem, dsem, kvs, kvr, yss, yrs, *sems,
):
    tokens, width = x_ref.shape
    reach = kvbuf.shape[0] - 1
    row_blocks = ROW_LENGTH // tokens
    kv_width = wk_ref.shape[1]
    kv_heads = kv_width // HEAD_SIZE
    group = wq.shape[1] // kv_width
    gather = Gather(dyall, sems, 2)
    base, a, b, c, t = place()
    me = a * 4 + b * 2 + c
    dp = base + me
    at = lax.rem(dp, row_blocks)
    loads = [
        pltpu.make_async_copy(wq_ref, wq, wsem.at[0]),
        pltpu.make_async_copy(wo_ref, wo, wsem.at[1]),
    ]
    for copy in loads:
        copy.start()
    dy = (cot_ref[...].astype(f32) * valid_ref[...]).astype(bf16)
    dyall[me] = dy
    dy_ref[...] = dy

    barrier = pltpu.get_barrier_semaphore()
    for d in range(1, reach + 1):
        @pl.when(at + d < row_blocks)
        def _():
            pl.semaphore_signal(barrier, inc=1, device_id=(dp + d, t), device_id_type=MESH)

        @pl.when(at >= d)
        def _():
            pl.semaphore_signal(barrier, inc=1, device_id=(dp - d, t), device_id_type=MESH)

    peers = jnp.minimum(at, reach) + jnp.minimum(row_blocks - 1 - at, reach)
    enter(True, peers)
    for h in range(2):
        gather.event(0, h)

    x = x_ref[...].astype(f32)
    inverse = lax.rsqrt(jnp.mean(x * x, axis=1, keepdims=True) + norm_eps)
    h1 = (x * inverse * gain1_ref[...]).astype(bf16)
    cosine, sine = cos_ref[...], sin_ref[...]
    kvbuf[reach, :, :kv_width] = rotated(dot_nn(h1, wk_ref[...]), cosine, sine).astype(bf16)
    kvbuf[reach, :, kv_width : 2 * kv_width] = dot_nn(h1, wv_ref[...]).astype(bf16)
    kvbuf[reach, :, 2 * kv_width :] = jnp.broadcast_to(
        doccol_ref[...], (tokens, 128)
    ).astype(bf16)

    def halo(d):
        return pltpu.make_async_remote_copy(
            kvbuf.at[reach], kvbuf.at[reach - d], kvs.at[d - 1], kvr.at[d - 1],
            device_id=(dp + d, t), device_id_type=MESH,
        )

    for d in range(1, reach + 1):
        @pl.when(at + d < row_blocks)
        def _():
            halo(d).start()

        @pl.when(at < d)
        def _():
            kvbuf[reach - d] = jnp.zeros(kvbuf.shape[1:], bf16)

    loads[0].wait()
    q = rotated(dot_nn(h1, wq[...]), cosine, sine)
    q_ref[...] = q.astype(bf16)
    q = (q * HEAD_SIZE**-0.5).astype(bf16)
    for i in range(group * kv_heads):
        qheads[i] = q[:, HEAD_SIZE * i : HEAD_SIZE * (i + 1)]
    gather.event(1, 0)
    gather.xevent(0, 0)

    for d in range(reach, -1, -1):
        s = reach - d
        if d:
            @pl.when(at >= d)
            def _():
                halo(d).wait_recv()
        far = (
            lax.broadcasted_iota(jnp.int32, (tokens, tokens), 1)
            - lax.broadcasted_iota(jnp.int32, (tokens, tokens), 0)
            + d * tokens
        )
        tags = kvbuf[s, :, 2 * kv_width :].astype(f32)
        tags = jnp.concatenate([tags] * (tokens // 128), axis=1)
        allowed = (tags == docrow_ref[...]) & (far >= 0) & (far < WINDOW)
        allowed = allowed & (at >= d)
        rows = slice(s * tokens, (s + 1) * tokens)
        bias[rows] = jnp.where(allowed, 0.0, masked_score)
        for i in range(kv_heads):
            cols = slice(HEAD_SIZE * i, HEAD_SIZE * (i + 1))
            kheads[i, rows] = kvbuf[s, :, cols]
        v = kvbuf[s, :, kv_width : 2 * kv_width].T
        for i in range(kv_heads):
            vt[i, :, rows] = v[HEAD_SIZE * i : HEAD_SIZE * (i + 1)]

    def one_kv(i, carry):
        for n in range(group):
            head = i * group + n
            scores = dot_nt(kheads[i], qheads[head]) + bias[...]
            top = jnp.max(scores, axis=0, keepdims=True)
            weights = jnp.exp(scores - top)
            total = jnp.sum(weights, axis=0, keepdims=True)
            mixedt[head] = (dot_nn(vt[i], weights.astype(bf16)) / total).astype(bf16)
            lse_ref[pl.ds(head, 1), :] = top + jnp.log(total)
        return carry

    lax.fori_loop(0, kv_heads, one_kv, 0)
    mixed_t = mixedt[...].reshape(group * kv_width, tokens)
    mixedt_ref[...] = mixed_t
    mixed = mixed_t.T
    mixed_ref[...] = mixed
    loads[1].wait()
    ysend[...] = dot_nn(mixed, wo[...]).astype(bf16)
    swap = pltpu.make_async_remote_copy(
        ysend, yrecv, yss, yrs, device_id=(dp, 1 - t), device_id_type=MESH
    )
    swap.start()
    gather.event(1, 1)
    gather.xevent(0, 1)
    gather.event(2, 0)
    gather.xevent(1, 0)
    swap.wait()
    middle = x + (ysend[...].astype(f32) + yrecv[...].astype(f32))
    middle_ref[...] = middle
    inverse = lax.rsqrt(jnp.mean(middle * middle, axis=1, keepdims=True) + norm_eps)
    h2 = (middle * inverse * gain2_ref[...]).astype(bf16)
    h2_ref[...] = h2
    logits = dot_nn(h2, wr_ref[...])
    lanes = lax.broadcasted_iota(jnp.int32, (tokens, 128), 1)
    logits = jnp.where(lanes < EXPERTS, logits, masked_score)
    raised = jnp.exp(logits - jnp.max(logits, axis=1, keepdims=True))
    router = raised / jnp.sum(raised, axis=1, keepdims=True)
    router_ref[...] = router
    picked = jnp.zeros((tokens, 128), f32)
    for i in range(routes_ref.shape[1]):
        picked = picked + jnp.where(routes_ref[:, i : i + 1] == lanes, 1.0, 0.0)
    gates = router * picked
    gates_ref[...] = gates
    gatest_ref[...] = gates.T[:EXPERTS]
    for h in range(2):
        if h:
            gather.event(2, h)
            gather.xevent(1, h)
        gather.event(3, h)
        gather.xevent(2, h)
    for h in range(2):
        gather.xevent(3, h)
    for j in range(LINE):
        for h in range(2):
            gather.from_core(j, h)
            gather.from_core_x(j, h)
    outs = [
        pltpu.make_async_copy(dyall, dyall_ref, osem.at[0]),
        pltpu.make_async_copy(kvbuf, kv_ref, osem.at[1]),
    ]
    for copy in outs:
        copy.start()
    for d in range(1, reach + 1):
        @pl.when(at + d < row_blocks)
        def _():
            halo(d).wait_send()
    for copy in outs:
        copy.wait()
    gather.finish()


def attn_call(x, cot, valid, docrow, doccol, routes, gain1, gain2, wq, wk, wv, wo, wr, cosine, sine):
    tokens, width = x.shape
    q_width, kv_width = wq.shape[1], wk.shape[1]
    heads, kv_heads = q_width // HEAD_SIZE, kv_width // HEAD_SIZE
    reach = (WINDOW + tokens - 1) // tokens
    keys = (reach + 1) * tokens
    vmem = pl.BlockSpec(memory_space=pltpu.VMEM)
    hbm = pl.BlockSpec(memory_space=pl.ANY)
    shape = jax.ShapeDtypeStruct
    dma = pltpu.SemaphoreType.DMA
    return pl.pallas_call(
        attn_kernel,
        out_shape=(
            shape((tokens, width), bf16),
            shape((tokens, width), f32),
            shape((tokens, 128), f32),
            shape((tokens, 128), f32),
            shape((EXPERTS, tokens), f32),
            shape((tokens, q_width), bf16),
            shape((reach + 1, tokens, 2 * kv_width + 128), bf16),
            shape((16, tokens), f32),
            shape((tokens, q_width), bf16),
            shape((q_width, tokens), bf16),
            shape((tokens, width), bf16),
            shape((EXPERTS, tokens, width), bf16),
        ),
        in_specs=[vmem] * 8 + [hbm, vmem, vmem, hbm, vmem, vmem, vmem],
        out_specs=(vmem,) * 6 + (hbm, vmem, vmem, vmem, vmem, hbm),
        scratch_shapes=[
            pltpu.VMEM((EXPERTS, tokens, width), bf16),
            pltpu.VMEM((reach + 1, tokens, 2 * kv_width + 128), bf16),
            pltpu.VMEM((width, q_width), bf16),
            pltpu.VMEM((q_width, width), bf16),
            pltpu.VMEM((kv_heads, keys, HEAD_SIZE), bf16),
            pltpu.VMEM((kv_heads, HEAD_SIZE, keys), bf16),
            pltpu.VMEM((heads, tokens, HEAD_SIZE), bf16),
            pltpu.VMEM((keys, tokens), f32),
            pltpu.VMEM((heads, HEAD_SIZE, tokens), bf16),
            pltpu.VMEM((tokens, width), bf16),
            pltpu.VMEM((tokens, width), bf16),
            dma((2,)),
            dma((2,)),
            dma((2,)),
            dma((reach,)),
            dma((reach,)),
            dma,
            dma,
        ]
        + gather_sems(2),
        compiler_params=pltpu.CompilerParams(
            collective_id=1, has_side_effects=True, vmem_limit_bytes=VMEM_LIMIT
        ),
        name="attention",
    )(x, cot, valid, docrow, doccol, routes, gain1, gain2, wq, wk, wv, wo, wr, cosine, sine)


def moe_kernel(
    h2_ref, dy_ref, cg_ref, ct_ref, middle_ref, wg_ref, wu_ref, wd_ref, dyall_ref,
    output_ref, dh2_ref, dprob_ref, grads_ref,
    h2all, ctall, gbuf, ubuf, dbuf, wgt, wut, wdo, dybuf, cat, acco, acch, accp, accg, accu, accd,
    ysend, yrecv, precv, wsem, lsem, dysem, yss, yrs, *sems,
):
    tokens = h2_ref.shape[0]
    gather = Gather(h2all, sems[:5], 2)
    gates = Gather(ctall, sems[5:], 1)
    base, a, b, c, t = place()
    me = a * 4 + b * 2 + c
    copies = [
        pltpu.make_async_copy(h2_ref, h2all.at[me], lsem.at[0]),
        pltpu.make_async_copy(ct_ref, ctall.at[me], lsem.at[1]),
    ]
    for copy in copies:
        copy.start()

    def weights(e, k):
        sides = ((wg_ref, gbuf), (wu_ref, ubuf), (wd_ref, dbuf))
        return [
            pltpu.make_async_copy(src.at[e], dst.at[k], wsem.at[i, k])
            for i, (src, dst) in enumerate(sides)
        ]

    for copy in weights(0, 0):
        copy.start()
    enter(True)
    for copy in copies:
        copy.wait()
    for h in range(2):
        gather.event(0, h)
    gates.event(0, 0)
    acco[...] = jnp.zeros_like(acco)
    acch[...] = jnp.zeros_like(acch)
    accp[...] = jnp.zeros_like(accp)
    accg[...] = jnp.zeros_like(accg)
    accu[...] = jnp.zeros_like(accu)
    accd[...] = jnp.zeros_like(accd)
    lanes = lax.broadcasted_iota(jnp.int32, (tokens, 128), 1)

    def one_expert(e, carry):
        k = lax.rem(e, 2)

        @pl.when(e < EXPERTS - 1)
        def _():
            for copy in weights(e + 1, 1 - k):
                copy.start()

        for copy in weights(e, k):
            copy.wait()

        @pl.when(e == me)
        def _():
            wgt[...] = gbuf[k].T
            wut[...] = ubuf[k].T
            wdo[...] = dbuf[k]

        own = h2all[me]
        g = dot_nn(own, gbuf[k])
        u = dot_nn(own, ubuf[k])
        p = dot_nt(dy_ref[...], dbuf[k])
        column = jnp.sum(jnp.where(lanes == e, cg_ref[...], 0.0), axis=1, keepdims=True)
        s = 1.0 / (1.0 + jnp.exp(-g))
        act = g * s
        hidden = act * u
        accp[...] += jnp.where(lanes == e, jnp.sum(hidden * p, axis=1, keepdims=True), 0.0)
        hc = (column * hidden).astype(bf16)
        hg = column * p
        dg = (hg * u * s * (1.0 + g * (1.0 - s))).astype(bf16)
        du = (hg * act).astype(bf16)
        acco[...] += dot_nn(hc, dbuf[k])
        acch[...] += dot_nt(dg, gbuf[k]) + dot_nt(du, ubuf[k])

        @pl.when(e == 5)
        def _():
            gather.event(1, 0)
            gather.xevent(0, 0)
            gates.event(1, 0)
            gates.xevent(0, 0)

        @pl.when(e == 9)
        def _():
            gather.event(1, 1)
            gather.xevent(0, 1)
            gates.event(2, 0)
            gates.xevent(1, 0)

        @pl.when(e == 13)
        def _():
            gather.event(2, 0)
            gather.xevent(1, 0)
            gates.event(3, 0)
            gates.xevent(2, 0)

        return carry

    lax.fori_loop(0, EXPERTS, one_expert, 0)

    other = (base + me, 1 - t)
    ysend[0] = acco[...].astype(bf16)
    ysend[1] = acch[...].astype(bf16)
    swaps = [
        pltpu.make_async_remote_copy(
            ysend.at[i], yrecv.at[i], yss.at[i], yrs.at[i], device_id=other, device_id_type=MESH
        )
        for i in range(2)
    ] + [
        pltpu.make_async_remote_copy(
            accp, precv, yss.at[2], yrs.at[2], device_id=other, device_id_type=MESH
        )
    ]
    swaps[1].start()
    swaps[2].start()
    swaps[0].start()
    gates.xevent(3, 0)

    def pair(k):
        j = k // 2
        side = lax.rem(b + lax.rem(k, 2), 2)
        return near(a, j) * 2 + side

    def dy_copy(k):
        slot = lax.rem(k, 2)
        return pltpu.make_async_copy(dyall_ref.at[pair(k)], dybuf.at[slot], dysem.at[slot])

    dy_copy(0).start()

    def one_pair(k, carry):
        @pl.when(k < 7)
        def _():
            dy_copy(k + 1).start()

        @pl.when(k == 1)
        def _():
            gather.event(2, 1)
            gather.xevent(1, 1)

        @pl.when(k == 3)
        def _():
            gather.event(3, 0)
            gather.xevent(2, 0)

        @pl.when(k == 4)
        def _():
            gather.event(3, 1)
            gather.xevent(2, 1)

        @pl.when(k == 6)
        def _():
            gather.xevent(3, 0)

        @pl.when(k == 7)
        def _():
            gather.xevent(3, 1)

        j = k // 2

        @pl.when(lax.rem(k, 2) == 0)
        def _():
            for h in range(2):
                gather.from_core(j, h)
            gates.from_core(j, 0)

        @pl.when(lax.rem(k, 2) == 1)
        def _():
            for h in range(2):
                gather.from_core_x(j, h)
            gates.from_core_x(j, 0)

        dy_copy(k).wait()
        at = pair(k)
        slot = lax.rem(k, 2)
        for q in range(2):
            h = h2all[2 * at + q]
            d = dybuf[slot, q * tokens : (q + 1) * tokens]
            g = dot_nt(wgt[...], h)
            u = dot_nt(wut[...], h)
            p = dot_nt(wdo[...], d)
            row = ctall[2 * at + q, pl.ds(me, 1), :]
            s = 1.0 / (1.0 + jnp.exp(-g))
            act = g * s
            hidden = act * u
            hg = row * p
            cols = slice(q * tokens, (q + 1) * tokens)
            cat[0, :, cols] = (row * hidden).astype(bf16)
            cat[1, :, cols] = (hg * u * s * (1.0 + g * (1.0 - s))).astype(bf16)
            cat[2, :, cols] = (hg * act).astype(bf16)
        both = h2all[pl.ds(2 * at, 2)].reshape(2 * tokens, h2all.shape[2])
        accd[...] += dot_nn(cat[0], dybuf[slot])
        accg[...] += dot_nn(cat[1], both)
        accu[...] += dot_nn(cat[2], both)
        return carry

    lax.fori_loop(0, 8, one_pair, 0)
    grads_ref[0] = accd[...].astype(bf16).T
    grads_ref[1] = accg[...].astype(bf16).T
    grads_ref[2] = accu[...].astype(bf16).T
    for copy in swaps:
        copy.wait()
    dprob_ref[...] = accp[...] + precv[...]
    dh2_ref[...] = ysend[1].astype(f32) + yrecv[1].astype(f32)
    total = ysend[0].astype(f32) + yrecv[0].astype(f32)
    output_ref[...] = (middle_ref[...] + total).astype(bf16)
    gather.finish()
    gates.finish()


def moe_call(h2, dy, cg, ct, middle, wg, wu, wd, dyall):
    tokens, width = h2.shape
    ff = wg.shape[2]
    vmem = pl.BlockSpec(memory_space=pltpu.VMEM)
    hbm = pl.BlockSpec(memory_space=pl.ANY)
    shape = jax.ShapeDtypeStruct
    dma = pltpu.SemaphoreType.DMA
    return pl.pallas_call(
        moe_kernel,
        out_shape=(
            shape((tokens, width), bf16),
            shape((tokens, width), f32),
            shape((tokens, 128), f32),
            shape((3, width, ff), bf16),
        ),
        in_specs=[hbm, vmem, vmem, hbm, vmem, hbm, hbm, hbm, hbm],
        out_specs=(vmem, vmem, vmem, vmem),
        scratch_shapes=[
            pltpu.VMEM((EXPERTS, tokens, width), bf16),
            pltpu.VMEM((EXPERTS, EXPERTS, tokens), f32),
            pltpu.VMEM((2, width, ff), bf16),
            pltpu.VMEM((2, width, ff), bf16),
            pltpu.VMEM((2, ff, width), bf16),
            pltpu.VMEM((ff, width), bf16),
            pltpu.VMEM((ff, width), bf16),
            pltpu.VMEM((ff, width), bf16),
            pltpu.VMEM((2, 2 * tokens, width), bf16),
            pltpu.VMEM((3, ff, 2 * tokens), bf16),
            pltpu.VMEM((tokens, width), f32),
            pltpu.VMEM((tokens, width), f32),
            pltpu.VMEM((tokens, 128), f32),
            pltpu.VMEM((ff, width), f32),
            pltpu.VMEM((ff, width), f32),
            pltpu.VMEM((ff, width), f32),
            pltpu.VMEM((2, tokens, width), bf16),
            pltpu.VMEM((2, tokens, width), bf16),
            pltpu.VMEM((tokens, 128), f32),
            dma((3, 2)),
            dma((2,)),
            dma((2,)),
            dma((3,)),
            dma((3,)),
        ]
        + gather_sems(2)
        + gather_sems(1),
        compiler_params=pltpu.CompilerParams(
            collective_id=0, has_side_effects=True, vmem_limit_bytes=VMEM_LIMIT
        ),
        name="moe",
    )(h2, dy, cg, ct, middle, wg, wu, wd, dyall)


class Scatter:
    def __init__(self, bufs, sems):
        self.part, self.cbuf, self.keep, self.xbuf, self.last, self.zbuf = bufs
        self.csem, self.xsem, self.zsend, self.zrecv = sems
        self.base, self.a, self.b, self.c, self.t = place()

    def target(self, a, b, c):
        return (self.base + a * 4 + b * 2 + c, self.t)

    def core(self):
        return pltpu.make_async_remote_copy(
            self.part.at[:, 1 - self.c], self.cbuf, self.csem.at[0], self.csem.at[1],
            device_id=self.target(self.a, self.b, 1 - self.c), device_id_type=MESH,
        )

    def cross(self):
        return pltpu.make_async_remote_copy(
            self.keep.at[:, 1 - self.b], self.xbuf, self.xsem.at[0], self.xsem.at[1],
            device_id=self.target(self.a, 1 - self.b, self.c), device_id_type=MESH,
        )

    def along(self, k):
        z = lax.rem(self.a + k, LINE)
        return pltpu.make_async_remote_copy(
            self.last.at[z], self.zbuf.at[k - 1], self.zsend.at[k - 1], self.zrecv.at[k - 1],
            device_id=self.target(z, self.b, self.c), device_id_type=MESH,
        )

    def start(self):
        self.core().start()

    def second(self):
        self.core().wait()

        def add(i, carry):
            for j in range(2):
                mine = self.part[2 * i + j, self.c].astype(f32)
                self.keep[i, j] = (mine + self.cbuf[2 * i + j].astype(f32)).astype(bf16)
            return carry

        lax.fori_loop(0, LINE, add, 0)
        self.cross().start()

    def third(self):
        self.cross().wait()

        def add(i, carry):
            mine = self.keep[i, self.b].astype(f32)
            self.last[i] = (mine + self.xbuf[i].astype(f32)).astype(bf16)
            return carry

        lax.fori_loop(0, LINE, add, 0)
        for k in range(1, LINE):
            self.along(k).start()

    def total(self):
        result = self.last[self.a].astype(f32)
        for k in range(1, LINE):
            self.along(k).wait_recv()
            result = result + self.zbuf[k - 1].astype(f32)
        return result

    def finish(self):
        for k in range(1, LINE):
            self.along(k).wait_send()


def scatter_bufs(rows, columns):
    shapes = [(8, 2), (8,), (4, 2), (4,), (4,), (3,)]
    return [pltpu.VMEM(s + (rows, columns), bf16) for s in shapes]


def scatter_sems():
    dma = pltpu.SemaphoreType.DMA
    return [dma((2,)), dma((2,)), dma((LINE - 1,)), dma((LINE - 1,))]


def back_kernel(
    grads_ref, dh2_ref, dprob_ref, router_ref, routes_ref, h2_ref, middle_ref, x_ref, dy_ref,
    gain1_ref, gain2_ref, wr_ref, mixed_ref, mixedt_ref, q_ref, kv_ref, lse_ref, docrow_ref,
    cos_ref, sin_ref, wq_ref, wk_ref, wv_ref, wo_ref,
    dtok_ref, experts_ref, out_ref, query_ref, rest_ref,
    wq, wk, wv, kheads, vheads, kt, qstack, qt, dmixt, dmixstack, delta, bias, wcat, scat, dqt,
    sendkv, ownkv, retkv, rowst, mgrad, ysend, yrecv, gsend, grecv,
    wsem, asend, arecv, lsem, kvs, kvr, ysem, *rest,
):
    tokens, width = x_ref.shape
    reach = retkv.shape[0]
    row_blocks = ROW_LENGTH // tokens
    kv_width = wk_ref.shape[1]
    kv_heads = kv_width // HEAD_SIZE
    q_width = wq_ref.shape[1]
    group = q_width // kv_width
    rows = width // EXPERTS
    keys = (reach + 1) * tokens
    outs = Scatter(rest[0:6], rest[18:22])
    quer = Scatter(rest[6:12], rest[22:26])
    tail = Scatter(rest[12:18], rest[26:30])
    base, a, b, c, t = place()
    me = a * 4 + b * 2 + c
    dp = base + me
    at = lax.rem(dp, row_blocks)
    loads = [
        pltpu.make_async_copy(src, dst, wsem.at[i])
        for i, (src, dst) in enumerate(((wq_ref, wq), (wk_ref, wk), (wv_ref, wv)))
    ]
    for copy in loads:
        copy.start()
    barrier = pltpu.get_barrier_semaphore()

    def greet(k, carry):
        peer = base + lax.rem(me + k, EXPERTS)
        pl.semaphore_signal(barrier, inc=1, device_id=(peer, t), device_id_type=MESH)
        return carry

    lax.fori_loop(1, EXPERTS, greet, 0)
    pl.semaphore_signal(barrier, inc=1, device_id=(dp, 1 - t), device_id_type=MESH)
    pl.semaphore_wait(barrier, EXPERTS)

    def deal(k):
        peer = lax.rem(me + k, EXPERTS)
        return pltpu.make_async_remote_copy(
            grads_ref.at[:, peer], experts_ref.at[me], asend.at[k], arecv.at[k],
            device_id=(base + peer, t), device_id_type=MESH,
        )

    def deal_start(k, carry):
        deal(k).start()
        return carry

    lax.fori_loop(1, EXPERTS, deal_start, 0)
    own = pltpu.make_async_copy(grads_ref.at[:, me], experts_ref.at[me], lsem)
    own.start()

    lanes = lax.broadcasted_iota(jnp.int32, (tokens, 128), 1)
    picked = lanes < 0
    for i in range(routes_ref.shape[1]):
        picked = picked | (routes_ref[:, i : i + 1] == lanes)
    router = router_ref[...]
    dprob = jnp.where(picked, dprob_ref[...], 0.0)
    dlogits = router * (dprob - jnp.sum(dprob * router, axis=1, keepdims=True))
    dlogits = dlogits.astype(bf16)
    grad = dh2_ref[...] + dot_nt(dlogits, wr_ref[...])
    middle = middle_ref[...]
    inverse = lax.rsqrt(jnp.mean(middle * middle, axis=1, keepdims=True) + norm_eps)
    scaled = grad * gain2_ref[...]
    inner = jnp.mean(scaled * middle, axis=1, keepdims=True)
    normed = middle * inverse
    dgain2 = jnp.sum(grad * normed, axis=0, keepdims=True)
    middle_grad = dy_ref[...].astype(f32) + (
        inverse * scaled - normed * (inverse * inverse) * inner
    )
    mgrad[...] = middle_grad
    attn_grad = middle_grad.astype(bf16)
    rowst[...] = attn_grad.T.reshape(rowst.shape)

    def out_rows(i, carry):
        block = dot_nn(rowst[i], mixed_ref[...]).astype(bf16)
        outs.part[pl.ds(2 * i, 2)] = block.reshape(2, 2, rows, q_width)
        return carry

    lax.fori_loop(0, 4, out_rows, 0)
    outs.start()
    dmix_t = dot_nt(wo_ref[...], attn_grad).astype(bf16)
    dmix = dmix_t.T
    both = (dmix_t.astype(f32) * mixedt_ref[...].astype(f32)).reshape(
        kv_heads * group, HEAD_SIZE, tokens
    )
    delta[: kv_heads * group] = jnp.sum(both, axis=1)
    small = jnp.concatenate(
        [dot_nn(dlogits.T, h2_ref[...])[:EXPERTS], dgain2, jnp.zeros((7, width), f32)], axis=0
    )

    q = (q_ref[...].astype(f32) * HEAD_SIZE**-0.5).astype(bf16)
    q_t = q.T
    for i in range(kv_heads):
        for n in range(group):
            head = i * group + n
            cols = slice(HEAD_SIZE * head, HEAD_SIZE * (head + 1))
            span = slice(n * tokens, (n + 1) * tokens)
            qstack[i, span] = q[:, cols]
            qt[head] = q_t[cols]
            dmixstack[i, span] = dmix[:, cols]
            dmixt[head] = dmix_t[cols]
    for d in range(reach, -1, -1):
        s = reach - d
        far = (
            lax.broadcasted_iota(jnp.int32, (tokens, tokens), 1)
            - lax.broadcasted_iota(jnp.int32, (tokens, tokens), 0)
            + d * tokens
        )
        tags = kv_ref[s, :, 2 * kv_width :].astype(f32)
        tags = jnp.concatenate([tags] * (tokens // 128), axis=1)
        allowed = (tags == docrow_ref[...]) & (far >= 0) & (far < WINDOW)
        allowed = allowed & (at >= d)
        span = slice(s * tokens, (s + 1) * tokens)
        bias[span] = jnp.where(allowed, 0.0, masked_score)
        k_t = kv_ref[s, :, :kv_width].T
        for i in range(kv_heads):
            cols = slice(HEAD_SIZE * i, HEAD_SIZE * (i + 1))
            kheads[i, span] = kv_ref[s, :, cols]
            vheads[i, span] = kv_ref[s, :, kv_width + HEAD_SIZE * i : kv_width + HEAD_SIZE * (i + 1)]
            kt[i, :, span] = k_t[cols]

    def home(d, i):
        return pltpu.make_async_remote_copy(
            sendkv.at[d - 1, i], retkv.at[d - 1, i], kvs.at[d - 1, i], kvr.at[d - 1, i],
            device_id=(dp - d, t), device_id_type=MESH,
        )

    def one_kv(i, carry):
        for n in range(group):
            head = i * group + n
            scores = dot_nn(kheads[i], qt[head]) + bias[...]
            weights = jnp.exp(scores - lse_ref[pl.ds(head, 1), :])
            pulled = dot_nn(vheads[i], dmixt[head])
            cols = slice(n * tokens, (n + 1) * tokens)
            wcat[:, cols] = weights.astype(bf16)
            scat[:, cols] = (weights * (pulled - delta[pl.ds(head, 1), :])).astype(bf16)
        dv = dot_nn(wcat[...], dmixstack[i])
        dk = dot_nn(scat[...], qstack[i])
        dq = dot_nn(kt[i], scat[...])
        for n in range(group):
            dqt[i * group + n] = dq[:, n * tokens : (n + 1) * tokens]
        dkv = jnp.concatenate([dk, dv], axis=1)
        for d in range(1, reach + 1):
            span = slice((reach - d) * tokens, (reach - d + 1) * tokens)
            sendkv[d - 1, i] = dkv[span].astype(bf16)

            @pl.when(at >= d)
            def _():
                home(d, i).start()

        ownkv[i] = dkv[reach * tokens :]

        @pl.when(i == 0)
        def _():
            outs.second()

        @pl.when(i == kv_heads - 1)
        def _():
            outs.third()

        return carry

    lax.fori_loop(0, kv_heads, one_kv, 0)

    cosine, sine = cos_ref[...], sin_ref[...]
    dq = dqt[...].reshape(q_width, tokens).T * HEAD_SIZE**-0.5
    dql = rotated(dq, cosine, -sine).astype(bf16)
    x = x_ref[...].astype(f32)
    inverse1 = lax.rsqrt(jnp.mean(x * x, axis=1, keepdims=True) + norm_eps)
    normed1 = x * inverse1
    h1 = (normed1 * gain1_ref[...]).astype(bf16)
    rowst[...] = h1.T.reshape(rowst.shape)

    def query_rows(i, carry):
        block = dot_nn(rowst[i], dql).astype(bf16)
        quer.part[pl.ds(2 * i, 2)] = block.reshape(2, 2, rows, q_width)
        return carry

    lax.fori_loop(0, 4, query_rows, 0)
    quer.start()
    for copy in loads:
        copy.wait()
    back = dot_nt(dql, wq[...])
    quer.second()
    for d in range(1, reach + 1):
        for i in range(kv_heads):
            @pl.when(at + d < row_blocks)
            def _():
                home(d, i).wait_recv()
                ownkv[i] = ownkv[i] + retkv[d - 1, i].astype(f32)

    dk = jnp.concatenate([ownkv[i, :, :HEAD_SIZE] for i in range(kv_heads)], axis=1)
    dv = jnp.concatenate([ownkv[i, :, HEAD_SIZE:] for i in range(kv_heads)], axis=1)
    dkl = rotated(dk, cosine, -sine).astype(bf16)
    dvl = dv.astype(bf16)
    back = back + dot_nt(dkl, wk[...]) + dot_nt(dvl, wv[...])
    ysend[...] = back.astype(bf16)
    swap = pltpu.make_async_remote_copy(
        ysend, yrecv, ysem.at[0], ysem.at[1], device_id=(dp, 1 - t), device_id_type=MESH
    )
    swap.start()
    dgain1 = jnp.sum(back * normed1, axis=0, keepdims=True)
    row = lax.broadcasted_iota(jnp.int32, small.shape, 0)
    small = jnp.where(row == EXPERTS + 1, dgain1, small)
    small = jnp.concatenate([small, jnp.zeros((128 - small.shape[0], width), f32)], axis=0)
    small_t = small.T.astype(bf16)
    for i in range(4):
        block = jnp.concatenate(
            [dot_nn(rowst[i], dkl).astype(bf16), dot_nn(rowst[i], dvl).astype(bf16),
             small_t[i * 4 * rows : (i + 1) * 4 * rows]],
            axis=1,
        )
        tail.part[2 * i : 2 * i + 2] = block.reshape(2, 2, rows, 2 * kv_width + 128)
    tail.start()
    out_ref[...] = outs.total()
    tail.second()
    quer.third()
    swap.wait()
    grad = ysend[...].astype(f32) + yrecv[...].astype(f32)
    scaled = grad * gain1_ref[...]
    inner = jnp.mean(scaled * x, axis=1, keepdims=True)
    step = inverse1 * scaled - normed1 * (inverse1 * inverse1) * inner
    dtok_ref[...] = (mgrad[...] + step).astype(bf16)
    tail.third()
    query_ref[...] = quer.total()
    sums = tail.total()
    rest_ref[...] = sums
    gsend[...] = sums[:, 2 * kv_width :]
    swap2 = pltpu.make_async_remote_copy(
        gsend, grecv, ysem.at[2], ysem.at[3], device_id=(dp, 1 - t), device_id_type=MESH
    )
    swap2.start()
    swap2.wait()
    lane = lax.broadcasted_iota(jnp.int32, (rows, 128), 1)
    rest_ref[:, 2 * kv_width :] = jnp.where(
        lane == EXPERTS + 1, gsend[...] + grecv[...], gsend[...]
    )
    own.wait()

    def deal_wait(k, carry):
        pltpu.make_async_remote_copy(
            grads_ref.at[:, me], experts_ref.at[me], asend.at[k], arecv.at[k],
            device_id=(base + lax.rem(me + k, EXPERTS), t), device_id_type=MESH,
        ).wait()
        return carry

    lax.fori_loop(1, EXPERTS, deal_wait, 0)
    for d in range(1, reach + 1):
        for i in range(kv_heads):
            @pl.when(at >= d)
            def _():
                home(d, i).wait_send()
    for s in (outs, quer, tail):
        s.finish()


def back_call(grads, dh2, dprob, router, routes, h2, middle, x, dy, gain1, gain2, wr, mixed, mixedt,
              q, kv, lse, docrow, cosine, sine, wq, wk, wv, wo):
    tokens, width = x.shape
    q_width, kv_width = wq.shape[1], wk.shape[1]
    heads, kv_heads = q_width // HEAD_SIZE, kv_width // HEAD_SIZE
    group = heads // kv_heads
    reach = kv.shape[0] - 1
    keys = (reach + 1) * tokens
    rows = width // EXPERTS
    ff = grads.shape[-1]
    vmem = pl.BlockSpec(memory_space=pltpu.VMEM)
    hbm = pl.BlockSpec(memory_space=pl.ANY)
    shape = jax.ShapeDtypeStruct
    dma = pltpu.SemaphoreType.DMA
    return pl.pallas_call(
        back_kernel,
        out_shape=(
            shape((tokens, width), bf16),
            shape((EXPERTS, 3, rows, ff), bf16),
            shape((rows, q_width), f32),
            shape((rows, q_width), f32),
            shape((rows, 2 * kv_width + 128), f32),
        ),
        in_specs=[hbm] + [vmem] * 19 + [hbm, hbm, hbm, vmem],
        out_specs=(vmem, hbm, vmem, vmem, vmem),
        scratch_shapes=[
            pltpu.VMEM((width, q_width), bf16),
            pltpu.VMEM((width, kv_width), bf16),
            pltpu.VMEM((width, kv_width), bf16),
            pltpu.VMEM((kv_heads, keys, HEAD_SIZE), bf16),
            pltpu.VMEM((kv_heads, keys, HEAD_SIZE), bf16),
            pltpu.VMEM((kv_heads, HEAD_SIZE, keys), bf16),
            pltpu.VMEM((kv_heads, group * tokens, HEAD_SIZE), bf16),
            pltpu.VMEM((heads, HEAD_SIZE, tokens), bf16),
            pltpu.VMEM((heads, HEAD_SIZE, tokens), bf16),
            pltpu.VMEM((kv_heads, group * tokens, HEAD_SIZE), bf16),
            pltpu.VMEM((16, tokens), f32),
            pltpu.VMEM((keys, tokens), f32),
            pltpu.VMEM((keys, group * tokens), bf16),
            pltpu.VMEM((keys, group * tokens), bf16),
            pltpu.VMEM((heads, HEAD_SIZE, tokens), f32),
            pltpu.VMEM((reach, kv_heads, tokens, 128), bf16),
            pltpu.VMEM((kv_heads, tokens, 128), f32),
            pltpu.VMEM((reach, kv_heads, tokens, 128), bf16),
            pltpu.VMEM((4, width // 4, tokens), bf16),
            pltpu.VMEM((tokens, width), f32),
            pltpu.VMEM((tokens, width), bf16),
            pltpu.VMEM((tokens, width), bf16),
            pltpu.VMEM((rows, 128), f32),
            pltpu.VMEM((rows, 128), f32),
            dma((3,)),
            dma((EXPERTS,)),
            dma((EXPERTS,)),
            dma,
            dma((reach, kv_heads)),
            dma((reach, kv_heads)),
            dma((4,)),
        ]
        + scatter_bufs(rows, q_width)
        + scatter_bufs(rows, q_width)
        + scatter_bufs(rows, 2 * kv_width + 128)
        + scatter_sems() * 3,
        compiler_params=pltpu.CompilerParams(
            collective_id=2, has_side_effects=True, vmem_limit_bytes=VMEM_LIMIT
        ),
        name="backward",
    )(grads, dh2, dprob, router, routes, h2, middle, x, dy, gain1, gain2, wr, mixed, mixedt,
      q, kv, lse, docrow, cosine, sine, wq, wk, wv, wo)


def own_rows(block, axis):
    size = lax.axis_size("dp")
    groups = size // EXPERTS
    if groups == 1:
        return block
    members = [[r * EXPERTS + m for m in range(EXPERTS)] for r in range(groups)]
    across = [[r * EXPERTS + m for r in range(groups)] for m in range(EXPERTS)]
    block = jnp.moveaxis(block, axis, 0).astype(bf16)
    full = lax.all_gather(block, "dp", axis=0, tiled=True, axis_index_groups=members)
    full = full.reshape((groups, EXPERTS, full.shape[0] // size) + full.shape[1:])
    member = lax.rem(lax.axis_index("dp"), EXPERTS)
    mine = lax.dynamic_index_in_dim(full, member, 1, keepdims=False).astype(f32)
    mine = lax.psum_scatter(
        mine, "dp", scatter_dimension=0, tiled=False, axis_index_groups=across
    )
    return jnp.moveaxis(mine, 0, axis)


def per_device(
    tokens,
    cotangent,
    document_numbers,
    valid,
    routes,
    gain_attn,
    gain_moe,
    w_query,
    key_weight,
    value_weight,
    w_out,
    w_router,
    w_gate,
    w_up,
    w_down,
):
    rows_dev, width = tokens.shape
    kv_width = key_weight.shape[1]
    device = lax.axis_index("dp")
    positions = (device * rows_dev + jnp.arange(rows_dev, dtype=jnp.int32)) % ROW_LENGTH
    half = HEAD_SIZE // 2
    freqs = rope_base ** (-2.0 * jnp.arange(half, dtype=f32) / HEAD_SIZE)
    angle = positions.astype(f32)[:, None] * freqs[None, :]
    cosine, sine = jnp.cos(angle), jnp.sin(angle)
    cosine = jnp.concatenate([cosine] * 4, axis=1)
    sine = jnp.concatenate([-sine, sine] * 2, axis=1)
    tags = document_numbers.astype(f32)
    router_w = jnp.pad(w_router, ((0, 0), (0, 128 - EXPERTS)))
    (
        h2, middle, router, gates, gates_t, query_rows, kv, lse, mixed, mixed_t, dy, all_dy
    ) = attn_call(
        tokens, cotangent, valid.astype(f32)[:, None], tags[None, :], tags[:, None], routes,
        gain_attn[None, :], gain_moe[None, :], w_query, key_weight, value_weight, w_out,
        router_w, cosine, sine,
    )
    output, dh2, dprob, grads = moe_call(
        h2, dy, gates, gates_t, middle, w_gate, w_up, w_down,
        all_dy.reshape(EXPERTS // 2, 2 * rows_dev, width),
    )
    d_tokens, experts, d_out, d_query, rest = back_call(
        grads.reshape(3, EXPERTS, width // EXPERTS, grads.shape[2]), dh2, dprob, router, routes,
        h2, middle, tokens, dy, gain_attn[None, :], gain_moe[None, :], router_w, mixed, mixed_t,
        query_rows, kv, lse, tags[None, :], cosine, sine, w_query, key_weight, value_weight, w_out,
    )
    experts = own_rows(experts, 2).astype(f32)
    d_query = own_rows(d_query, 0)
    d_out = own_rows(d_out, 0)
    rest = own_rows(rest, 0)
    small = rest[:, 2 * kv_width :]
    return (
        output,
        d_tokens,
        small[:, EXPERTS + 1],
        small[:, EXPERTS],
        d_query,
        rest[:, :kv_width],
        rest[:, kv_width : 2 * kv_width],
        d_out.T,
        small[:, :EXPERTS],
        experts[:, 1],
        experts[:, 2],
        jnp.swapaxes(experts[:, 0], 1, 2),
    )


def solution(mesh):
    in_specs = (
        P("dp", None),
        P("dp", None),
        P("dp"),
        P("dp"),
        P("dp", None),
        P(),
        P(),
        P(None, "tensor"),
        P(None, "tensor"),
        P(None, "tensor"),
        P("tensor", None),
        P(),
        P(None, None, "tensor"),
        P(None, None, "tensor"),
        P(None, "tensor", None),
    )
    out_specs = (
        P("dp", None),
        P("dp", None),
        P("dp"),
        P("dp"),
        P("dp", "tensor"),
        P("dp", "tensor"),
        P("dp", "tensor"),
        P("tensor", "dp"),
        P("dp", None),
        P(None, "dp", "tensor"),
        P(None, "dp", "tensor"),
        P(None, "tensor", "dp"),
    )
    return jax.shard_map(
        per_device, mesh=mesh, in_specs=in_specs, out_specs=out_specs, check_vma=False
    )
```

```python
import jax
import jax.numpy as jnp
from jax import lax
from jax.experimental import pallas as pl
from jax.experimental.pallas import tpu as pltpu
from jax.sharding import PartitionSpec as P

HEAD_SIZE = 64
EXPERTS = 16
ROW_LENGTH = 2048
WINDOW = 1024
norm_eps = 1e-06
rope_base = 10000.0
masked_score = -1e30
MESH = pl.DeviceIdType.MESH
f32 = jnp.float32
bf16 = jnp.bfloat16
LINE = 4
VMEM_LIMIT = 62 * 2**20


def dot_nn(a,b): return lax.dot_general(a,b,(((1,),(0,)),((),())),preferred_element_type=f32)
def dot_nt(a,b): return lax.dot_general(a,b,(((1,),(1,)),((),())),preferred_element_type=f32)

def place():
    dp=lax.axis_index("dp"); t=lax.axis_index("tensor")
    m=lax.rem(dp,EXPERTS); base=dp-m
    a=m//4; b=lax.rem(m//2,2); c=lax.rem(m,2)
    return base,a,b,c,t

def near(a,j):
    low=(a<2).astype(jnp.int32)
    z=a*low+(3-a)*(1-low)
    o=j+z*((j==0)*1-(j==1)*1)
    return o*low+(3-o)*(1-low)

class Gather:
    def __init__(self, buf, sems, halves, outer):
        self.buf = buf
        self.recv, self.srecv, self.up, self.dn, self.bx, self.cx, self.sy, self.sc = sems
        self.halves = halves
        self.rows = buf.shape[1] // halves
        self.outer = outer
        self.inner = buf.shape[2] - outer
        self.base, self.a, self.b, self.c, self.t = place()

    def slot(self, a, b, c):
        return a * 4 + b * 2 + c

    def part(self, s, h, first, count):
        first = pl.multiple_of(first, 128)
        return self.buf.at[s, pl.ds(h * self.rows, self.rows), pl.ds(first, count)]

    def send(self, s, h, side, sem, a, b, c, t):
        if side is None:
            ref, done = self.part(s, h, self.t * self.outer, self.inner), self.recv
        else:
            ref, done = self.part(s, h, side * self.inner, self.outer), self.srecv
        return pltpu.make_async_remote_copy(
            src_ref=ref, dst_ref=ref, send_sem=sem, recv_sem=done.at[s, h],
            device_id=(self.base + self.slot(a, b, c), t), device_id_type=MESH,
        )

    def main(self, s, h, sem, a, b, c):
        return self.send(s, h, None, sem, a, b, c, self.t)

    def over(self, s, h, sem):
        return self.send(s, h, self.t, sem, self.a, self.b, self.c, 1 - self.t)

    def aside(self, s, h, sem):
        return self.send(s, h, 1 - self.t, sem, self.a, self.b, 1 - self.c, self.t)

    def wait_main(self, s, h):
        self.main(s, h, self.cx.at[0, h], self.a, self.b, 1 - self.c).wait_recv()

    def wait_side(self, s, h):
        self.aside(s, h, self.cx.at[0, h]).wait_recv()

    def own(self, j):
        return self.slot(near(self.a, j), self.b, self.c)

    def far(self, j):
        return self.slot(near(self.a, j), 1 - self.b, self.c)

    def event(self, j, h):
        a, b, c = self.a, self.b, self.c
        z, s = near(a, j), self.own(j)
        if j:
            self.wait_main(s, h)

        @pl.when((z <= a) & (a < LINE - 1))
        def _():
            self.main(s, h, self.up.at[j, h], a + 1, b, c).start()

        @pl.when((z >= a) & (a > 0))
        def _():
            self.main(s, h, self.dn.at[j, h], a - 1, b, c).start()

        self.main(s, h, self.bx.at[j, h], a, 1 - b, c).start()
        self.main(s, h, self.cx.at[j, h], a, b, 1 - c).start()
        if j:
            self.over(s, h, self.sy.at[j, h]).start()
        else:
            self.aside(s, h, self.sc.at[j, h]).start()

    def hop(self, k, h):
        middle = (self.a > 0) & (self.a < LINE - 1)

        @pl.when(jnp.logical_not(middle))
        def _():
            self.event(k, h)

        if k < LINE - 1:
            @pl.when(middle)
            def _():
                if k == 1:
                    self.event(1, h)
                self.event(k + 1, h)

    def xevent(self, j, h):
        s = self.far(j)
        self.wait_main(s, h)
        self.main(s, h, self.cx.at[LINE + j, h], self.a, self.b, 1 - self.c).start()
        self.over(s, h, self.sy.at[LINE + j, h]).start()

    def sevent(self, j, h):
        s = self.own(j)
        self.wait_side(s, h)
        self.aside(s, h, self.sc.at[j, h]).start()

    def sxevent(self, j, h):
        s = self.far(j)
        self.wait_side(s, h)
        self.aside(s, h, self.sc.at[LINE + j, h]).start()

    def from_core(self, j, h):
        s = self.slot(near(self.a, j), self.b, 1 - self.c)
        self.wait_main(s, h)
        self.wait_side(s, h)

    def from_core_x(self, j, h):
        s = self.slot(near(self.a, j), 1 - self.b, 1 - self.c)
        self.wait_main(s, h)
        self.wait_side(s, h)

    def finish(self):
        a, b, c = self.a, self.b, self.c
        for j in range(LINE):
            z, s, x = near(a, j), self.own(j), self.far(j)
            for h in range(self.halves):
                @pl.when((z <= a) & (a < LINE - 1))
                def _():
                    self.main(s, h, self.up.at[j, h], a + 1, b, c).wait_send()

                @pl.when((z >= a) & (a > 0))
                def _():
                    self.main(s, h, self.dn.at[j, h], a - 1, b, c).wait_send()

                self.main(s, h, self.bx.at[j, h], a, 1 - b, c).wait_send()
                self.main(s, h, self.cx.at[j, h], a, b, 1 - c).wait_send()
                self.main(x, h, self.cx.at[LINE + j, h], a, b, 1 - c).wait_send()
                if j:
                    self.over(s, h, self.sy.at[j, h]).wait_send()
                self.over(x, h, self.sy.at[LINE + j, h]).wait_send()
                self.aside(s, h, self.sc.at[j, h]).wait_send()
                self.aside(x, h, self.sc.at[LINE + j, h]).wait_send()


def gather_sems(halves):
    dma = pltpu.SemaphoreType.DMA
    line, both = (LINE, halves), (2 * LINE, halves)
    return [dma((EXPERTS, halves))] * 2 + [dma(line)] * 3 + [dma(both)] * 3


def planned(gather, plan, tick, more=None):
    steps = dict(hop=gather.hop, x=gather.xevent, s=gather.sevent, sx=gather.sxevent)
    steps.update(more or {})
    for at, names in plan.items():
        @pl.when(tick == at)
        def _():
            for name, j, h in names:
                steps[name](j, h)


def enter(with_y,more=0):
    base,a,b,c,t=place()
    bar=pltpu.get_barrier_semaphore()
    def sig(a2,b2,c2,t2): pl.semaphore_signal(bar,inc=1,device_id=(base+a2*4+b2*2+c2,t2),device_id_type=MESH)
    @pl.when(a<LINE-1)
    def _(): sig(a+1,b,c,t)
    @pl.when(a>0)
    def _(): sig(a-1,b,c,t)
    sig(a,1-b,c,t); sig(a,b,1-c,t)
    n=2
    if with_y: sig(a,b,c,1-t); n=3
    ends=(a==0).astype(jnp.int32)+(a==LINE-1).astype(jnp.int32)
    pl.semaphore_wait(bar,n+2-ends+more)


HEAD_PLAN = {
    1: (("x", 0, 1),),
    2: (("hop", 1, 1),),
}
STEP_PLAN = dict(
    queries=(("hop", 1, 0), ("x", 0, 0)),
    keys=(("sx", 0, 0), ("s", 1, 0)),
    project=(("hop", 2, 0),),
    exchange=(("x", 1, 0), ("hop", 2, 1), ("hop", 3, 0), ("hop", 3, 1), ("x", 1, 1), ("sx", 1, 0)),
    middle=(("x", 2, 1), ("s", 1, 1), ("s", 2, 1)),
    late=(
        ("x", 2, 0), ("s", 2, 0), ("sx", 0, 1), ("x", 3, 0), ("x", 3, 1), ("s", 3, 0),
        ("s", 3, 1), ("sx", 1, 1), ("sx", 2, 0), ("sx", 2, 1), ("sx", 3, 0), ("sx", 3, 1),
    ),
)


def steps(gather, name):
    todo = dict(hop=gather.hop, x=gather.xevent, s=gather.sevent, sx=gather.sxevent)
    for step, j, h in STEP_PLAN[name]:
        todo[step](j, h)


def swapped(block):
    lane = lax.broadcasted_iota(jnp.int32, block.shape, 1)
    low = lax.rem(lane, HEAD_SIZE) < HEAD_SIZE // 2
    return jnp.where(low, pltpu.roll(block, 128 - HEAD_SIZE // 2, 1), pltpu.roll(block, HEAD_SIZE // 2, 1))


def rotated(rows, cosine, sine):
    pieces = []
    for i in range(rows.shape[1] // 128):
        block = rows[:, 128 * i : 128 * (i + 1)]
        pieces.append(block * cosine + swapped(block) * sine)
    return jnp.concatenate(pieces, axis=1)


def attn_kernel(
    x_ref, cot_ref, valid_ref, docrow_ref, routes_ref, gain1_ref, gain2_ref,
    wq_ref, wk_ref, wv_ref, wo_ref, wr_ref, cos_ref, sin_ref,
    h2_ref, middle_ref, router_ref, gates_ref, gatest_ref, q_ref, kv_ref, lse_ref, mixed_ref, mixedt_ref,
    dy_ref, dyall_ref,
    dyall, kvbuf, wq, wo, kheads, vt, qheads, bias, mixedt, ysend, yrecv,
    wsem, osem, dsem, kvs, kvr, yss, yrs, *sems,
):
    tokens, width = x_ref.shape
    reach = kvbuf.shape[0] - 1
    row_blocks = ROW_LENGTH // tokens
    kv_width = wk_ref.shape[1]
    kv_heads = kv_width // HEAD_SIZE
    group = wq.shape[1] // kv_width
    gather = Gather(dyall, sems, 2, dyall.shape[2] // 6)
    base, a, b, c, t = place()
    me = a * 4 + b * 2 + c
    dp = base + me
    at = lax.rem(dp, row_blocks)
    loads = [
        pltpu.make_async_copy(wq_ref, wq, wsem.at[0]),
        pltpu.make_async_copy(wo_ref, wo, wsem.at[1]),
    ]
    for copy in loads:
        copy.start()
    dy = (cot_ref[...].astype(f32) * valid_ref[...]).astype(bf16)
    dyall[me] = dy
    dy_ref[...] = dy

    barrier = pltpu.get_barrier_semaphore()
    for d in range(1, reach + 1):
        @pl.when(at + d < row_blocks)
        def _():
            pl.semaphore_signal(barrier, inc=1, device_id=(dp + d, t), device_id_type=MESH)

        @pl.when(at >= d)
        def _():
            pl.semaphore_signal(barrier, inc=1, device_id=(dp - d, t), device_id_type=MESH)

    peers = jnp.minimum(at, reach) + jnp.minimum(row_blocks - 1 - at, reach)
    enter(True, peers)
    gather.event(0, 0)

    x = x_ref[...].astype(f32)
    inverse = lax.rsqrt(jnp.mean(x * x, axis=1, keepdims=True) + norm_eps)
    h1 = (x * inverse * gain1_ref[...]).astype(bf16)
    cosine, sine = cos_ref[...], sin_ref[...]
    kvbuf[reach, :tokens, :kv_width] = rotated(dot_nn(h1, wk_ref[...]), cosine, sine).astype(bf16)
    kvbuf[reach, :tokens, kv_width:] = dot_nn(h1, wv_ref[...]).astype(bf16)
    kvbuf[reach, tokens:, :tokens] = jnp.broadcast_to(docrow_ref[...], (16, tokens)).astype(bf16)
    kvbuf[reach, tokens:, tokens:] = jnp.zeros((16, kvbuf.shape[2] - tokens), bf16)

    def halo(d):
        return pltpu.make_async_remote_copy(
            kvbuf.at[reach], kvbuf.at[reach - d], kvs.at[d - 1], kvr.at[d - 1],
            device_id=(dp + d, t), device_id_type=MESH,
        )

    for d in range(1, reach + 1):
        @pl.when(at + d < row_blocks)
        def _():
            halo(d).start()

        @pl.when(at < d)
        def _():
            kvbuf[reach - d] = jnp.zeros(kvbuf.shape[1:], bf16)

    gather.event(0, 1)
    steps(gather, "queries")
    loads[0].wait()
    q = rotated(dot_nn(h1, wq[...]), cosine, sine)
    q_ref[...] = q.astype(bf16)
    q = (q * HEAD_SIZE**-0.5).astype(bf16)
    for i in range(group * kv_heads):
        qheads[i] = q[:, HEAD_SIZE * i : HEAD_SIZE * (i + 1)]

    steps(gather, "keys")
    for d in range(reach, -1, -1):
        s = reach - d
        if d:
            @pl.when(at >= d)
            def _():
                halo(d).wait_recv()
        far = (
            lax.broadcasted_iota(jnp.int32, (tokens, tokens), 1)
            - lax.broadcasted_iota(jnp.int32, (tokens, tokens), 0)
            + d * tokens
        )
        tags = kvbuf[s, tokens:, :tokens].T[:, :1].astype(f32)
        allowed = (tags == docrow_ref[...]) & (far >= 0) & (far < WINDOW)
        allowed = allowed & (at >= d)
        rows = slice(s * tokens, (s + 1) * tokens)
        bias[rows] = jnp.where(allowed, 0.0, masked_score)
        for i in range(kv_heads):
            cols = slice(HEAD_SIZE * i, HEAD_SIZE * (i + 1))
            kheads[i, rows] = kvbuf[s, :tokens, cols]
        v = kvbuf[s, :tokens, kv_width:].T
        for i in range(kv_heads):
            vt[i, :, rows] = v[HEAD_SIZE * i : HEAD_SIZE * (i + 1)]


    def one_kv(i, carry):
        planned(gather, HEAD_PLAN, i)
        for n in range(group):
            head = i * group + n
            scores = dot_nt(kheads[i], qheads[head]) + bias[...]
            top = jnp.max(scores, axis=0, keepdims=True)
            weights = jnp.exp(scores - top)
            total = jnp.sum(weights, axis=0, keepdims=True)
            mixedt[head] = (dot_nn(vt[i], weights.astype(bf16)) / total).astype(bf16)
            lse_ref[pl.ds(head, 1), :] = top + jnp.log(total)
        return carry

    lax.fori_loop(0, kv_heads, one_kv, 0)
    mixed_t = mixedt[...].reshape(group * kv_width, tokens)
    mixedt_ref[...] = mixed_t
    mixed = mixed_t.T
    mixed_ref[...] = mixed
    loads[1].wait()
    ysend[...] = dot_nn(mixed, wo[...]).astype(bf16)
    swap = pltpu.make_async_remote_copy(
        ysend, yrecv, yss, yrs, device_id=(dp, 1 - t), device_id_type=MESH
    )
    steps(gather, "project")
    swap.start()
    steps(gather, "exchange")
    swap.wait()
    steps(gather, "middle")
    middle = x + (ysend[...].astype(f32) + yrecv[...].astype(f32))
    middle_ref[...] = middle
    inverse = lax.rsqrt(jnp.mean(middle * middle, axis=1, keepdims=True) + norm_eps)
    h2 = (middle * inverse * gain2_ref[...]).astype(bf16)
    h2_ref[...] = h2
    logits = dot_nn(h2, wr_ref[...])
    lanes = lax.broadcasted_iota(jnp.int32, (tokens, 128), 1)
    logits = jnp.where(lanes < EXPERTS, logits, masked_score)
    raised = jnp.exp(logits - jnp.max(logits, axis=1, keepdims=True))
    router = raised / jnp.sum(raised, axis=1, keepdims=True)
    router_ref[...] = router
    picked = jnp.zeros((tokens, 128), f32)
    for i in range(routes_ref.shape[1]):
        picked = picked + jnp.where(routes_ref[:, i : i + 1] == lanes, 1.0, 0.0)
    gates = router * picked
    gates_ref[...] = gates
    gatest_ref[...] = gates.T[:EXPERTS]

    def write(j, side):
        pair = near(a, j) * 2 + lax.rem(b + side, 2)
        span = pl.ds(2 * pair, 2)
        return pltpu.make_async_copy(dyall.at[span], dyall_ref.at[span], osem.at[2 * j + side])

    kv_out = pltpu.make_async_copy(kvbuf, kv_ref, osem.at[2 * LINE])
    kv_out.start()
    steps(gather, "late")
    for j in range(LINE):
        for h in range(2):
            gather.from_core(j, h)
            gather.from_core_x(j, h)
        write(j, 0).start()
        write(j, 1).start()
    for d in range(1, reach + 1):
        @pl.when(at + d < row_blocks)
        def _():
            halo(d).wait_send()
    for j in range(LINE):
        write(j, 0).wait()
        write(j, 1).wait()
    kv_out.wait()
    gather.finish()


def attn_call(x, cot, valid, docrow, routes, gain1, gain2, wq, wk, wv, wo, wr, cosine, sine):
    tokens, width = x.shape
    q_width, kv_width = wq.shape[1], wk.shape[1]
    heads, kv_heads = q_width // HEAD_SIZE, kv_width // HEAD_SIZE
    reach = (WINDOW + tokens - 1) // tokens
    keys = (reach + 1) * tokens
    vmem = pl.BlockSpec(memory_space=pltpu.VMEM)
    hbm = pl.BlockSpec(memory_space=pl.ANY)
    shape = jax.ShapeDtypeStruct
    dma = pltpu.SemaphoreType.DMA
    return pl.pallas_call(
        attn_kernel,
        out_shape=(
            shape((tokens, width), bf16),
            shape((tokens, width), f32),
            shape((tokens, 128), f32),
            shape((tokens, 128), f32),
            shape((EXPERTS, tokens), f32),
            shape((tokens, q_width), bf16),
            shape((reach + 1, tokens + 16, 2 * kv_width), bf16),
            shape((16, tokens), f32),
            shape((tokens, q_width), bf16),
            shape((q_width, tokens), bf16),
            shape((tokens, width), bf16),
            shape((EXPERTS, tokens, width), bf16),
        ),
        in_specs=[vmem] * 7 + [hbm, vmem, vmem, hbm, vmem, vmem, vmem],
        out_specs=(vmem,) * 6 + (hbm, vmem, vmem, vmem, vmem, hbm),
        scratch_shapes=[
            pltpu.VMEM((EXPERTS, tokens, width), bf16),
            pltpu.VMEM((reach + 1, tokens + 16, 2 * kv_width), bf16),
            pltpu.VMEM((width, q_width), bf16),
            pltpu.VMEM((q_width, width), bf16),
            pltpu.VMEM((kv_heads, keys, HEAD_SIZE), bf16),
            pltpu.VMEM((kv_heads, HEAD_SIZE, keys), bf16),
            pltpu.VMEM((heads, tokens, HEAD_SIZE), bf16),
            pltpu.VMEM((keys, tokens), f32),
            pltpu.VMEM((heads, HEAD_SIZE, tokens), bf16),
            pltpu.VMEM((tokens, width), bf16),
            pltpu.VMEM((tokens, width), bf16),
            dma((2,)),
            dma((2 * LINE + 1,)),
            dma((2,)),
            dma((reach,)),
            dma((reach,)),
            dma,
            dma,
        ]
        + gather_sems(2),
        compiler_params=pltpu.CompilerParams(
            collective_id=1, has_side_effects=True, vmem_limit_bytes=VMEM_LIMIT
        ),
        name="attention",
    )(x, cot, valid, docrow, routes, gain1, gain2, wq, wk, wv, wo, wr, cosine, sine)


def greet_all(base, me, t):
    barrier = pltpu.get_barrier_semaphore()

    def greet(k, carry):
        peer = base + lax.rem(me + k, EXPERTS)
        pl.semaphore_signal(barrier, inc=1, device_id=(peer, t), device_id_type=MESH)
        return carry

    lax.fori_loop(1, EXPERTS, greet, 0)
    pl.semaphore_signal(barrier, inc=1, device_id=(base + me, 1 - t), device_id_type=MESH)
    pl.semaphore_wait(barrier, EXPERTS)


EXPERT_PLAN = {
    4: (("hop", 1, 0),),
    5: (("x", 0, 0),),
    7: (("hop", 1, 1),),
    9: (("x", 0, 1),),
    10: (("x", 1, 0),),
    11: (("hop", 2, 0),),
    12: (("sx", 0, 0),),
    13: (("hop", 2, 1),),
    15: (("x", 1, 1), ("s", 1, 0), ("s", 1, 1)),
}
PAIR_PLAN = {
    0: (("hop", 3, 0), ("x", 2, 0), ("sx", 0, 1), ("sx", 1, 0)),
    1: (("hop", 3, 1), ("x", 2, 1), ("s", 2, 0), ("s", 3, 0), ("w", 0, 0)),
    2: (("x", 3, 0), ("s", 2, 1), ("sx", 1, 1), ("sx", 2, 0)),
    3: (("x", 3, 1), ("s", 3, 1), ("w", 1, 0)),
    4: (("sx", 2, 1), ("w", 2, 0)),
    5: (("sx", 3, 0), ("sx", 3, 1), ("w", 3, 0)),
}


def moe_kernel(
    h2_ref, dy_ref, cg_ref, ct_ref, wg_ref, wu_ref, wd_ref, dyall_ref,
    opart_ref, dh2_ref, dprob_ref, grads_ref,
    h2all, ctsend, ctall, gbuf, ubuf, dbuf, wgt, wut, wdo, dybuf, cat, acco, acch, accp, accg, accu, accd,
    ysend, yrecv, psend, precv, wsem, lsem, dysem, yss, yrs, cts, ctr, *sems,
):
    tokens = h2_ref.shape[0]
    gather = Gather(h2all, sems, 2, h2all.shape[2] // 3)
    base, a, b, c, t = place()
    me = a * 4 + b * 2 + c
    load = pltpu.make_async_copy(h2_ref, h2all.at[me], lsem)
    load.start()
    ctsend[...] = jnp.broadcast_to(ct_ref[...][:, None, :], ctsend.shape)
    ctall[me] = ctsend[me]

    def row_out(k):
        peer = lax.rem(me + k, EXPERTS)
        return pltpu.make_async_remote_copy(
            ctsend.at[peer], ctall.at[me], cts.at[k], ctr.at[k],
            device_id=(base + peer, t), device_id_type=MESH,
        )

    def weights(e, k):
        sides = ((wg_ref, gbuf), (wu_ref, ubuf), (wd_ref, dbuf))
        return [
            pltpu.make_async_copy(src.at[e], dst.at[k], wsem.at[i, k])
            for i, (src, dst) in enumerate(sides)
        ]

    for copy in weights(0, 0):
        copy.start()
    greet_all(base, me, t)
    lax.fori_loop(1, EXPERTS, lambda k, carry: (row_out(k).start(), carry)[1], 0)
    load.wait()
    for h in range(2):
        gather.event(0, h)
    acco[...] = jnp.zeros_like(acco)
    acch[...] = jnp.zeros_like(acch)
    accp[...] = jnp.zeros_like(accp)
    accg[...] = jnp.zeros_like(accg)
    accu[...] = jnp.zeros_like(accu)
    accd[...] = jnp.zeros_like(accd)
    lanes = lax.broadcasted_iota(jnp.int32, (tokens, 128), 1)

    def one_expert(e, carry):
        k = lax.rem(e, 2)
        planned(gather, EXPERT_PLAN, e)

        @pl.when(e < EXPERTS - 1)
        def _():
            for copy in weights(e + 1, 1 - k):
                copy.start()

        for copy in weights(e, k):
            copy.wait()

        @pl.when(e == me)
        def _():
            wgt[...] = gbuf[k].T
            wut[...] = ubuf[k].T
            wdo[...] = dbuf[k]

        own = h2all[me]
        g = dot_nn(own, gbuf[k])
        u = dot_nn(own, ubuf[k])
        p = dot_nt(dy_ref[...], dbuf[k])
        column = jnp.sum(jnp.where(lanes == e, cg_ref[...], 0.0), axis=1, keepdims=True)
        s = 1.0 / (1.0 + jnp.exp(-g))
        act = g * s
        hidden = act * u
        accp[...] += jnp.where(lanes == e, jnp.sum(hidden * p, axis=1, keepdims=True), 0.0)
        hc = (column * hidden).astype(bf16)
        hg = column * p
        dg = (hg * u * s * (1.0 + g * (1.0 - s))).astype(bf16)
        du = (hg * act).astype(bf16)
        acco[...] += dot_nn(hc, dbuf[k])
        acch[...] += dot_nt(dg, gbuf[k]) + dot_nt(du, ubuf[k])
        return carry

    lax.fori_loop(0, EXPERTS, one_expert, 0)

    other = (base + me, 1 - t)
    quarter = tokens // 4
    opart_ref[...] = acco[...].astype(bf16)
    ysend[...] = acch[...].astype(bf16)
    psend[...] = accp[...].T[:EXPERTS]

    def swap(i):
        span = pl.ds(i * quarter, quarter)
        return pltpu.make_async_remote_copy(
            ysend.at[span], yrecv.at[span], yss.at[i], yrs.at[i],
            device_id=other, device_id_type=MESH,
        )

    small = pltpu.make_async_remote_copy(
        psend, precv, yss.at[4], yrs.at[4], device_id=other, device_id_type=MESH
    )
    small.start()
    lax.fori_loop(1, EXPERTS, lambda k, carry: (row_out(k).wait(), carry)[1], 0)

    def pair(k):
        j = k // 2
        side = lax.rem(b + lax.rem(k, 2), 2)
        return near(a, j) * 2 + side

    def dy_copy(k):
        slot = lax.rem(k, 2)
        return pltpu.make_async_copy(dyall_ref.at[pair(k)], dybuf.at[slot], dysem.at[slot])

    dy_copy(0).start()

    def one_pair(k, carry):
        @pl.when(k < 7)
        def _():
            dy_copy(k + 1).start()

        planned(gather, PAIR_PLAN, k, dict(w=lambda i, h: swap(i).start()))
        j = k // 2

        @pl.when(lax.rem(k, 2) == 0)
        def _():
            for h in range(2):
                gather.from_core(j, h)

        @pl.when(lax.rem(k, 2) == 1)
        def _():
            for h in range(2):
                gather.from_core_x(j, h)

        dy_copy(k).wait()
        at = pair(k)
        slot = lax.rem(k, 2)
        for q in range(2):
            h = h2all[2 * at + q]
            d = dybuf[slot, q * tokens : (q + 1) * tokens]
            g = dot_nt(wgt[...], h)
            u = dot_nt(wut[...], h)
            p = dot_nt(wdo[...], d)
            row = ctall[2 * at + q, 0:1, :]
            s = 1.0 / (1.0 + jnp.exp(-g))
            act = g * s
            hidden = act * u
            hg = row * p
            cols = slice(q * tokens, (q + 1) * tokens)
            cat[0, :, cols] = (row * hidden).astype(bf16)
            cat[1, :, cols] = (hg * u * s * (1.0 + g * (1.0 - s))).astype(bf16)
            cat[2, :, cols] = (hg * act).astype(bf16)
        both = h2all[pl.ds(2 * at, 2)].reshape(2 * tokens, h2all.shape[2])
        accd[...] += dot_nn(cat[0], dybuf[slot])
        accg[...] += dot_nn(cat[1], both)
        accu[...] += dot_nn(cat[2], both)
        return carry

    lax.fori_loop(0, 8, one_pair, 0)
    grads_ref[0] = accd[...].astype(bf16).T
    grads_ref[1] = accg[...].astype(bf16).T
    grads_ref[2] = accu[...].astype(bf16).T
    small.wait()
    dprob_ref[...] = psend[...] + precv[...]
    for i in range(4):
        swap(i).wait()
    dh2_ref[...] = ysend[...].astype(f32) + yrecv[...].astype(f32)
    gather.finish()


def moe_call(h2, dy, cg, ct, wg, wu, wd, dyall):
    tokens, width = h2.shape
    ff = wg.shape[2]
    vmem = pl.BlockSpec(memory_space=pltpu.VMEM)
    hbm = pl.BlockSpec(memory_space=pl.ANY)
    shape = jax.ShapeDtypeStruct
    dma = pltpu.SemaphoreType.DMA
    return pl.pallas_call(
        moe_kernel,
        out_shape=(
            shape((tokens, width), bf16),
            shape((tokens, width), f32),
            shape((EXPERTS, tokens), f32),
            shape((3, width, ff), bf16),
        ),
        in_specs=[hbm, vmem, vmem, vmem, hbm, hbm, hbm, hbm],
        out_specs=(vmem, vmem, vmem, vmem),
        scratch_shapes=[
            pltpu.VMEM((EXPERTS, tokens, width), bf16),
            pltpu.VMEM((EXPERTS, 8, tokens), f32),
            pltpu.VMEM((EXPERTS, 8, tokens), f32),
            pltpu.VMEM((2, width, ff), bf16),
            pltpu.VMEM((2, width, ff), bf16),
            pltpu.VMEM((2, ff, width), bf16),
            pltpu.VMEM((ff, width), bf16),
            pltpu.VMEM((ff, width), bf16),
            pltpu.VMEM((ff, width), bf16),
            pltpu.VMEM((2, 2 * tokens, width), bf16),
            pltpu.VMEM((3, ff, 2 * tokens), bf16),
            pltpu.VMEM((tokens, width), f32),
            pltpu.VMEM((tokens, width), f32),
            pltpu.VMEM((tokens, 128), f32),
            pltpu.VMEM((ff, width), f32),
            pltpu.VMEM((ff, width), f32),
            pltpu.VMEM((ff, width), f32),
            pltpu.VMEM((tokens, width), bf16),
            pltpu.VMEM((tokens, width), bf16),
            pltpu.VMEM((EXPERTS, tokens), f32),
            pltpu.VMEM((EXPERTS, tokens), f32),
            dma((3, 2)),
            dma,
            dma((2,)),
            dma((5,)),
            dma((5,)),
            dma((EXPERTS,)),
            dma((EXPERTS,)),
        ]
        + gather_sems(2),
        compiler_params=pltpu.CompilerParams(
            collective_id=0, has_side_effects=True, vmem_limit_bytes=VMEM_LIMIT
        ),
        name="moe",
    )(h2, dy, cg, ct, wg, wu, wd, dyall)


class Scatter:
    def __init__(self, bufs, sems):
        self.part, self.cbuf, self.keep, self.xbuf, self.last, self.zbuf = bufs
        self.csem, self.xsem, self.zsend, self.zrecv = sems
        self.base, self.a, self.b, self.c, self.t = place()

    def target(self, a, b, c):
        return (self.base + a * 4 + b * 2 + c, self.t)

    def core(self):
        return pltpu.make_async_remote_copy(
            self.part.at[:, 1 - self.c], self.cbuf, self.csem.at[0], self.csem.at[1],
            device_id=self.target(self.a, self.b, 1 - self.c), device_id_type=MESH,
        )

    def cross(self):
        return pltpu.make_async_remote_copy(
            self.keep.at[:, 1 - self.b], self.xbuf, self.xsem.at[0], self.xsem.at[1],
            device_id=self.target(self.a, 1 - self.b, self.c), device_id_type=MESH,
        )

    def along(self, k):
        z = lax.rem(self.a + k, LINE)
        return pltpu.make_async_remote_copy(
            self.last.at[z], self.zbuf.at[k - 1], self.zsend.at[k - 1], self.zrecv.at[k - 1],
            device_id=self.target(z, self.b, self.c), device_id_type=MESH,
        )

    def start(self):
        self.core().start()

    def second(self):
        self.core().wait()

        def add(i, carry):
            for j in range(2):
                mine = self.part[2 * i + j, self.c].astype(f32)
                self.keep[i, j] = (mine + self.cbuf[2 * i + j].astype(f32)).astype(bf16)
            return carry

        lax.fori_loop(0, LINE, add, 0)
        self.cross().start()

    def third(self):
        self.cross().wait()

        def add(i, carry):
            mine = self.keep[i, self.b].astype(f32)
            self.last[i] = (mine + self.xbuf[i].astype(f32)).astype(bf16)
            return carry

        lax.fori_loop(0, LINE, add, 0)
        for k in range(1, LINE):
            self.along(k).start()

    def total(self):
        result = self.last[self.a].astype(f32)
        for k in range(1, LINE):
            self.along(k).wait_recv()
            result = result + self.zbuf[k - 1].astype(f32)
        return result

    def finish(self):
        for k in range(1, LINE):
            self.along(k).wait_send()


def scatter_bufs(rows, columns):
    shapes = [(8, 2), (8,), (4, 2), (4,), (4,), (3,)]
    return [pltpu.VMEM(s + (rows, columns), bf16) for s in shapes]


def scatter_sems():
    dma = pltpu.SemaphoreType.DMA
    return [dma((2,)), dma((2,)), dma((LINE - 1,)), dma((LINE - 1,))]


def back_kernel(
    grads_ref, opart_ref, dh2_ref, dprob_ref, router_ref, routes_ref, h2_ref, middle_ref, x_ref, dy_ref,
    gain1_ref, gain2_ref, wr_ref, mixed_ref, mixedt_ref, q_ref, kv_ref, lse_ref, docrow_ref,
    cos_ref, sin_ref, wq_ref, wk_ref, wv_ref, wo_ref,
    output_ref, dtok_ref, experts_ref, out_ref, query_ref, rest_ref,
    wq, wk, wv, kheads, vheads, kt, qstack, qt, dmixt, dmixstack, delta, bias, wcat, scat, dqt,
    sendkv, ownkv, retkv, rowst, mgrad, ysend, yrecv, orecv, gsend, grecv,
    wsem, asend, arecv, lsem, kvs, kvr, ysem, *rest,
):
    tokens, width = x_ref.shape
    reach = retkv.shape[0]
    row_blocks = ROW_LENGTH // tokens
    kv_width = wk_ref.shape[1]
    kv_heads = kv_width // HEAD_SIZE
    q_width = wq_ref.shape[1]
    group = q_width // kv_width
    rows = width // EXPERTS
    keys = (reach + 1) * tokens
    outs = Scatter(rest[0:6], rest[18:22])
    quer = Scatter(rest[6:12], rest[22:26])
    tail = Scatter(rest[12:18], rest[26:30])
    base, a, b, c, t = place()
    me = a * 4 + b * 2 + c
    dp = base + me
    at = lax.rem(dp, row_blocks)
    loads = [
        pltpu.make_async_copy(src, dst, wsem.at[i])
        for i, (src, dst) in enumerate(((wq_ref, wq), (wk_ref, wk), (wv_ref, wv)))
    ]
    for copy in loads:
        copy.start()
    greet_all(base, me, t)

    def deal(k):
        peer = lax.rem(me + k, EXPERTS)
        return pltpu.make_async_remote_copy(
            grads_ref.at[:, peer], experts_ref.at[me], asend.at[k], arecv.at[k],
            device_id=(base + peer, t), device_id_type=MESH,
        )

    def deal_start(k, carry):
        deal(k).start()
        return carry

    lax.fori_loop(1, EXPERTS, deal_start, 0)
    swap_out = pltpu.make_async_remote_copy(
        opart_ref, orecv, ysem.at[4], ysem.at[5], device_id=(dp, 1 - t), device_id_type=MESH
    )
    swap_out.start()
    own = pltpu.make_async_copy(grads_ref.at[:, me], experts_ref.at[me], lsem)
    own.start()

    lanes = lax.broadcasted_iota(jnp.int32, (tokens, 128), 1)
    picked = lanes < 0
    for i in range(routes_ref.shape[1]):
        picked = picked | (routes_ref[:, i : i + 1] == lanes)
    router = router_ref[...]
    dprob = jnp.concatenate([dprob_ref[...], jnp.zeros((128 - EXPERTS, tokens), f32)], axis=0).T
    dprob = jnp.where(picked, dprob, 0.0)
    dlogits = router * (dprob - jnp.sum(dprob * router, axis=1, keepdims=True))
    dlogits = dlogits.astype(bf16)
    grad = dh2_ref[...] + dot_nt(dlogits, wr_ref[...])
    middle = middle_ref[...]
    inverse = lax.rsqrt(jnp.mean(middle * middle, axis=1, keepdims=True) + norm_eps)
    scaled = grad * gain2_ref[...]
    inner = jnp.mean(scaled * middle, axis=1, keepdims=True)
    normed = middle * inverse
    dgain2 = jnp.sum(grad * normed, axis=0, keepdims=True)
    middle_grad = dy_ref[...].astype(f32) + (
        inverse * scaled - normed * (inverse * inverse) * inner
    )
    mgrad[...] = middle_grad
    attn_grad = middle_grad.astype(bf16)
    rowst[...] = attn_grad.T.reshape(rowst.shape)

    def out_rows(i, carry):
        block = dot_nn(rowst[i], mixed_ref[...]).astype(bf16)
        outs.part[pl.ds(2 * i, 2)] = block.reshape(2, 2, rows, q_width)
        return carry

    lax.fori_loop(0, 4, out_rows, 0)
    outs.start()
    dmix_t = dot_nt(wo_ref[...], attn_grad).astype(bf16)
    dmix = dmix_t.T
    both = (dmix_t.astype(f32) * mixedt_ref[...].astype(f32)).reshape(
        kv_heads * group, HEAD_SIZE, tokens
    )
    delta[: kv_heads * group] = jnp.sum(both, axis=1)
    small = jnp.concatenate(
        [dot_nn(dlogits.T, h2_ref[...])[:EXPERTS], dgain2, jnp.zeros((7, width), f32)], axis=0
    )

    q = (q_ref[...].astype(f32) * HEAD_SIZE**-0.5).astype(bf16)
    q_t = q.T
    for i in range(kv_heads):
        for n in range(group):
            head = i * group + n
            cols = slice(HEAD_SIZE * head, HEAD_SIZE * (head + 1))
            span = slice(n * tokens, (n + 1) * tokens)
            qstack[i, span] = q[:, cols]
            qt[head] = q_t[cols]
            dmixstack[i, span] = dmix[:, cols]
            dmixt[head] = dmix_t[cols]
    for d in range(reach, -1, -1):
        s = reach - d
        far = (
            lax.broadcasted_iota(jnp.int32, (tokens, tokens), 1)
            - lax.broadcasted_iota(jnp.int32, (tokens, tokens), 0)
            + d * tokens
        )
        tags = kv_ref[s, tokens:, :tokens].T[:, :1].astype(f32)
        allowed = (tags == docrow_ref[...]) & (far >= 0) & (far < WINDOW)
        allowed = allowed & (at >= d)
        span = slice(s * tokens, (s + 1) * tokens)
        bias[span] = jnp.where(allowed, 0.0, masked_score)
        k_t = kv_ref[s, :tokens, :kv_width].T
        for i in range(kv_heads):
            cols = slice(HEAD_SIZE * i, HEAD_SIZE * (i + 1))
            kheads[i, span] = kv_ref[s, :tokens, cols]
            vheads[i, span] = kv_ref[
                s, :tokens, kv_width + HEAD_SIZE * i : kv_width + HEAD_SIZE * (i + 1)
            ]
            kt[i, :, span] = k_t[cols]

    def home(d, i):
        return pltpu.make_async_remote_copy(
            sendkv.at[d - 1, i], retkv.at[d - 1, i], kvs.at[d - 1, i], kvr.at[d - 1, i],
            device_id=(dp - d, t), device_id_type=MESH,
        )

    def one_kv(i, carry):
        for n in range(group):
            head = i * group + n
            scores = dot_nn(kheads[i], qt[head]) + bias[...]
            weights = jnp.exp(scores - lse_ref[pl.ds(head, 1), :])
            pulled = dot_nn(vheads[i], dmixt[head])
            cols = slice(n * tokens, (n + 1) * tokens)
            wcat[:, cols] = weights.astype(bf16)
            scat[:, cols] = (weights * (pulled - delta[pl.ds(head, 1), :])).astype(bf16)
        dv = dot_nn(wcat[...], dmixstack[i])
        dk = dot_nn(scat[...], qstack[i])
        dq = dot_nn(kt[i], scat[...])
        for n in range(group):
            dqt[i * group + n] = dq[:, n * tokens : (n + 1) * tokens]
        dkv = jnp.concatenate([dk, dv], axis=1)
        for d in range(1, reach + 1):
            span = slice((reach - d) * tokens, (reach - d + 1) * tokens)
            sendkv[d - 1, i] = dkv[span].astype(bf16)

            @pl.when(at >= d)
            def _():
                home(d, i).start()

        ownkv[i] = dkv[reach * tokens :]

        @pl.when(i == 0)
        def _():
            outs.second()

        @pl.when(i == kv_heads - 1)
        def _():
            outs.third()

        return carry

    lax.fori_loop(0, kv_heads, one_kv, 0)

    swap_out.wait()
    total = opart_ref[...].astype(f32) + orecv[...].astype(f32)
    output_ref[...] = (middle_ref[...] + total).astype(bf16)
    cosine, sine = cos_ref[...], sin_ref[...]
    dq = dqt[...].reshape(q_width, tokens).T * HEAD_SIZE**-0.5
    dql = rotated(dq, cosine, -sine).astype(bf16)
    x = x_ref[...].astype(f32)
    inverse1 = lax.rsqrt(jnp.mean(x * x, axis=1, keepdims=True) + norm_eps)
    normed1 = x * inverse1
    h1 = (normed1 * gain1_ref[...]).astype(bf16)
    rowst[...] = h1.T.reshape(rowst.shape)

    def query_rows(i, carry):
        block = dot_nn(rowst[i], dql).astype(bf16)
        quer.part[pl.ds(2 * i, 2)] = block.reshape(2, 2, rows, q_width)
        return carry

    lax.fori_loop(0, 4, query_rows, 0)
    quer.start()
    for copy in loads:
        copy.wait()
    back = dot_nt(dql, wq[...])
    quer.second()
    for d in range(1, reach + 1):
        for i in range(kv_heads):
            @pl.when(at + d < row_blocks)
            def _():
                home(d, i).wait_recv()
                ownkv[i] = ownkv[i] + retkv[d - 1, i].astype(f32)

    dk = jnp.concatenate([ownkv[i, :, :HEAD_SIZE] for i in range(kv_heads)], axis=1)
    dv = jnp.concatenate([ownkv[i, :, HEAD_SIZE:] for i in range(kv_heads)], axis=1)
    dkl = rotated(dk, cosine, -sine).astype(bf16)
    dvl = dv.astype(bf16)
    back = back + dot_nt(dkl, wk[...]) + dot_nt(dvl, wv[...])
    ysend[...] = back.astype(bf16)
    swap = pltpu.make_async_remote_copy(
        ysend, yrecv, ysem.at[0], ysem.at[1], device_id=(dp, 1 - t), device_id_type=MESH
    )
    swap.start()
    dgain1 = jnp.sum(back * normed1, axis=0, keepdims=True)
    row = lax.broadcasted_iota(jnp.int32, small.shape, 0)
    small = jnp.where(row == EXPERTS + 1, dgain1, small)
    small = jnp.concatenate([small, jnp.zeros((128 - small.shape[0], width), f32)], axis=0)
    small_t = small.T.astype(bf16)
    for i in range(4):
        block = jnp.concatenate(
            [dot_nn(rowst[i], dkl).astype(bf16), dot_nn(rowst[i], dvl).astype(bf16),
             small_t[i * 4 * rows : (i + 1) * 4 * rows]],
            axis=1,
        )
        tail.part[2 * i : 2 * i + 2] = block.reshape(2, 2, rows, 2 * kv_width + 128)
    tail.start()
    out_ref[...] = outs.total()
    tail.second()
    quer.third()
    swap.wait()
    grad = ysend[...].astype(f32) + yrecv[...].astype(f32)
    scaled = grad * gain1_ref[...]
    inner = jnp.mean(scaled * x, axis=1, keepdims=True)
    step = inverse1 * scaled - normed1 * (inverse1 * inverse1) * inner
    dtok_ref[...] = (mgrad[...] + step).astype(bf16)
    tail.third()
    query_ref[...] = quer.total()
    sums = tail.total()
    rest_ref[...] = sums
    gsend[...] = sums[:, 2 * kv_width :]
    swap2 = pltpu.make_async_remote_copy(
        gsend, grecv, ysem.at[2], ysem.at[3], device_id=(dp, 1 - t), device_id_type=MESH
    )
    swap2.start()
    swap2.wait()
    lane = lax.broadcasted_iota(jnp.int32, (rows, 128), 1)
    rest_ref[:, 2 * kv_width :] = jnp.where(
        lane == EXPERTS + 1, gsend[...] + grecv[...], gsend[...]
    )
    own.wait()

    def deal_wait(k, carry):
        pltpu.make_async_remote_copy(
            grads_ref.at[:, me], experts_ref.at[me], asend.at[k], arecv.at[k],
            device_id=(base + lax.rem(me + k, EXPERTS), t), device_id_type=MESH,
        ).wait()
        return carry

    lax.fori_loop(1, EXPERTS, deal_wait, 0)
    for d in range(1, reach + 1):
        for i in range(kv_heads):
            @pl.when(at >= d)
            def _():
                home(d, i).wait_send()
    for s in (outs, quer, tail):
        s.finish()


def back_call(grads, opart, dh2, dprob, router, routes, h2, middle, x, dy, gain1, gain2, wr, mixed, mixedt,
              q, kv, lse, docrow, cosine, sine, wq, wk, wv, wo):
    tokens, width = x.shape
    q_width, kv_width = wq.shape[1], wk.shape[1]
    heads, kv_heads = q_width // HEAD_SIZE, kv_width // HEAD_SIZE
    group = heads // kv_heads
    reach = kv.shape[0] - 1
    keys = (reach + 1) * tokens
    rows = width // EXPERTS
    ff = grads.shape[-1]
    vmem = pl.BlockSpec(memory_space=pltpu.VMEM)
    hbm = pl.BlockSpec(memory_space=pl.ANY)
    shape = jax.ShapeDtypeStruct
    dma = pltpu.SemaphoreType.DMA
    return pl.pallas_call(
        back_kernel,
        out_shape=(
            shape((tokens, width), bf16),
            shape((tokens, width), bf16),
            shape((EXPERTS, 3, rows, ff), bf16),
            shape((rows, q_width), f32),
            shape((rows, q_width), f32),
            shape((rows, 2 * kv_width + 128), f32),
        ),
        in_specs=[hbm] + [vmem] * 20 + [hbm, hbm, hbm, vmem],
        out_specs=(vmem, vmem, hbm, vmem, vmem, vmem),
        scratch_shapes=[
            pltpu.VMEM((width, q_width), bf16),
            pltpu.VMEM((width, kv_width), bf16),
            pltpu.VMEM((width, kv_width), bf16),
            pltpu.VMEM((kv_heads, keys, HEAD_SIZE), bf16),
            pltpu.VMEM((kv_heads, keys, HEAD_SIZE), bf16),
            pltpu.VMEM((kv_heads, HEAD_SIZE, keys), bf16),
            pltpu.VMEM((kv_heads, group * tokens, HEAD_SIZE), bf16),
            pltpu.VMEM((heads, HEAD_SIZE, tokens), bf16),
            pltpu.VMEM((heads, HEAD_SIZE, tokens), bf16),
            pltpu.VMEM((kv_heads, group * tokens, HEAD_SIZE), bf16),
            pltpu.VMEM((16, tokens), f32),
            pltpu.VMEM((keys, tokens), f32),
            pltpu.VMEM((keys, group * tokens), bf16),
            pltpu.VMEM((keys, group * tokens), bf16),
            pltpu.VMEM((heads, HEAD_SIZE, tokens), f32),
            pltpu.VMEM((reach, kv_heads, tokens, 128), bf16),
            pltpu.VMEM((kv_heads, tokens, 128), f32),
            pltpu.VMEM((reach, kv_heads, tokens, 128), bf16),
            pltpu.VMEM((4, width // 4, tokens), bf16),
            pltpu.VMEM((tokens, width), f32),
            pltpu.VMEM((tokens, width), bf16),
            pltpu.VMEM((tokens, width), bf16),
            pltpu.VMEM((tokens, width), bf16),
            pltpu.VMEM((rows, 128), f32),
            pltpu.VMEM((rows, 128), f32),
            dma((3,)),
            dma((EXPERTS,)),
            dma((EXPERTS,)),
            dma,
            dma((reach, kv_heads)),
            dma((reach, kv_heads)),
            dma((6,)),
        ]
        + scatter_bufs(rows, q_width)
        + scatter_bufs(rows, q_width)
        + scatter_bufs(rows, 2 * kv_width + 128)
        + scatter_sems() * 3,
        compiler_params=pltpu.CompilerParams(
            collective_id=2, has_side_effects=True, vmem_limit_bytes=VMEM_LIMIT
        ),
        name="backward",
    )(grads, opart, dh2, dprob, router, routes, h2, middle, x, dy, gain1, gain2, wr, mixed, mixedt,
      q, kv, lse, docrow, cosine, sine, wq, wk, wv, wo)


def own_rows(block, axis):
    size = lax.axis_size("dp")
    groups = size // EXPERTS
    if groups == 1:
        return block
    members = [[r * EXPERTS + m for m in range(EXPERTS)] for r in range(groups)]
    across = [[r * EXPERTS + m for r in range(groups)] for m in range(EXPERTS)]
    block = jnp.moveaxis(block, axis, 0).astype(bf16)
    full = lax.all_gather(block, "dp", axis=0, tiled=True, axis_index_groups=members)
    full = full.reshape((groups, EXPERTS, full.shape[0] // size) + full.shape[1:])
    member = lax.rem(lax.axis_index("dp"), EXPERTS)
    mine = lax.dynamic_index_in_dim(full, member, 1, keepdims=False).astype(f32)
    mine = lax.psum_scatter(
        mine, "dp", scatter_dimension=0, tiled=False, axis_index_groups=across
    )
    return jnp.moveaxis(mine, 0, axis)


def per_device(
    tokens,
    cotangent,
    document_numbers,
    valid,
    routes,
    gain_attn,
    gain_moe,
    w_query,
    key_weight,
    value_weight,
    w_out,
    w_router,
    w_gate,
    w_up,
    w_down,
):
    rows_dev, width = tokens.shape
    kv_width = key_weight.shape[1]
    device = lax.axis_index("dp")
    positions = (device * rows_dev + jnp.arange(rows_dev, dtype=jnp.int32)) % ROW_LENGTH
    half = HEAD_SIZE // 2
    freqs = rope_base ** (-2.0 * jnp.arange(half, dtype=f32) / HEAD_SIZE)
    angle = positions.astype(f32)[:, None] * freqs[None, :]
    cosine, sine = jnp.cos(angle), jnp.sin(angle)
    cosine = jnp.concatenate([cosine] * 4, axis=1)
    sine = jnp.concatenate([-sine, sine] * 2, axis=1)
    tags = document_numbers.astype(f32)
    router_w = jnp.pad(w_router, ((0, 0), (0, 128 - EXPERTS)))
    (
        h2, middle, router, gates, gates_t, query_rows, kv, lse, mixed, mixed_t, dy, all_dy
    ) = attn_call(
        tokens, cotangent, valid.astype(f32)[:, None], tags[None, :], routes,
        gain_attn[None, :], gain_moe[None, :], w_query, key_weight, value_weight, w_out,
        router_w, cosine, sine,
    )
    opart, dh2, dprob, grads = moe_call(
        h2, dy, gates, gates_t, w_gate, w_up, w_down,
        all_dy.reshape(EXPERTS // 2, 2 * rows_dev, width),
    )
    output, d_tokens, experts, d_out, d_query, rest = back_call(
        grads.reshape(3, EXPERTS, width // EXPERTS, grads.shape[2]), opart, dh2, dprob, router, routes,
        h2, middle, tokens, dy, gain_attn[None, :], gain_moe[None, :], router_w, mixed, mixed_t,
        query_rows, kv, lse, tags[None, :], cosine, sine, w_query, key_weight, value_weight, w_out,
    )
    experts = own_rows(experts, 2).astype(f32)
    d_query = own_rows(d_query, 0)
    d_out = own_rows(d_out, 0)
    rest = own_rows(rest, 0)
    small = rest[:, 2 * kv_width :]
    return (
        output,
        d_tokens,
        small[:, EXPERTS + 1],
        small[:, EXPERTS],
        d_query,
        rest[:, :kv_width],
        rest[:, kv_width : 2 * kv_width],
        d_out.T,
        small[:, :EXPERTS],
        experts[:, 1],
        experts[:, 2],
        jnp.swapaxes(experts[:, 0], 1, 2),
    )


def solution(mesh):
    in_specs = (
        P("dp", None),
        P("dp", None),
        P("dp"),
        P("dp"),
        P("dp", None),
        P(),
        P(),
        P(None, "tensor"),
        P(None, "tensor"),
        P(None, "tensor"),
        P("tensor", None),
        P(),
        P(None, None, "tensor"),
        P(None, None, "tensor"),
        P(None, "tensor", None),
    )
    out_specs = (
        P("dp", None),
        P("dp", None),
        P("dp"),
        P("dp"),
        P("dp", "tensor"),
        P("dp", "tensor"),
        P("dp", "tensor"),
        P("tensor", "dp"),
        P("dp", None),
        P(None, "dp", "tensor"),
        P(None, "dp", "tensor"),
        P(None, "tensor", "dp"),
    )
    return jax.shard_map(
        per_device, mesh=mesh, in_specs=in_specs, out_specs=out_specs, check_vma=False
    )
```

```python
import jax
import jax.numpy as jnp
import numpy as np
from jax import lax
from jax.experimental import pallas as pl
from jax.experimental.pallas import tpu as pltpu
from jax.sharding import PartitionSpec as P

HEAD_SIZE = 64
EXPERTS = 16
ROW_LENGTH = 2048
WINDOW = 1024
norm_eps = 1e-06
rope_base = 10000.0
masked_score = -1e30
MESH = pl.DeviceIdType.MESH
f32 = jnp.float32
bf16 = jnp.bfloat16
LINE = 4
VMEM_LIMIT = 63 * 2**20


def dot_nn(a,b): return lax.dot_general(a,b,(((1,),(0,)),((),())),preferred_element_type=f32)
def dot_nt(a,b): return lax.dot_general(a,b,(((1,),(1,)),((),())),preferred_element_type=f32)

def place():
    dp=lax.axis_index("dp"); t=lax.axis_index("tensor")
    m=lax.rem(dp,EXPERTS); base=dp-m
    a=m//4; b=lax.rem(m//2,2); c=lax.rem(m,2)
    return base,a,b,c,t

def near(a,j):
    low=(a<2).astype(jnp.int32)
    z=a*low+(3-a)*(1-low)
    o=j+z*((j==0)*1-(j==1)*1)
    return o*low+(3-o)*(1-low)

class Gather:
    def __init__(self, buf, sems, halves):
        self.buf = buf
        self.recv, self.srecv, self.up, self.dn, self.cx, self.sy, self.sc = sems
        self.halves = halves
        self.rows = buf.shape[1] // halves
        self.cols = buf.shape[2] // 2
        self.base, self.a, self.b, self.c, self.t = place()

    def slot(self, j):
        return near(self.a, j) * 2 + self.c

    def send(self, s, h, side, done, sem, a, c, t):
        first = pl.multiple_of(side * self.cols, 128)
        ref = self.buf.at[s, pl.ds(h * self.rows, self.rows), pl.ds(first, self.cols)]
        return pltpu.make_async_remote_copy(
            src_ref=ref, dst_ref=ref, send_sem=sem, recv_sem=done.at[s, h],
            device_id=(self.base + a * 4 + self.b * 2 + c, t), device_id_type=MESH,
        )

    def main(self, s, h, sem, a, c):
        return self.send(s, h, self.t, self.recv, sem, a, c, self.t)

    def over(self, s, h, sem):
        return self.send(s, h, self.t, self.srecv, sem, self.a, self.c, 1 - self.t)

    def aside(self, s, h, sem):
        return self.send(s, h, 1 - self.t, self.srecv, sem, self.a, 1 - self.c, self.t)

    def event(self, j, h):
        a, c = self.a, self.c
        z, s = near(a, j), self.slot(j)
        if j:
            self.main(s, h, self.cx.at[j, h], a, 1 - c).wait_recv()

        @pl.when((z <= a) & (a < LINE - 1))
        def _():
            self.main(s, h, self.up.at[j, h], a + 1, c).start()

        @pl.when((z >= a) & (a > 0))
        def _():
            self.main(s, h, self.dn.at[j, h], a - 1, c).start()

        self.main(s, h, self.cx.at[j, h], a, 1 - c).start()
        if j:
            self.over(s, h, self.sy.at[j, h]).start()
        else:
            self.aside(s, h, self.sc.at[j, h]).start()

    def hop(self, k, h):
        middle = (self.a > 0) & (self.a < LINE - 1)

        @pl.when(jnp.logical_not(middle))
        def _():
            self.event(k, h)

        if k < LINE - 1:
            @pl.when(middle)
            def _():
                if k == 1:
                    self.event(1, h)
                self.event(k + 1, h)

    def sevent(self, j, h):
        s = self.slot(j)
        self.aside(s, h, self.sc.at[j, h]).wait_recv()
        self.aside(s, h, self.sc.at[j, h]).start()

    def from_core(self, j, h):
        s = near(self.a, j) * 2 + 1 - self.c
        self.main(s, h, self.cx.at[0, h], self.a, 1 - self.c).wait_recv()
        self.aside(s, h, self.sc.at[0, h]).wait_recv()

    def finish(self):
        a, c = self.a, self.c
        for j in range(LINE):
            z, s = near(a, j), self.slot(j)
            for h in range(self.halves):
                @pl.when((z <= a) & (a < LINE - 1))
                def _():
                    self.main(s, h, self.up.at[j, h], a + 1, c).wait_send()

                @pl.when((z >= a) & (a > 0))
                def _():
                    self.main(s, h, self.dn.at[j, h], a - 1, c).wait_send()

                self.main(s, h, self.cx.at[j, h], a, 1 - c).wait_send()
                if j:
                    self.over(s, h, self.sy.at[j, h]).wait_send()
                self.aside(s, h, self.sc.at[j, h]).wait_send()


def gather_sems(halves):
    dma = pltpu.SemaphoreType.DMA
    return [dma((2 * LINE, halves))] * 2 + [dma((LINE, halves))] * 5


def planned(gather, plan, tick, more=None):
    todo = dict(hop=gather.hop, s=gather.sevent)
    todo.update(more or {})
    for at, names in plan.items():
        @pl.when(tick == at)
        def _():
            for name, j, h in names:
                todo[name](j, h)


def enter():
    base, a, b, c, t = place()
    barrier = pltpu.get_barrier_semaphore()

    def greet(a, b, c, t):
        peer = (base + a * 4 + b * 2 + c, t)
        pl.semaphore_signal(barrier, inc=1, device_id=peer, device_id_type=MESH)

    @pl.when(a < LINE - 1)
    def _():
        greet(a + 1, b, c, t)

    @pl.when(a > 0)
    def _():
        greet(a - 1, b, c, t)

    greet(a, 1 - b, c, t)
    greet(a, b, 1 - c, t)
    greet(a, b, c, 1 - t)
    ends = (a == 0).astype(jnp.int32) + (a == LINE - 1).astype(jnp.int32)
    pl.semaphore_wait(barrier, 5 - ends)


def as_column(row):
    return jnp.broadcast_to(row.astype(f32), (8, row.shape[1])).T[:, :1]


def as_row(vector_ref):
    return vector_ref[...].reshape(1, vector_ref.shape[0])


def router_rows(wr_ref):
    blank = jnp.zeros((128 - EXPERTS, wr_ref.shape[1]), bf16)
    return jnp.concatenate([wr_ref[...], blank], axis=0)


def named(routes_ref):
    routes = routes_ref[...].astype(f32).T
    lanes = lax.broadcasted_iota(jnp.int32, (routes.shape[0], 128), 1).astype(f32)
    picked = lanes < 0
    for i in range(routes.shape[1]):
        picked = picked | (routes[:, i : i + 1] == lanes)
    return picked


HEAD_PLAN = {
    0: (("hop", 1, 1),),
    1: (("hop", 2, 0),),
    2: (("hop", 2, 1), ("s", 1, 0)),
    3: (("s", 1, 1),),
}
STEP_PLAN = dict(
    queries=(("hop", 1, 0),),
    keys=(),
    project=(),
    exchange=(),
    middle=(("hop", 3, 0), ("hop", 3, 1), ("s", 2, 0), ("s", 2, 1)),
    late=(("s", 3, 0), ("s", 3, 1)),
)


def steps(gather, name):
    todo = dict(hop=gather.hop, s=gather.sevent)
    for step, j, h in STEP_PLAN[name]:
        todo[step](j, h)


def swapped(block):
    lane = lax.broadcasted_iota(jnp.int32, block.shape, 1)
    low = lax.rem(lane, HEAD_SIZE) < HEAD_SIZE // 2
    return jnp.where(low, pltpu.roll(block, 128 - HEAD_SIZE // 2, 1), pltpu.roll(block, HEAD_SIZE // 2, 1))


def rotated(rows, cosine, sine):
    pieces = []
    for i in range(rows.shape[1] // 128):
        block = rows[:, 128 * i : 128 * (i + 1)]
        pieces.append(block * cosine + swapped(block) * sine)
    return jnp.concatenate(pieces, axis=1)


def attn_kernel(
    x_ref, cot_ref, valid_ref, docrow_ref, routes_ref, gain1_ref, gain2_ref,
    wq_ref, wk_ref, wv_ref, wo_ref, wr_ref, turns_ref,
    h2_ref, middle_ref, router_ref, gates_ref, gatest_ref, q_ref, kv_ref, lse_ref, mixed_ref, mixedt_ref,
    dy_ref, dyall_ref,
    turns, dyall, kvbuf, wq, wo, kheads, vt, qheads, bias, mixedt, ysend, yrecv,
    wsem, osem, dsem, kvs, kvr, yss, yrs, *sems,
):
    tokens, width = x_ref.shape
    reach = kvbuf.shape[0] - 1
    row_blocks = ROW_LENGTH // tokens
    assert (reach, row_blocks) == (4, 8)
    kv_width = wk_ref.shape[1]
    kv_heads = kv_width // HEAD_SIZE
    group = wq.shape[1] // kv_width
    gather = Gather(dyall, sems, 2)
    base, a, b, c, t = place()
    me = a * 4 + b * 2 + c
    dp = base + me
    at = lax.rem(dp, row_blocks)
    load_turns = pltpu.make_async_copy(
        turns_ref.at[pl.ds(pl.multiple_of(at * tokens, tokens), tokens)], turns, wsem.at[2]
    )
    load_turns.start()
    loads = [
        pltpu.make_async_copy(wq_ref, wq, wsem.at[0]),
        pltpu.make_async_copy(wo_ref, wo, wsem.at[1]),
    ]
    for copy in loads:
        copy.start()
    dy = (cot_ref[...].astype(f32) * as_column(valid_ref[...])).astype(bf16)
    dyall[a * 2 + c] = dy
    dy_ref[...] = dy

    enter()
    gather.event(0, 0)

    x = x_ref[...].astype(f32)
    inverse = lax.rsqrt(jnp.mean(x * x, axis=1, keepdims=True) + norm_eps)
    h1 = (x * inverse * as_row(gain1_ref)).astype(bf16)
    load_turns.wait()
    cosine, sine = turns[:, :128], turns[:, 128:]
    kvbuf[reach, :tokens, :kv_width] = rotated(dot_nn(h1, wk_ref[...]), cosine, sine).astype(bf16)
    kvbuf[reach, :tokens, kv_width:] = dot_nn(h1, wv_ref[...]).astype(bf16)
    kvbuf[reach, tokens:, :tokens] = jnp.broadcast_to(
        docrow_ref[...].astype(f32), (16, tokens)
    ).astype(bf16)
    kvbuf[reach, tokens:, tokens:] = jnp.zeros((16, kvbuf.shape[2] - tokens), bf16)

    own, two, four = reach, reach - 2, reach - 4

    def pass_on(source, target, step, peer):
        return pltpu.make_async_remote_copy(
            kvbuf.at[source], kvbuf.at[target], kvs.at[step], kvr.at[target],
            device_id=(peer, t), device_id_type=MESH,
        )

    def arrived(target):
        pass_on(own, target, 0, dp).wait_recv()

    halo = [
        (at + 4 < row_blocks, own, four, 0, dp + 4),
        (b == 0, own, two, 1, dp + 2),
        ((b == 1) & (at >= 4), four, two, 1, dp - 2),
        (c == 0, own, reach - 1, 2, dp + 1),
        ((c == 0) & (at >= 2), two, reach - 3, 3, dp + 1),
        ((c == 1) & (at >= 2), two, reach - 1, 2, dp - 1),
        ((c == 1) & (at >= 4), four, reach - 3, 3, dp - 1),
    ]

    def halo_send(source):
        for there, first, *way in halo:
            if first == source:
                @pl.when(there)
                def _():
                    pass_on(first, *way).start()

    halo_send(own)
    for d in range(1, reach + 1):
        @pl.when(at < d)
        def _():
            kvbuf[reach - d] = jnp.zeros(kvbuf.shape[1:], bf16)

    gather.event(0, 1)
    steps(gather, "queries")
    loads[0].wait()
    q = rotated(dot_nn(h1, wq[...]), cosine, sine)
    q_ref[...] = q.astype(bf16)
    q = (q * HEAD_SIZE**-0.5).astype(bf16)
    for i in range(group * kv_heads):
        qheads[i] = q[:, HEAD_SIZE * i : HEAD_SIZE * (i + 1)]

    steps(gather, "keys")

    @pl.when(at >= 4)
    def _():
        arrived(four)

    halo_send(four)

    @pl.when(at >= 2)
    def _():
        arrived(two)

    halo_send(two)
    for d in range(reach, -1, -1):
        s = reach - d
        if d % 2:
            @pl.when(at >= d)
            def _():
                arrived(s)

        far = (
            lax.broadcasted_iota(jnp.int32, (tokens, tokens), 1)
            - lax.broadcasted_iota(jnp.int32, (tokens, tokens), 0)
            + d * tokens
        )
        tags = kvbuf[s, tokens:, :tokens].T[:, :1].astype(f32)
        allowed = (tags == docrow_ref[...].astype(f32)) & (far >= 0) & (far < WINDOW)
        allowed = allowed & (at >= d)
        rows = slice(s * tokens, (s + 1) * tokens)
        bias[rows] = jnp.where(allowed, 0.0, masked_score)
        for i in range(kv_heads):
            cols = slice(HEAD_SIZE * i, HEAD_SIZE * (i + 1))
            kheads[i, rows] = kvbuf[s, :tokens, cols]
        v = kvbuf[s, :tokens, kv_width:].T
        for i in range(kv_heads):
            vt[i, :, rows] = v[HEAD_SIZE * i : HEAD_SIZE * (i + 1)]


    def one_kv(i, carry):
        planned(gather, HEAD_PLAN, i)
        for n in range(group):
            head = i * group + n
            scores = dot_nt(kheads[i], qheads[head]) + bias[...]
            top = jnp.max(scores, axis=0, keepdims=True)
            weights = jnp.exp(scores - top)
            total = jnp.sum(weights, axis=0, keepdims=True)
            mixedt[head] = (dot_nn(vt[i], weights.astype(bf16)) / total).astype(bf16)
            lse_ref[pl.ds(head, 1), :] = top + jnp.log(total)
        return carry

    lax.fori_loop(0, kv_heads, one_kv, 0)
    mixed_t = mixedt[...].reshape(group * kv_width, tokens)
    mixedt_ref[...] = mixed_t
    mixed = mixed_t.T
    mixed_ref[...] = mixed
    loads[1].wait()
    ysend[...] = dot_nn(mixed, wo[...]).astype(bf16)
    swap = pltpu.make_async_remote_copy(
        ysend, yrecv, yss, yrs, device_id=(dp, 1 - t), device_id_type=MESH
    )
    steps(gather, "project")
    swap.start()
    steps(gather, "exchange")
    swap.wait()
    steps(gather, "middle")
    middle = x + (ysend[...].astype(f32) + yrecv[...].astype(f32))
    middle_ref[...] = middle
    inverse = lax.rsqrt(jnp.mean(middle * middle, axis=1, keepdims=True) + norm_eps)
    h2 = (middle * inverse * as_row(gain2_ref)).astype(bf16)
    h2_ref[...] = h2
    logits = dot_nt(h2, router_rows(wr_ref))
    lanes = lax.broadcasted_iota(jnp.int32, (tokens, 128), 1)
    logits = jnp.where(lanes < EXPERTS, logits, masked_score)
    raised = jnp.exp(logits - jnp.max(logits, axis=1, keepdims=True))
    router = raised / jnp.sum(raised, axis=1, keepdims=True)
    router_ref[...] = router
    gates = jnp.where(named(routes_ref), router, 0.0)
    gates_ref[...] = gates
    gatest_ref[...] = gates.T[:EXPERTS]

    def write(j):
        span = pl.ds(2 * near(a, j), 2)
        return pltpu.make_async_copy(dyall.at[span], dyall_ref.at[span], osem.at[j])

    kv_out = pltpu.make_async_copy(kvbuf, kv_ref, osem.at[LINE])
    kv_out.start()
    steps(gather, "late")
    for j in range(LINE):
        for h in range(2):
            gather.from_core(j, h)
        write(j).start()
    for there, *way in halo:
        @pl.when(there)
        def _():
            pass_on(*way).wait_send()

    for j in range(LINE):
        write(j).wait()
    kv_out.wait()
    gather.finish()


def attn_call(x, cot, valid, docrow, routes, gain1, gain2, wq, wk, wv, wo, wr, turns):
    tokens, width = x.shape
    q_width, kv_width = wq.shape[1], wk.shape[1]
    heads, kv_heads = q_width // HEAD_SIZE, kv_width // HEAD_SIZE
    reach = (WINDOW + tokens - 1) // tokens
    keys = (reach + 1) * tokens
    vmem = pl.BlockSpec(memory_space=pltpu.VMEM)
    hbm = pl.BlockSpec(memory_space=pl.ANY)
    shape = jax.ShapeDtypeStruct
    dma = pltpu.SemaphoreType.DMA
    return pl.pallas_call(
        attn_kernel,
        out_shape=(
            shape((tokens, width), bf16),
            shape((tokens, width), f32),
            shape((tokens, 128), f32),
            shape((tokens, 128), f32),
            shape((EXPERTS, tokens), f32),
            shape((tokens, q_width), bf16),
            shape((reach + 1, tokens + 16, 2 * kv_width), bf16),
            shape((16, tokens), f32),
            shape((tokens, q_width), bf16),
            shape((q_width, tokens), bf16),
            shape((tokens, width), bf16),
            shape((2 * LINE, tokens, width), bf16),
        ),
        in_specs=[vmem] * 7 + [hbm, vmem, vmem, hbm, vmem, hbm],
        out_specs=(vmem,) * 6 + (hbm, vmem, vmem, vmem, vmem, hbm),
        scratch_shapes=[
            pltpu.VMEM((tokens, 256), f32),
            pltpu.VMEM((2 * LINE, tokens, width), bf16),
            pltpu.VMEM((reach + 1, tokens + 16, 2 * kv_width), bf16),
            pltpu.VMEM((width, q_width), bf16),
            pltpu.VMEM((q_width, width), bf16),
            pltpu.VMEM((kv_heads, keys, HEAD_SIZE), bf16),
            pltpu.VMEM((kv_heads, HEAD_SIZE, keys), bf16),
            pltpu.VMEM((heads, tokens, HEAD_SIZE), bf16),
            pltpu.VMEM((keys, tokens), f32),
            pltpu.VMEM((heads, HEAD_SIZE, tokens), bf16),
            pltpu.VMEM((tokens, width), bf16),
            pltpu.VMEM((tokens, width), bf16),
            dma((3,)),
            dma((LINE + 1,)),
            dma((2,)),
            dma((reach,)),
            dma((reach,)),
            dma,
            dma,
        ]
        + gather_sems(2),
        compiler_params=pltpu.CompilerParams(
            collective_id=1, has_side_effects=True, vmem_limit_bytes=VMEM_LIMIT
        ),
        name="attention",
    )(x, cot, valid, docrow, routes, gain1, gain2, wq, wk, wv, wo, wr, turns)


def greet_all(base, me, t, beyond=()):
    barrier = pltpu.get_barrier_semaphore()

    def greet(k, carry):
        peer = base + lax.rem(me + k, EXPERTS)
        pl.semaphore_signal(barrier, inc=1, device_id=(peer, t), device_id_type=MESH)
        return carry

    lax.fori_loop(1, EXPERTS, greet, 0)
    for peer in [me, *beyond]:
        pl.semaphore_signal(barrier, inc=1, device_id=(base + peer, 1 - t), device_id_type=MESH)
    pl.semaphore_wait(barrier, EXPERTS + len(beyond))


FIRST_EXPERTS = 12
EXPERT_PLAN = {
    3: (("hop", 1, 0),),
    5: (("hop", 1, 1),),
    6: (("s", 1, 0),),
    8: (("hop", 2, 0), ("s", 1, 1)),
    10: (("hop", 2, 1), ("s", 2, 0)),
    11: (("hop", 3, 0),),
}
PAIR_PLAN = {
    0: (("s", 2, 1),),
    1: (("hop", 3, 1), ("s", 3, 0)),
    2: (("s", 3, 1),),
}


def moe_kernel(
    h2_ref, dy_ref, cg_ref, ct_ref, wg_ref, wu_ref, wd_ref, dyall_ref,
    opart_ref, dh2_ref, dprob_ref, grads_ref,
    h2all, dyall, ctsend, ctall, gbuf, ubuf, dbuf, rawg, rawu, wgt, wut, wdo, cat, acco, acch, accp, down,
    ysend, yrecv, psend, precv, wsem, lsem, yss, yrs, cts, ctr, xsem, *sems,
):
    tokens = h2_ref.shape[0]
    ff = wdo.shape[0] // 2
    gather = Gather(h2all, sems, 2)
    base, a, b, c, t = place()
    me = a * 4 + b * 2 + c
    mine = a * 2 + c
    load = pltpu.make_async_copy(h2_ref, h2all.at[mine], lsem.at[0])
    load.start()
    load_dy = pltpu.make_async_copy(dyall_ref, dyall, lsem.at[1])
    load_dy.start()
    rows = jnp.broadcast_to(ct_ref[...][:, None, :], (EXPERTS, 8, tokens))
    for i in range(2 * LINE):
        for n in range(2):
            ctsend[i, n] = rows[(i // 2) * 4 + n * 2 + i % 2]
    ctall[mine] = ctsend[mine]

    def row_out(k):
        peer = lax.rem(mine + k, 2 * LINE)
        return pltpu.make_async_remote_copy(
            ctsend.at[peer], ctall.at[mine], cts.at[k], ctr.at[k],
            device_id=(base + (peer // 2) * 4 + b * 2 + lax.rem(peer, 2), t), device_id_type=MESH,
        )

    def weights(e, k):
        sides = ((wg_ref, gbuf), (wu_ref, ubuf), (wd_ref, dbuf))
        return [
            pltpu.make_async_copy(src.at[e], dst.at[k], wsem.at[i, k])
            for i, (src, dst) in enumerate(sides)
        ]

    for copy in weights(0, 0):
        copy.start()
    greet_all(base, me, t)
    lax.fori_loop(1, 2 * LINE, lambda k, carry: (row_out(k).start(), carry)[1], 0)
    load.wait()
    for h in range(2):
        gather.event(0, h)
    acco[...] = jnp.zeros_like(acco)
    acch[...] = jnp.zeros_like(acch)
    accp[...] = jnp.zeros_like(accp)
    lanes = lax.broadcasted_iota(jnp.int32, (tokens, 128), 1)

    def one_expert(e, carry):
        k = lax.rem(e, 2)
        planned(gather, EXPERT_PLAN, e)

        @pl.when(e < EXPERTS - 1)
        def _():
            for copy in weights(e + 1, 1 - k):
                copy.start()

        for copy in weights(e, k):
            copy.wait()

        own = h2all[mine]
        g = dot_nn(own, gbuf[k])
        u = dot_nn(own, ubuf[k])
        p = dot_nt(dy_ref[...], dbuf[k])
        column = jnp.sum(jnp.where(lanes == e, cg_ref[...], 0.0), axis=1, keepdims=True)
        s = 1.0 / (1.0 + jnp.exp(-g))
        act = g * s
        hidden = act * u
        accp[...] += jnp.where(lanes == e, jnp.sum(hidden * p, axis=1, keepdims=True), 0.0)
        hc = (column * hidden).astype(bf16)
        hg = column * p
        dg = (hg * u * s * (1.0 + g * (1.0 - s))).astype(bf16)
        du = (hg * act).astype(bf16)
        acco[...] += dot_nn(hc, dbuf[k])
        acch[...] += dot_nt(dg, gbuf[k]) + dot_nt(du, ubuf[k])
        return carry

    def own_experts():
        copies = []
        for n in range(2):
            e = a * 4 + n * 2 + c
            half = pl.ds(n * ff, ff)
            copies.append(pltpu.make_async_copy(wd_ref.at[e], wdo.at[half], lsem.at[2 + n]))
            copies.append(pltpu.make_async_copy(wg_ref.at[e], rawg.at[n], lsem.at[4 + n]))
            copies.append(pltpu.make_async_copy(wu_ref.at[e], rawu.at[n], lsem.at[6 + n]))
        return copies

    for copy in own_experts():
        copy.start()
    lax.fori_loop(0, FIRST_EXPERTS, one_expert, 0)
    lax.fori_loop(1, 2 * LINE, lambda k, carry: (row_out(k).wait(), carry)[1], 0)
    load_dy.wait()
    for copy in own_experts():
        copy.wait()
    for n in range(2):
        wgt[n * ff : (n + 1) * ff] = rawg[n].T
        wut[n * ff : (n + 1) * ff] = rawu[n].T

    def one_pair(j, carry):
        planned(gather, PAIR_PLAN, j)
        for h in range(2):
            gather.from_core(j, h)
        for q in range(2):
            s = near(a, j) * 2 + q
            h = h2all[s]
            d = dyall[s]
            span = pl.ds(pl.multiple_of(s * tokens, 128), tokens)
            g_both = dot_nt(wgt[...], h)
            u_both = dot_nt(wut[...], h)
            pull = dot_nt(wdo[...], d)
            for n in range(2):
                half = slice(n * ff, (n + 1) * ff)
                g, u = g_both[half], u_both[half]
                row = ctall[s, n, 0:1, :]
                sig = 1.0 / (1.0 + jnp.exp(-g))
                act = g * sig
                hg = row * pull[half]
                cat[0, half, span] = (row * act * u).astype(bf16)
                cat[1, half, span] = (hg * u * sig * (1.0 + g * (1.0 - sig))).astype(bf16)
                cat[2, half, span] = (hg * act).astype(bf16)
        return carry

    lax.fori_loop(0, LINE, one_pair, 0)
    width = h2all.shape[2]
    tile = 4 * (width // EXPERTS)

    def gradient(i, buf):
        def one_tile(n, carry):
            cols = pl.ds(pl.multiple_of(n * tile, 128), tile)
            right = buf[:, :, cols].reshape(2 * LINE * tokens, tile)
            block = dot_nn(cat[i], right).astype(bf16).T
            grads_ref[i, n] = block.reshape(grads_ref.shape[2:])
            return carry

        lax.fori_loop(0, LINE, one_tile, 0)

    gradient(0, dyall)
    cross = pltpu.make_async_remote_copy(
        grads_ref.at[0, :, 1 - b], down, xsem.at[0], xsem.at[1],
        device_id=(base + a * 4 + (1 - b) * 2 + c, t), device_id_type=MESH,
    )
    cross.start()
    lax.fori_loop(FIRST_EXPERTS, EXPERTS, one_expert, 0)
    other = (base + me, 1 - t)
    opart_ref[...] = acco[...].astype(bf16)
    ysend[...] = acch[...].astype(bf16)
    psend[...] = accp[...].T[:EXPERTS]
    swaps = [
        pltpu.make_async_remote_copy(
            src, dst, yss.at[i], yrs.at[i], device_id=other, device_id_type=MESH
        )
        for i, (src, dst) in enumerate(((ysend, yrecv), (psend, precv)))
    ]
    for copy in swaps:
        copy.start()
    gradient(1, h2all)
    gradient(2, h2all)
    cross.wait()
    for z in range(LINE):
        both = grads_ref[0, z, b].astype(f32) + down[z].astype(f32)
        grads_ref[0, z, b] = both.astype(bf16)
    for copy in swaps:
        copy.wait()
    dprob_ref[...] = psend[...] + precv[...]
    dh2_ref[...] = ysend[...].astype(f32) + yrecv[...].astype(f32)
    gather.finish()


def moe_call(h2, dy, cg, ct, wg, wu, wd, dyall):
    tokens, width = h2.shape
    ff = wg.shape[2]
    rows = width // EXPERTS
    vmem = pl.BlockSpec(memory_space=pltpu.VMEM)
    hbm = pl.BlockSpec(memory_space=pl.ANY)
    shape = jax.ShapeDtypeStruct
    dma = pltpu.SemaphoreType.DMA
    return pl.pallas_call(
        moe_kernel,
        out_shape=(
            shape((tokens, width), bf16),
            shape((tokens, width), f32),
            shape((EXPERTS, tokens), f32),
            shape((3, LINE, 2, 2, rows, 2 * ff), bf16),
        ),
        in_specs=[hbm, vmem, vmem, vmem, hbm, hbm, hbm, hbm],
        out_specs=(vmem, vmem, vmem, vmem),
        scratch_shapes=[
            pltpu.VMEM((2 * LINE, tokens, width), bf16),
            pltpu.VMEM((2 * LINE, tokens, width), bf16),
            pltpu.VMEM((2 * LINE, 2, 8, tokens), f32),
            pltpu.VMEM((2 * LINE, 2, 8, tokens), f32),
            pltpu.VMEM((2, width, ff), bf16),
            pltpu.VMEM((2, width, ff), bf16),
            pltpu.VMEM((2, ff, width), bf16),
            pltpu.VMEM((2, width, ff), bf16),
            pltpu.VMEM((2, width, ff), bf16),
            pltpu.VMEM((2 * ff, width), bf16),
            pltpu.VMEM((2 * ff, width), bf16),
            pltpu.VMEM((2 * ff, width), bf16),
            pltpu.VMEM((3, 2 * ff, 2 * LINE * tokens), bf16),
            pltpu.VMEM((tokens, width), f32),
            pltpu.VMEM((tokens, width), f32),
            pltpu.VMEM((tokens, 128), f32),
            pltpu.VMEM((LINE, 2, rows, 2 * ff), bf16),
            pltpu.VMEM((tokens, width), bf16),
            pltpu.VMEM((tokens, width), bf16),
            pltpu.VMEM((EXPERTS, tokens), f32),
            pltpu.VMEM((EXPERTS, tokens), f32),
            dma((3, 2)),
            dma((8,)),
            dma((2,)),
            dma((2,)),
            dma((2 * LINE,)),
            dma((2 * LINE,)),
            dma((2,)),
        ]
        + gather_sems(2),
        compiler_params=pltpu.CompilerParams(
            collective_id=0, has_side_effects=True, vmem_limit_bytes=VMEM_LIMIT
        ),
        name="moe",
    )(h2, dy, cg, ct, wg, wu, wd, dyall)


class Scatter:
    def __init__(self, bufs, sems):
        self.part, self.cbuf, self.keep, self.xbuf, self.last, self.zbuf = bufs
        self.csem, self.xsem, self.zsend, self.zrecv = sems
        self.base, self.a, self.b, self.c, self.t = place()

    def target(self, a, b, c):
        return (self.base + a * 4 + b * 2 + c, self.t)

    def core(self):
        return pltpu.make_async_remote_copy(
            self.part.at[:, 1 - self.c], self.cbuf, self.csem.at[0], self.csem.at[1],
            device_id=self.target(self.a, self.b, 1 - self.c), device_id_type=MESH,
        )

    def cross(self):
        return pltpu.make_async_remote_copy(
            self.keep.at[:, 1 - self.b], self.xbuf, self.xsem.at[0], self.xsem.at[1],
            device_id=self.target(self.a, 1 - self.b, self.c), device_id_type=MESH,
        )

    def along(self, k):
        z = lax.rem(self.a + k, LINE)
        return pltpu.make_async_remote_copy(
            self.last.at[z], self.zbuf.at[k - 1], self.zsend.at[k - 1], self.zrecv.at[k - 1],
            device_id=self.target(z, self.b, self.c), device_id_type=MESH,
        )

    def start(self):
        self.core().start()

    def second(self):
        self.core().wait()

        def add(i, carry):
            for j in range(2):
                mine = self.part[2 * i + j, self.c].astype(f32)
                self.keep[i, j] = (mine + self.cbuf[2 * i + j].astype(f32)).astype(bf16)
            return carry

        lax.fori_loop(0, LINE, add, 0)
        self.cross().start()

    def third(self):
        self.cross().wait()

        def add(i, carry):
            mine = self.keep[i, self.b].astype(f32)
            self.last[i] = (mine + self.xbuf[i].astype(f32)).astype(bf16)
            return carry

        lax.fori_loop(0, LINE, add, 0)
        for k in range(1, LINE):
            self.along(k).start()

    def total(self):
        result = self.last[self.a].astype(f32)
        for k in range(1, LINE):
            self.along(k).wait_recv()
            result = result + self.zbuf[k - 1].astype(f32)
        return result

    def finish(self):
        for k in range(1, LINE):
            self.along(k).wait_send()

    def put(self, matrix, columns):
        def some(i, carry):
            block = dot_nn(matrix[i], columns).astype(bf16)
            self.part[pl.ds(2 * i, 2)] = block.reshape((2,) + self.part.shape[1:])
            return carry

        lax.fori_loop(0, 4, some, 0)


def scatter_bufs(rows, columns):
    shapes = [(8, 2), (8,), (4, 2), (4,), (4,), (3,)]
    return [pltpu.VMEM(s + (rows, columns), bf16) for s in shapes]


def scatter_sems():
    dma = pltpu.SemaphoreType.DMA
    return [dma((2,)), dma((2,)), dma((LINE - 1,)), dma((LINE - 1,))]


def back_kernel(
    grads_ref, opart_ref, dh2_ref, dprob_ref, router_ref, routes_ref, h2_ref, middle_ref, x_ref, dy_ref,
    gain1_ref, gain2_ref, wr_ref, mixed_ref, mixedt_ref, q_ref, kv_ref, lse_ref, docrow_ref,
    turns_ref, wq_ref, wk_ref, wv_ref, wo_ref,
    output_ref, dtok_ref, experts_ref, out_ref, query_ref, rest_ref,
    turns, wq, wk, wv, kheads, vheads, kt, qstack, qt, dmixt, dmixstack, delta, bias, wcat, scat, dqt,
    coresend, corerecv, pairsend, pairrecv, linesend, linerecv, parts, rowst, mgrad, ysend, yrecv, orecv, gbuf, summed, crossed,
    wsem, asend, arecv, lsem, csem, kvs, kvr, ysem, gsem, *rest,
):
    tokens, width = x_ref.shape
    reach = kv_ref.shape[0] - 1
    assert (reach, ROW_LENGTH // tokens) == (4, 8)
    row_blocks = ROW_LENGTH // tokens
    kv_width = wk_ref.shape[1]
    kv_heads = kv_width // HEAD_SIZE
    q_width = wq_ref.shape[1]
    group = q_width // kv_width
    rows = width // EXPERTS
    keys = (reach + 1) * tokens
    outs = Scatter(rest[0:6], rest[23:27])
    q_low = Scatter(rest[6:12], rest[27:31])
    q_high = Scatter(rest[6:7] + rest[12:17], rest[31:35])
    tail = Scatter(rest[17:23], rest[35:39])
    base, a, b, c, t = place()
    me = a * 4 + b * 2 + c
    dp = base + me
    at = lax.rem(dp, row_blocks)
    loads = [
        pltpu.make_async_copy(src, dst, wsem.at[i])
        for i, (src, dst) in enumerate(((wq_ref, wq), (wk_ref, wk), (wv_ref, wv)))
    ]
    for copy in loads:
        copy.start()
    load_turns = pltpu.make_async_copy(
        turns_ref.at[pl.ds(pl.multiple_of(at * tokens, tokens), tokens)], turns, wsem.at[4]
    )
    load_turns.start()
    load_dh2 = pltpu.make_async_copy(dh2_ref, mgrad, wsem.at[3])
    load_dh2.start()
    greet_all(base, me, t, [lax.rem(a + k, LINE) * 4 + b * 2 + c for k in range(1, LINE)])

    def deal(p, k, n):
        z, core = lax.rem(a + k, LINE), lax.rem(c + n, 2)
        source = grads_ref.at[0, z, b, core] if p == 0 else summed.at[p - 1, z, core]
        return pltpu.make_async_remote_copy(
            source, experts_ref.at[a * 2 + c, p], asend.at[p, 2 * k + n], arecv.at[p, 2 * k + n],
            device_id=(base + z * 4 + b * 2 + core, t), device_id_type=MESH,
        )

    def keep_own(p):
        source = grads_ref.at[0, a, b, c] if p == 0 else summed.at[p - 1, a, c]
        return pltpu.make_async_copy(source, experts_ref.at[a * 2 + c, p], lsem.at[p])

    places = [(k, n) for k in range(LINE) for n in range(2) if k or n]

    def deal_out(p):
        keep_own(p).start()
        for k, n in places:
            deal(p, k, n).start()

    def half_load(p):
        return pltpu.make_async_copy(grads_ref.at[p, :, b], summed.at[p - 1], lsem.at[2 + p])

    def cross(p):
        return pltpu.make_async_remote_copy(
            grads_ref.at[p, :, 1 - b], crossed.at[p - 1], csem.at[0, p - 1], csem.at[1, p - 1],
            device_id=(base + a * 4 + (1 - b) * 2 + c, t), device_id_type=MESH,
        )

    def merge(p):
        half_load(p).wait()
        cross(p).wait()

        def add(z, carry):
            for n in range(2):
                both = summed[p - 1, z, n].astype(f32) + crossed[p - 1, z, n].astype(f32)
                summed[p - 1, z, n] = both.astype(bf16)
            return carry

        lax.fori_loop(0, LINE, add, 0)
        deal_out(p)

    cross(1).start()
    half_load(1).start()
    half_load(2).start()
    deal_out(0)
    swap_out = pltpu.make_async_remote_copy(
        opart_ref, orecv, ysem.at[4], ysem.at[5], device_id=(dp, 1 - t), device_id_type=MESH
    )
    swap_out.start()

    router = router_ref[...]
    dprob = jnp.concatenate([dprob_ref[...], jnp.zeros((128 - EXPERTS, tokens), f32)], axis=0).T
    dprob = jnp.where(named(routes_ref), dprob, 0.0)
    dlogits = router * (dprob - jnp.sum(dprob * router, axis=1, keepdims=True))
    dlogits = dlogits.astype(bf16)
    load_dh2.wait()
    grad = mgrad[...] + dot_nn(dlogits, router_rows(wr_ref))
    middle = middle_ref[...]
    inverse = lax.rsqrt(jnp.mean(middle * middle, axis=1, keepdims=True) + norm_eps)
    scaled = grad * as_row(gain2_ref)
    inner = jnp.mean(scaled * middle, axis=1, keepdims=True)
    normed = middle * inverse
    dgain2 = jnp.sum(grad * normed, axis=0, keepdims=True)
    middle_grad = dy_ref[...].astype(f32) + (
        inverse * scaled - normed * (inverse * inverse) * inner
    )
    mgrad[...] = middle_grad
    attn_grad = middle_grad.astype(bf16)
    rowst[...] = attn_grad.T.reshape(rowst.shape)

    outs.put(rowst, mixed_ref[...])
    outs.start()
    dmix_t = dot_nt(wo_ref[...], attn_grad).astype(bf16)
    dmix = dmix_t.T
    both = (dmix_t.astype(f32) * mixedt_ref[...].astype(f32)).reshape(
        kv_heads * group, HEAD_SIZE, tokens
    )
    delta[: kv_heads * group] = jnp.sum(both, axis=1)
    small = jnp.concatenate(
        [dot_nn(dlogits.T, h2_ref[...])[:EXPERTS], dgain2, jnp.zeros((7, width), f32)], axis=0
    )

    q = (q_ref[...].astype(f32) * HEAD_SIZE**-0.5).astype(bf16)
    q_t = q.T
    for i in range(kv_heads):
        for n in range(group):
            head = i * group + n
            cols = slice(HEAD_SIZE * head, HEAD_SIZE * (head + 1))
            span = slice(n * tokens, (n + 1) * tokens)
            qstack[i, span] = q[:, cols]
            qt[head] = q_t[cols]
            dmixstack[i, span] = dmix[:, cols]
            dmixt[head] = dmix_t[cols]
    for d in range(reach, -1, -1):
        s = reach - d
        far = (
            lax.broadcasted_iota(jnp.int32, (tokens, tokens), 1)
            - lax.broadcasted_iota(jnp.int32, (tokens, tokens), 0)
            + d * tokens
        )
        tags = kv_ref[s, tokens:, :tokens].T[:, :1].astype(f32)
        allowed = (tags == docrow_ref[...].astype(f32)) & (far >= 0) & (far < WINDOW)
        allowed = allowed & (at >= d)
        span = slice(s * tokens, (s + 1) * tokens)
        bias[span] = jnp.where(allowed, 0.0, masked_score)
        k_t = kv_ref[s, :tokens, :kv_width].T
        for i in range(kv_heads):
            cols = slice(HEAD_SIZE * i, HEAD_SIZE * (i + 1))
            kheads[i, span] = kv_ref[s, :tokens, cols]
            vheads[i, span] = kv_ref[
                s, :tokens, kv_width + HEAD_SIZE * i : kv_width + HEAD_SIZE * (i + 1)
            ]
            kt[i, :, span] = k_t[cols]

    def shared(k):
        z = lax.rem(a + k, LINE)
        return pltpu.make_async_remote_copy(
            tail.last.at[z, :, pl.ds(2 * kv_width, 128)], gbuf.at[k], gsem.at[0, k], gsem.at[1, k],
            device_id=(base + z * 4 + b * 2 + c, 1 - t), device_id_type=MESH,
        )

    def by_core(n, i):
        return pltpu.make_async_remote_copy(
            coresend.at[n, i], corerecv.at[n, i], kvs.at[n, i], kvr.at[n, i],
            device_id=(base + a * 4 + b * 2 + 1 - c, t), device_id_type=MESH,
        )

    def by_pair(i):
        return pltpu.make_async_remote_copy(
            pairsend.at[i], pairrecv.at[i], kvs.at[2, i], kvr.at[2, i],
            device_id=(base + a * 4 + (1 - b) * 2 + c, t), device_id_type=MESH,
        )

    def by_line(i):
        return pltpu.make_async_remote_copy(
            linesend.at[i], linerecv.at[i], kvs.at[3, i], kvr.at[3, i],
            device_id=(dp - 4, t), device_id_type=MESH,
        )

    pair_sends = (b == 1) | (at >= 4)
    pair_takes = (b == 0) | (at >= 4)

    def after_core(i):
        for n in range(2):
            there = (c == 0) | (at >= 2 + 2 * n)
            if n:
                there = there & (at >= 2)

            @pl.when(there)
            def _():
                by_core(n, i).wait_recv()
                share = corerecv[n, i].astype(f32)

                @pl.when(c == 0)
                def _():
                    parts[n, i] = parts[n, i] + share

                @pl.when(c == 1)
                def _():
                    parts[n + 1, i] = parts[n + 1, i] + share

        @pl.when(pair_sends)
        def _():
            pairsend[i] = parts[1, i].astype(bf16)
            by_pair(i).start()

    def after_pair(i):
        @pl.when(pair_takes)
        def _():
            by_pair(i).wait_recv()
            share = pairrecv[i].astype(f32)

            @pl.when(b == 0)
            def _():
                parts[0, i] = parts[0, i] + share

            @pl.when(b == 1)
            def _():
                parts[2, i] = parts[2, i] + share

        @pl.when(at >= 4)
        def _():
            linesend[i] = parts[2, i].astype(bf16)
            by_line(i).start()

    def one_kv(i, carry):
        for n in range(group):
            head = i * group + n
            scores = dot_nn(kheads[i], qt[head]) + bias[...]
            weights = jnp.exp(scores - lse_ref[pl.ds(head, 1), :])
            pulled = dot_nn(vheads[i], dmixt[head])
            cols = slice(n * tokens, (n + 1) * tokens)
            wcat[:, cols] = weights.astype(bf16)
            scat[:, cols] = (weights * (pulled - delta[pl.ds(head, 1), :])).astype(bf16)
        dv = dot_nn(wcat[...], dmixstack[i])
        dk = dot_nn(scat[...], qstack[i])
        dq = dot_nn(kt[i], scat[...])
        for n in range(group):
            dqt[i * group + n] = dq[:, n * tokens : (n + 1) * tokens]
        dkv = jnp.concatenate([dk, dv], axis=1)
        for d in range(reach + 1):
            share = dkv[(reach - d) * tokens : (reach - d + 1) * tokens]
            if d % 2:
                coresend[d // 2, i] = share.astype(bf16)

                @pl.when(at >= d)
                def _():
                    by_core(d // 2, i).start()
            else:
                parts[d // 2, i] = share

        @pl.when(i >= 1)
        def _():
            after_core(i - 1)

        @pl.when(i == 1)
        def _():
            outs.second()

        @pl.when(i == 3)
        def _():
            q_low.second()
            merge(1)

        return carry

    load_turns.wait()
    cosine, sine = turns[:, :128], turns[:, 128:]
    x = x_ref[...].astype(f32)
    inverse1 = lax.rsqrt(jnp.mean(x * x, axis=1, keepdims=True) + norm_eps)
    normed1 = x * inverse1
    rowst[...] = (normed1 * as_row(gain1_ref)).astype(bf16).T.reshape(rowst.shape)
    half = kv_heads // 2
    half_width = q_width // 2

    def query_grad(first):
        heads = dqt[first * group : (first + half) * group]
        grad = heads.reshape(half_width, tokens).T * HEAD_SIZE**-0.5
        return rotated(grad, cosine, -sine).astype(bf16)

    lax.fori_loop(0, half, one_kv, 0)
    low = query_grad(0)
    q_low.put(rowst, low)
    q_low.start()
    lax.fori_loop(half, kv_heads, one_kv, 0)
    high = query_grad(half)
    q_high.put(rowst, high)
    q_high.start()
    after_core(kv_heads - 1)
    swap_out.wait()
    total = opart_ref[...].astype(f32) + orecv[...].astype(f32)
    output_ref[...] = (middle_ref[...] + total).astype(bf16)
    for copy in loads:
        copy.wait()
    back = dot_nt(low, wq[:, :half_width]) + dot_nt(high, wq[:, half_width:])
    q_high.second()
    cross(2).start()
    for i in range(kv_heads):
        after_pair(i)
    outs.third()
    for i in range(kv_heads):
        @pl.when(at + 4 < row_blocks)
        def _():
            by_line(i).wait_recv()
            parts[0, i] = parts[0, i] + linerecv[i].astype(f32)

    dk = jnp.concatenate([parts[0, i, :, :HEAD_SIZE] for i in range(kv_heads)], axis=1)
    dv = jnp.concatenate([parts[0, i, :, HEAD_SIZE:] for i in range(kv_heads)], axis=1)
    dkl = rotated(dk, cosine, -sine).astype(bf16)
    dvl = dv.astype(bf16)
    back = back + dot_nt(dkl, wk[...]) + dot_nt(dvl, wv[...])
    ysend[...] = back.astype(bf16)
    swap = pltpu.make_async_remote_copy(
        ysend, yrecv, ysem.at[0], ysem.at[1], device_id=(dp, 1 - t), device_id_type=MESH
    )
    swap.start()
    dgain1 = jnp.sum(back * normed1, axis=0, keepdims=True)
    row = lax.broadcasted_iota(jnp.int32, small.shape, 0)
    small = jnp.where(row == EXPERTS + 1, dgain1, small)
    small = jnp.concatenate([small, jnp.zeros((128 - small.shape[0], width), f32)], axis=0)
    small_t = small.T.astype(bf16)
    for i in range(4):
        block = jnp.concatenate(
            [dot_nn(rowst[i], dkl).astype(bf16), dot_nn(rowst[i], dvl).astype(bf16),
             small_t[i * 4 * rows : (i + 1) * 4 * rows]],
            axis=1,
        )
        tail.part[2 * i : 2 * i + 2] = block.reshape(2, 2, rows, 2 * kv_width + 128)
    tail.start()
    q_low.third()
    tail.second()
    q_high.third()
    out_ref[...] = outs.total()
    swap.wait()
    grad = ysend[...].astype(f32) + yrecv[...].astype(f32)
    scaled = grad * as_row(gain1_ref)
    inner = jnp.mean(scaled * x, axis=1, keepdims=True)
    step = inverse1 * scaled - normed1 * (inverse1 * inverse1) * inner
    dtok_ref[...] = (mgrad[...] + step).astype(bf16)
    merge(2)
    tail.third()
    for k in range(LINE):
        shared(k).start()
    query_ref[:, :half_width] = q_low.total()
    query_ref[:, half_width:] = q_high.total()
    sums = tail.total()
    rest_ref[...] = sums
    both = sums[:, 2 * kv_width :]
    for k in range(LINE):
        shared(k).wait_recv()
        both = both + gbuf[k].astype(f32)
    lane = lax.broadcasted_iota(jnp.int32, (rows, 128), 1)
    rest_ref[:, 2 * kv_width :] = jnp.where(lane == EXPERTS + 1, both, sums[:, 2 * kv_width :])
    for p in range(3):
        keep_own(p).wait()
        for k, n in places:
            deal(p, k, n).wait()
    for i in range(kv_heads):
        for n in range(2):
            @pl.when(at >= 1 + 2 * n)
            def _():
                by_core(n, i).wait_send()

        @pl.when(pair_sends)
        def _():
            by_pair(i).wait_send()

        @pl.when(at >= 4)
        def _():
            by_line(i).wait_send()

    for k in range(LINE):
        shared(k).wait_send()
    for s in (outs, q_low, q_high, tail):
        s.finish()


def back_call(grads, opart, dh2, dprob, router, routes, h2, middle, x, dy, gain1, gain2, wr, mixed, mixedt,
              q, kv, lse, docrow, turns, wq, wk, wv, wo):
    tokens, width = x.shape
    q_width, kv_width = wq.shape[1], wk.shape[1]
    heads, kv_heads = q_width // HEAD_SIZE, kv_width // HEAD_SIZE
    group = heads // kv_heads
    reach = kv.shape[0] - 1
    keys = (reach + 1) * tokens
    rows = width // EXPERTS
    ff = grads.shape[-1]
    vmem = pl.BlockSpec(memory_space=pltpu.VMEM)
    hbm = pl.BlockSpec(memory_space=pl.ANY)
    shape = jax.ShapeDtypeStruct
    dma = pltpu.SemaphoreType.DMA
    return pl.pallas_call(
        back_kernel,
        out_shape=(
            shape((tokens, width), bf16),
            shape((tokens, width), bf16),
            shape((2 * LINE, 3, rows, ff), bf16),
            shape((rows, q_width), f32),
            shape((rows, q_width), f32),
            shape((rows, 2 * kv_width + 128), f32),
        ),
        in_specs=[hbm, vmem, hbm] + [vmem] * 16 + [hbm, hbm, hbm, hbm, vmem],
        out_specs=(vmem, vmem, hbm, vmem, vmem, vmem),
        scratch_shapes=[
            pltpu.VMEM((tokens, 256), f32),
            pltpu.VMEM((width, q_width), bf16),
            pltpu.VMEM((width, kv_width), bf16),
            pltpu.VMEM((width, kv_width), bf16),
            pltpu.VMEM((kv_heads, keys, HEAD_SIZE), bf16),
            pltpu.VMEM((kv_heads, keys, HEAD_SIZE), bf16),
            pltpu.VMEM((kv_heads, HEAD_SIZE, keys), bf16),
            pltpu.VMEM((kv_heads, group * tokens, HEAD_SIZE), bf16),
            pltpu.VMEM((heads, HEAD_SIZE, tokens), bf16),
            pltpu.VMEM((heads, HEAD_SIZE, tokens), bf16),
            pltpu.VMEM((kv_heads, group * tokens, HEAD_SIZE), bf16),
            pltpu.VMEM((16, tokens), f32),
            pltpu.VMEM((keys, tokens), f32),
            pltpu.VMEM((keys, group * tokens), bf16),
            pltpu.VMEM((keys, group * tokens), bf16),
            pltpu.VMEM((heads, HEAD_SIZE, tokens), f32),
            pltpu.VMEM((2, kv_heads, tokens, 128), bf16),
            pltpu.VMEM((2, kv_heads, tokens, 128), bf16),
            pltpu.VMEM((kv_heads, tokens, 128), bf16),
            pltpu.VMEM((kv_heads, tokens, 128), bf16),
            pltpu.VMEM((kv_heads, tokens, 128), bf16),
            pltpu.VMEM((kv_heads, tokens, 128), bf16),
            pltpu.VMEM((3, kv_heads, tokens, 128), f32),
            pltpu.VMEM((4, width // 4, tokens), bf16),
            pltpu.VMEM((tokens, width), f32),
            pltpu.VMEM((tokens, width), bf16),
            pltpu.VMEM((tokens, width), bf16),
            pltpu.VMEM((tokens, width), bf16),
            pltpu.VMEM((LINE, rows, 128), bf16),
            pltpu.VMEM((2, LINE, 2, rows, ff), bf16),
            pltpu.VMEM((2, LINE, 2, rows, ff), bf16),
            dma((5,)),
            dma((3, 2 * LINE)),
            dma((3, 2 * LINE)),
            dma((5,)),
            dma((2, 2)),
            dma((reach, kv_heads)),
            dma((reach, kv_heads)),
            dma((6,)),
            dma((2, LINE)),
        ]
        + scatter_bufs(rows, q_width)
        + scatter_bufs(rows, q_width // 2)
        + scatter_bufs(rows, q_width // 2)[1:]
        + scatter_bufs(rows, 2 * kv_width + 128)
        + scatter_sems() * 4,
        compiler_params=pltpu.CompilerParams(
            collective_id=2, has_side_effects=True, vmem_limit_bytes=VMEM_LIMIT
        ),
        name="backward",
    )(grads, opart, dh2, dprob, router, routes, h2, middle, x, dy, gain1, gain2, wr, mixed, mixedt,
      q, kv, lse, docrow, turns, wq, wk, wv, wo)


def rope_table():
    half = HEAD_SIZE // 2
    freqs = rope_base ** (-2.0 * np.arange(half) / HEAD_SIZE)
    angle = np.arange(ROW_LENGTH)[:, None] * freqs[None, :]
    cosine, sine = np.cos(angle), np.sin(angle)
    table = np.concatenate([cosine] * 4 + [-sine, sine] * 2, axis=1)
    return jnp.asarray(table, dtype=f32)


def final_kernel(
    output_ref, dtok_ref, experts_ref, dout_ref, query_ref, rest_ref,
    o_output, o_dtok, o_gain1, o_gain2, o_query, o_key, o_value, o_out, o_router, o_gate, o_up,
    o_down,
):
    o_output[...] = output_ref[...]
    o_dtok[...] = dtok_ref[...]
    ff = o_gate.shape[-1]
    for n in range(2):
        cols = slice(n * ff, (n + 1) * ff)
        o_down[0, n, 0] = experts_ref[0, 0, :, cols].astype(f32)
        o_gate[0, n, 0] = experts_ref[0, 1, :, cols].astype(f32)
        o_up[0, n, 0] = experts_ref[0, 2, :, cols].astype(f32)

    @pl.when((pl.program_id(0) == 0) & (pl.program_id(1) == 0))
    def _():
        kv_width = o_key.shape[1]
        o_query[...] = query_ref[...]
        o_out[...] = dout_ref[...]
        rest = rest_ref[...]
        o_key[...] = rest[:, :kv_width]
        o_value[...] = rest[:, kv_width : 2 * kv_width]
        small = rest[:, 2 * kv_width :]
        small = small.T
        o_router[...] = small[:EXPERTS]
        o_gain2[...] = small[EXPERTS : EXPERTS + 1]
        o_gain1[...] = small[EXPERTS + 1 : EXPERTS + 2]


def final_call(output, dtok, experts, dout, query, rest):
    tokens, width = output.shape
    rows, q_width = query.shape
    kv_width = (rest.shape[1] - 128) // 2
    ff = experts.shape[3] // 2
    piece = tokens // (2 * LINE)
    shape = jax.ShapeDtypeStruct
    whole = lambda *dims: pl.BlockSpec(dims, lambda z, c: (0,) * len(dims))
    strip = pl.BlockSpec((piece, width), lambda z, c: (2 * z + c, 0))
    each = lambda *dims: pl.BlockSpec((1, 2, 1) + dims, lambda z, c: (z, 0, c, 0, 0))
    outs = pl.pallas_call(
        final_kernel,
        grid=(LINE, 2),
        out_shape=(
            shape((tokens, width), bf16),
            shape((tokens, width), bf16),
            shape((1, rows), f32),
            shape((1, rows), f32),
            shape((rows, q_width), f32),
            shape((rows, kv_width), f32),
            shape((rows, kv_width), f32),
            shape((rows, q_width), f32),
            shape((EXPERTS, rows), f32),
            shape((LINE, 2, 2, rows, ff), f32),
            shape((LINE, 2, 2, rows, ff), f32),
            shape((LINE, 2, 2, rows, ff), f32),
        ),
        in_specs=[
            strip,
            strip,
            pl.BlockSpec((1, 3, rows, 2 * ff), lambda z, c: (2 * z + c, 0, 0, 0)),
            whole(rows, q_width),
            whole(rows, q_width),
            whole(rows, 2 * kv_width + 128),
        ],
        out_specs=(
            strip,
            strip,
            whole(1, rows),
            whole(1, rows),
            whole(rows, q_width),
            whole(rows, kv_width),
            whole(rows, kv_width),
            whole(rows, q_width),
            whole(EXPERTS, rows),
            each(rows, ff),
            each(rows, ff),
            each(rows, ff),
        ),
        compiler_params=pltpu.CompilerParams(vmem_limit_bytes=VMEM_LIMIT),
        name="final",
    )(output, dtok, experts, dout, query, rest)
    outs = list(outs)
    outs[2], outs[3] = outs[2].reshape(rows), outs[3].reshape(rows)
    for i in range(9, 12):
        outs[i] = outs[i].reshape((EXPERTS,) + outs[i].shape[3:])
    outs[7], outs[8], outs[11] = outs[7].T, outs[8].T, jnp.swapaxes(outs[11], 1, 2)
    return tuple(outs)


def own_rows(block, axis):
    size = lax.axis_size("dp")
    groups = size // EXPERTS
    if groups == 1:
        return block
    members = [[r * EXPERTS + m for m in range(EXPERTS)] for r in range(groups)]
    across = [[r * EXPERTS + m for r in range(groups)] for m in range(EXPERTS)]
    block = jnp.moveaxis(block, axis, 0).astype(bf16)
    full = lax.all_gather(block, "dp", axis=0, tiled=True, axis_index_groups=members)
    full = full.reshape((groups, EXPERTS, full.shape[0] // size) + full.shape[1:])
    member = lax.rem(lax.axis_index("dp"), EXPERTS)
    mine = lax.dynamic_index_in_dim(full, member, 1, keepdims=False).astype(f32)
    mine = lax.psum_scatter(
        mine, "dp", scatter_dimension=0, tiled=False, axis_index_groups=across
    )
    return jnp.moveaxis(mine, 0, axis)


def per_device(
    tokens,
    cotangent,
    document_numbers,
    valid,
    routes,
    gain_attn,
    gain_moe,
    w_query,
    key_weight,
    value_weight,
    w_out,
    w_router,
    w_gate,
    w_up,
    w_down,
):
    turns = rope_table()
    router_w = w_router.T
    tags = document_numbers[None, :]
    names = routes.T
    (
        h2, middle, router, gates, gates_t, query_rows, kv, lse, mixed, mixed_t, dy, all_dy
    ) = attn_call(
        tokens, cotangent, valid[None, :], tags, names, gain_attn, gain_moe,
        w_query, key_weight, value_weight, w_out, router_w, turns,
    )
    opart, dh2, dprob, grads = moe_call(
        h2, dy, gates, gates_t, w_gate, w_up, w_down,
        all_dy,
    )
    output, d_tokens, experts, d_out, d_query, rest = back_call(
        grads, opart, dh2, dprob, router, names, h2, middle, tokens, dy, gain_attn, gain_moe,
        router_w, mixed, mixed_t, query_rows, kv, lse, tags, turns,
        w_query, key_weight, value_weight, w_out,
    )
    return final_call(
        output, d_tokens, own_rows(experts, 2), own_rows(d_out, 0), own_rows(d_query, 0),
        own_rows(rest, 0),
    )


def solution(mesh):
    in_specs = (
        P("dp", None),
        P("dp", None),
        P("dp"),
        P("dp"),
        P("dp", None),
        P(),
        P(),
        P(None, "tensor"),
        P(None, "tensor"),
        P(None, "tensor"),
        P("tensor", None),
        P(),
        P(None, None, "tensor"),
        P(None, None, "tensor"),
        P(None, "tensor", None),
    )
    out_specs = (
        P("dp", None),
        P("dp", None),
        P("dp"),
        P("dp"),
        P("dp", "tensor"),
        P("dp", "tensor"),
        P("dp", "tensor"),
        P("tensor", "dp"),
        P("dp", None),
        P(None, "dp", "tensor"),
        P(None, "dp", "tensor"),
        P(None, "tensor", "dp"),
    )
    return jax.shard_map(
        per_device, mesh=mesh, in_specs=in_specs, out_specs=out_specs, check_vma=False
    )
```

```python
import jax
import jax.numpy as jnp
import numpy as np
from jax import lax
from jax.experimental import pallas as pl
from jax.experimental.pallas import tpu as pltpu
from jax.sharding import PartitionSpec as P

HEAD_SIZE = 64
EXPERTS = 16
ROW_LENGTH = 2048
WINDOW = 1024
norm_eps = 1e-06
rope_base = 10000.0
masked_score = -1e30
MESH = pl.DeviceIdType.MESH
f32 = jnp.float32
bf16 = jnp.bfloat16
LINE = 4
VMEM_LIMIT = 63 * 2**20


def dot_nn(a,b): return lax.dot_general(a,b,(((1,),(0,)),((),())),preferred_element_type=f32)
def dot_nt(a,b): return lax.dot_general(a,b,(((1,),(1,)),((),())),preferred_element_type=f32)

def place():
    dp=lax.axis_index("dp"); t=lax.axis_index("tensor")
    m=lax.rem(dp,EXPERTS); base=dp-m
    a=m//4; b=lax.rem(m//2,2); c=lax.rem(m,2)
    return base,a,b,c,t

def near(a,j):
    low=(a<2).astype(jnp.int32)
    z=a*low+(3-a)*(1-low)
    o=j+z*((j==0)*1-(j==1)*1)
    return o*low+(3-o)*(1-low)

class Gather:
    def __init__(self, buf, sems, halves, sides):
        self.buf = buf
        self.sides = sides
        self.recv, self.srecv, self.up, self.dn, self.cx, self.sy, self.sc = sems
        self.halves = halves
        self.rows = buf.shape[1] // halves
        self.cols = buf.shape[2] // 2
        self.base, self.a, self.b, self.c, self.t = place()

    def slot(self, j):
        return near(self.a, j) * 2 + self.c

    def send(self, s, h, side, done, sem, a, c, t):
        first = pl.multiple_of(side * self.cols, 128)
        ref = self.buf.at[s, pl.ds(h * self.rows, self.rows), pl.ds(first, self.cols)]
        return pltpu.make_async_remote_copy(
            src_ref=ref, dst_ref=ref, send_sem=sem, recv_sem=done.at[s, h],
            device_id=(self.base + a * 4 + self.b * 2 + c, t), device_id_type=MESH,
        )

    def main(self, s, h, sem, a, c):
        return self.send(s, h, self.t, self.recv, sem, a, c, self.t)

    def over(self, s, h, sem):
        return self.send(s, h, self.t, self.srecv, sem, self.a, self.c, 1 - self.t)

    def aside(self, s, h, sem):
        return self.send(s, h, 1 - self.t, self.srecv, sem, self.a, 1 - self.c, self.t)

    def event(self, j, h):
        a, c = self.a, self.c
        z, s = near(a, j), self.slot(j)
        if j:
            self.main(s, h, self.cx.at[j, h], a, 1 - c).wait_recv()

        @pl.when((z <= a) & (a < LINE - 1))
        def _():
            self.main(s, h, self.up.at[j, h], a + 1, c).start()

        @pl.when((z >= a) & (a > 0))
        def _():
            self.main(s, h, self.dn.at[j, h], a - 1, c).start()

        self.main(s, h, self.cx.at[j, h], a, 1 - c).start()
        if j == 0:
            self.aside(s, h, self.sc.at[j, h]).start()
        elif j < self.sides:
            self.over(s, h, self.sy.at[j, h]).start()

    def late(self, j, h):
        self.over(self.slot(j), h, self.sy.at[j, h]).start()

    def hop(self, k, h):
        middle = (self.a > 0) & (self.a < LINE - 1)

        @pl.when(jnp.logical_not(middle))
        def _():
            self.event(k, h)

        if k < LINE - 1:
            @pl.when(middle)
            def _():
                if k == 1:
                    self.event(1, h)
                self.event(k + 1, h)

    def sevent(self, j, h):
        s = self.slot(j)
        self.aside(s, h, self.sc.at[j, h]).wait_recv()
        self.aside(s, h, self.sc.at[j, h]).start()

    def from_core(self, j, h):
        s = near(self.a, j) * 2 + 1 - self.c
        self.main(s, h, self.cx.at[0, h], self.a, 1 - self.c).wait_recv()
        if isinstance(j, int) and j >= self.sides:
            return
        self.aside(s, h, self.sc.at[0, h]).wait_recv()

    def late_from_core(self, j, h):
        s = near(self.a, j) * 2 + 1 - self.c
        self.aside(s, h, self.sc.at[0, h]).wait_recv()

    def finish_late(self, first):
        for j in range(first, LINE):
            for h in range(self.halves):
                self.over(self.slot(j), h, self.sy.at[j, h]).wait_send()
                self.aside(self.slot(j), h, self.sc.at[j, h]).wait_send()

    def finish(self):
        a, c = self.a, self.c
        for j in range(LINE):
            z, s = near(a, j), self.slot(j)
            for h in range(self.halves):
                @pl.when((z <= a) & (a < LINE - 1))
                def _():
                    self.main(s, h, self.up.at[j, h], a + 1, c).wait_send()

                @pl.when((z >= a) & (a > 0))
                def _():
                    self.main(s, h, self.dn.at[j, h], a - 1, c).wait_send()

                self.main(s, h, self.cx.at[j, h], a, 1 - c).wait_send()
                if 0 < j < self.sides:
                    self.over(s, h, self.sy.at[j, h]).wait_send()
                if j < self.sides:
                    self.aside(s, h, self.sc.at[j, h]).wait_send()


def gather_sems(halves):
    dma = pltpu.SemaphoreType.DMA
    return [dma((2 * LINE, halves))] * 2 + [dma((LINE, halves))] * 5


def planned(gather, plan, tick, more=None):
    todo = dict(hop=gather.hop, s=gather.sevent)
    todo.update(more or {})
    for at, names in plan.items():
        @pl.when(tick == at)
        def _():
            for name, j, h in names:
                todo[name](j, h)


def enter():
    base, a, b, c, t = place()
    barrier = pltpu.get_barrier_semaphore()

    def greet(a, b, c, t):
        peer = (base + a * 4 + b * 2 + c, t)
        pl.semaphore_signal(barrier, inc=1, device_id=peer, device_id_type=MESH)

    @pl.when(a < LINE - 1)
    def _():
        greet(a + 1, b, c, t)

    @pl.when(a > 0)
    def _():
        greet(a - 1, b, c, t)

    greet(a, 1 - b, c, t)
    greet(a, b, 1 - c, t)
    greet(a, b, c, 1 - t)
    ends = (a == 0).astype(jnp.int32) + (a == LINE - 1).astype(jnp.int32)
    pl.semaphore_wait(barrier, 5 - ends)


def as_column(row):
    return jnp.broadcast_to(row.astype(f32), (8, row.shape[1])).T[:, :1]


def as_row(vector_ref):
    return vector_ref[...].reshape(1, vector_ref.shape[0])


def router_rows(wr_ref):
    blank = jnp.zeros((128 - EXPERTS, wr_ref.shape[1]), bf16)
    return jnp.concatenate([wr_ref[...], blank], axis=0)


def named(routes_ref):
    routes = routes_ref[...].astype(f32).T
    lanes = lax.broadcasted_iota(jnp.int32, (routes.shape[0], 128), 1).astype(f32)
    picked = lanes < 0
    for i in range(routes.shape[1]):
        picked = picked | (routes[:, i : i + 1] == lanes)
    return picked


LATE = 3
HEAD_PLAN = {
    0: (("hop", 1, 1),),
    1: (("hop", 2, 0),),
    2: (("hop", 2, 1), ("s", 1, 0)),
    3: (("s", 1, 1),),
}
STEP_PLAN = dict(
    queries=(("hop", 1, 0),),
    keys=(),
    project=(),
    exchange=(("hop", 3, 0), ("hop", 3, 1), ("s", 2, 0), ("s", 2, 1)),
    middle=(),
    late=(),
)


def steps(gather, name):
    todo = dict(hop=gather.hop, s=gather.sevent)
    for step, j, h in STEP_PLAN[name]:
        todo[step](j, h)


def swapped(block):
    lane = lax.broadcasted_iota(jnp.int32, block.shape, 1)
    low = lax.rem(lane, HEAD_SIZE) < HEAD_SIZE // 2
    return jnp.where(low, pltpu.roll(block, 128 - HEAD_SIZE // 2, 1), pltpu.roll(block, HEAD_SIZE // 2, 1))


def rotated(rows, cosine, sine):
    pieces = []
    for i in range(rows.shape[1] // 128):
        block = rows[:, 128 * i : 128 * (i + 1)]
        pieces.append(block * cosine + swapped(block) * sine)
    return jnp.concatenate(pieces, axis=1)


def attn_kernel(
    x_ref, cot_ref, valid_ref, docrow_ref, routes_ref, gain1_ref, gain2_ref,
    wq_ref, wk_ref, wv_ref, wo_ref, wr_ref, turns_ref,
    h2_ref, middle_ref, router_ref, gates_ref, gatest_ref, q_ref, kv_ref, lse_ref, mixed_ref, mixedt_ref,
    dy_ref, dyall_ref,
    turns, dyall, kvbuf, wq, wo, kheads, vt, qheads, bias, mixedt, ysend, yrecv,
    wsem, osem, dsem, kvs, kvr, yss, yrs, *sems,
):
    tokens, width = x_ref.shape
    reach = kvbuf.shape[0] - 1
    row_blocks = ROW_LENGTH // tokens
    assert (reach, row_blocks) == (4, 8)
    kv_width = wk_ref.shape[1]
    kv_heads = kv_width // HEAD_SIZE
    group = wq.shape[1] // kv_width
    gather = Gather(dyall, sems, 2, LATE)
    base, a, b, c, t = place()
    me = a * 4 + b * 2 + c
    dp = base + me
    at = lax.rem(dp, row_blocks)
    load_turns = pltpu.make_async_copy(
        turns_ref.at[pl.ds(pl.multiple_of(at * tokens, tokens), tokens)], turns, wsem.at[2]
    )
    load_turns.start()
    loads = [
        pltpu.make_async_copy(wq_ref, wq, wsem.at[0]),
        pltpu.make_async_copy(wo_ref, wo, wsem.at[1]),
    ]
    for copy in loads:
        copy.start()
    dy = (cot_ref[...].astype(f32) * as_column(valid_ref[...])).astype(bf16)
    dyall[a * 2 + c] = dy
    dy_ref[...] = dy

    enter()
    gather.event(0, 0)

    x = x_ref[...].astype(f32)
    inverse = lax.rsqrt(jnp.mean(x * x, axis=1, keepdims=True) + norm_eps)
    h1 = (x * inverse * as_row(gain1_ref)).astype(bf16)
    load_turns.wait()
    cosine, sine = turns[:, :128], turns[:, 128:]
    kvbuf[reach, :tokens, :kv_width] = rotated(dot_nn(h1, wk_ref[...]), cosine, sine).astype(bf16)
    kvbuf[reach, :tokens, kv_width:] = dot_nn(h1, wv_ref[...]).astype(bf16)
    kvbuf[reach, tokens:, :tokens] = jnp.broadcast_to(
        docrow_ref[...].astype(f32), (16, tokens)
    ).astype(bf16)
    kvbuf[reach, tokens:, tokens:] = jnp.zeros((16, kvbuf.shape[2] - tokens), bf16)

    own, two, four = reach, reach - 2, reach - 4

    def pass_on(source, target, step, peer):
        return pltpu.make_async_remote_copy(
            kvbuf.at[source], kvbuf.at[target], kvs.at[step], kvr.at[target],
            device_id=(peer, t), device_id_type=MESH,
        )

    def arrived(target):
        pass_on(own, target, 0, dp).wait_recv()

    halo = [
        (at + 4 < row_blocks, own, four, 0, dp + 4),
        (b == 0, own, two, 1, dp + 2),
        ((b == 1) & (at >= 4), four, two, 1, dp - 2),
        (c == 0, own, reach - 1, 2, dp + 1),
        ((c == 0) & (at >= 2), two, reach - 3, 3, dp + 1),
        ((c == 1) & (at >= 2), two, reach - 1, 2, dp - 1),
        ((c == 1) & (at >= 4), four, reach - 3, 3, dp - 1),
    ]

    def halo_send(source):
        for there, first, *way in halo:
            if first == source:
                @pl.when(there)
                def _():
                    pass_on(first, *way).start()

    halo_send(own)
    for d in range(1, reach + 1):
        @pl.when(at < d)
        def _():
            kvbuf[reach - d] = jnp.zeros(kvbuf.shape[1:], bf16)

    gather.event(0, 1)
    steps(gather, "queries")
    loads[0].wait()
    q = rotated(dot_nn(h1, wq[...]), cosine, sine)
    q_ref[...] = q.astype(bf16)
    q = (q * HEAD_SIZE**-0.5).astype(bf16)
    for i in range(group * kv_heads):
        qheads[i] = q[:, HEAD_SIZE * i : HEAD_SIZE * (i + 1)]

    steps(gather, "keys")

    @pl.when(at >= 4)
    def _():
        arrived(four)

    halo_send(four)

    @pl.when(at >= 2)
    def _():
        arrived(two)

    halo_send(two)
    for d in range(reach, -1, -1):
        s = reach - d
        if d % 2:
            @pl.when(at >= d)
            def _():
                arrived(s)

        far = (
            lax.broadcasted_iota(jnp.int32, (tokens, tokens), 1)
            - lax.broadcasted_iota(jnp.int32, (tokens, tokens), 0)
            + d * tokens
        )
        tags = kvbuf[s, tokens:, :tokens].T[:, :1].astype(f32)
        allowed = (tags == docrow_ref[...].astype(f32)) & (far >= 0) & (far < WINDOW)
        allowed = allowed & (at >= d)
        rows = slice(s * tokens, (s + 1) * tokens)
        bias[rows] = jnp.where(allowed, 0.0, masked_score)
        for i in range(kv_heads):
            cols = slice(HEAD_SIZE * i, HEAD_SIZE * (i + 1))
            kheads[i, rows] = kvbuf[s, :tokens, cols]
        v = kvbuf[s, :tokens, kv_width:].T
        for i in range(kv_heads):
            vt[i, :, rows] = v[HEAD_SIZE * i : HEAD_SIZE * (i + 1)]


    def one_kv(i, carry):
        planned(gather, HEAD_PLAN, i)
        for n in range(group):
            head = i * group + n
            scores = dot_nt(kheads[i], qheads[head]) + bias[...]
            top = jnp.max(scores, axis=0, keepdims=True)
            weights = jnp.exp(scores - top)
            total = jnp.sum(weights, axis=0, keepdims=True)
            mixedt[head] = (dot_nn(vt[i], weights.astype(bf16)) / total).astype(bf16)
            lse_ref[pl.ds(head, 1), :] = top + jnp.log(total)
        return carry

    lax.fori_loop(0, kv_heads, one_kv, 0)
    mixed_t = mixedt[...].reshape(group * kv_width, tokens)
    mixedt_ref[...] = mixed_t
    mixed = mixed_t.T
    mixed_ref[...] = mixed
    loads[1].wait()
    ysend[...] = dot_nn(mixed, wo[...]).astype(bf16)
    swap = pltpu.make_async_remote_copy(
        ysend, yrecv, yss, yrs, device_id=(dp, 1 - t), device_id_type=MESH
    )
    steps(gather, "project")
    swap.start()
    steps(gather, "exchange")
    swap.wait()
    steps(gather, "middle")
    middle = x + (ysend[...].astype(f32) + yrecv[...].astype(f32))
    middle_ref[...] = middle
    inverse = lax.rsqrt(jnp.mean(middle * middle, axis=1, keepdims=True) + norm_eps)
    h2 = (middle * inverse * as_row(gain2_ref)).astype(bf16)
    h2_ref[...] = h2
    logits = dot_nt(h2, router_rows(wr_ref))
    lanes = lax.broadcasted_iota(jnp.int32, (tokens, 128), 1)
    logits = jnp.where(lanes < EXPERTS, logits, masked_score)
    raised = jnp.exp(logits - jnp.max(logits, axis=1, keepdims=True))
    router = raised / jnp.sum(raised, axis=1, keepdims=True)
    router_ref[...] = router
    gates = jnp.where(named(routes_ref), router, 0.0)
    gates_ref[...] = gates
    gatest_ref[...] = gates.T[:EXPERTS]

    def write(j):
        span = pl.ds(2 * near(a, j), 2)
        return pltpu.make_async_copy(dyall.at[span], dyall_ref.at[span], osem.at[j])

    kv_out = pltpu.make_async_copy(kvbuf, kv_ref, osem.at[LINE])
    kv_out.start()
    steps(gather, "late")
    for j in range(LINE):
        for h in range(2):
            gather.from_core(j, h)
        write(j).start()
    for there, *way in halo:
        @pl.when(there)
        def _():
            pass_on(*way).wait_send()

    for j in range(LINE):
        write(j).wait()
    kv_out.wait()
    gather.finish()


def attn_call(x, cot, valid, docrow, routes, gain1, gain2, wq, wk, wv, wo, wr, turns):
    tokens, width = x.shape
    q_width, kv_width = wq.shape[1], wk.shape[1]
    heads, kv_heads = q_width // HEAD_SIZE, kv_width // HEAD_SIZE
    reach = (WINDOW + tokens - 1) // tokens
    keys = (reach + 1) * tokens
    vmem = pl.BlockSpec(memory_space=pltpu.VMEM)
    hbm = pl.BlockSpec(memory_space=pl.ANY)
    shape = jax.ShapeDtypeStruct
    dma = pltpu.SemaphoreType.DMA
    return pl.pallas_call(
        attn_kernel,
        out_shape=(
            shape((tokens, width), bf16),
            shape((tokens, width), f32),
            shape((tokens, 128), f32),
            shape((tokens, 128), f32),
            shape((EXPERTS, tokens), f32),
            shape((tokens, q_width), bf16),
            shape((reach + 1, tokens + 16, 2 * kv_width), bf16),
            shape((16, tokens), f32),
            shape((tokens, q_width), bf16),
            shape((q_width, tokens), bf16),
            shape((tokens, width), bf16),
            shape((2 * LINE, tokens, width), bf16),
        ),
        in_specs=[vmem] * 7 + [hbm, vmem, vmem, hbm, vmem, hbm],
        out_specs=(vmem,) * 6 + (hbm, vmem, vmem, vmem, vmem, hbm),
        scratch_shapes=[
            pltpu.VMEM((tokens, 256), f32),
            pltpu.VMEM((2 * LINE, tokens, width), bf16),
            pltpu.VMEM((reach + 1, tokens + 16, 2 * kv_width), bf16),
            pltpu.VMEM((width, q_width), bf16),
            pltpu.VMEM((q_width, width), bf16),
            pltpu.VMEM((kv_heads, keys, HEAD_SIZE), bf16),
            pltpu.VMEM((kv_heads, HEAD_SIZE, keys), bf16),
            pltpu.VMEM((heads, tokens, HEAD_SIZE), bf16),
            pltpu.VMEM((keys, tokens), f32),
            pltpu.VMEM((heads, HEAD_SIZE, tokens), bf16),
            pltpu.VMEM((tokens, width), bf16),
            pltpu.VMEM((tokens, width), bf16),
            dma((3,)),
            dma((LINE + 1,)),
            dma((2,)),
            dma((reach,)),
            dma((reach,)),
            dma,
            dma,
        ]
        + gather_sems(2),
        compiler_params=pltpu.CompilerParams(
            collective_id=1, has_side_effects=True, vmem_limit_bytes=VMEM_LIMIT
        ),
        name="attention",
    )(x, cot, valid, docrow, routes, gain1, gain2, wq, wk, wv, wo, wr, turns)


def greet_all(base, me, t, beyond=()):
    barrier = pltpu.get_barrier_semaphore()

    def greet(k, carry):
        peer = base + lax.rem(me + k, EXPERTS)
        pl.semaphore_signal(barrier, inc=1, device_id=(peer, t), device_id_type=MESH)
        return carry

    lax.fori_loop(1, EXPERTS, greet, 0)
    for peer in [me, *beyond]:
        pl.semaphore_signal(barrier, inc=1, device_id=(base + peer, 1 - t), device_id_type=MESH)
    pl.semaphore_wait(barrier, EXPERTS + len(beyond))


EXPERT_PLAN = {
    1: (("d", 3, 0), ("d", 3, 1)),
    3: (("hop", 1, 0),),
    5: (("hop", 1, 1),),
    8: (("hop", 2, 0),),
    10: (("hop", 2, 1), ("ds", 3, 0), ("ds", 3, 1)),
    12: (("hop", 3, 0), ("s", 1, 0), ("s", 1, 1)),
    15: (("hop", 3, 1),),
}
PAIR_PLAN = {
    1: (("s", 2, 0), ("s", 2, 1)),
    3: (("s", 3, 0), ("s", 3, 1)),
}


def moe_kernel(
    h2_ref, dy_ref, cg_ref, ct_ref, wg_ref, wu_ref, wd_ref, dyall_ref,
    opart_ref, dh2_ref, dprob_ref, grads_ref,
    h2all, dyall, ctsend, ctall, gbuf, ubuf, dbuf, rawg, rawu, wgt, wut, wdo, cat, glin, ulin, acco, acch, accp, down,
    ysend, yrecv, psend, precv, wsem, lsem, yss, yrs, cts, ctr, xsem, *sems,
):
    tokens = h2_ref.shape[0]
    ff = wdo.shape[0] // 2
    gather = Gather(h2all, sems[:7], 2, LINE)
    dy_gather = Gather(dyall, sems[7:], 2, LINE)
    base, a, b, c, t = place()
    me = a * 4 + b * 2 + c
    mine = a * 2 + c
    load = pltpu.make_async_copy(h2_ref, h2all.at[mine], lsem.at[0])
    load.start()
    load_dy = pltpu.make_async_copy(dyall_ref, dyall, lsem.at[1])
    load_dy.start()
    rows = jnp.broadcast_to(ct_ref[...][:, None, :], (EXPERTS, 8, tokens))
    for i in range(2 * LINE):
        for n in range(2):
            ctsend[i, n] = rows[(i // 2) * 4 + n * 2 + i % 2]
    ctall[mine] = ctsend[mine]

    def row_out(k):
        peer = lax.rem(mine + k, 2 * LINE)
        return pltpu.make_async_remote_copy(
            ctsend.at[peer], ctall.at[mine], cts.at[k], ctr.at[k],
            device_id=(base + (peer // 2) * 4 + b * 2 + lax.rem(peer, 2), t), device_id_type=MESH,
        )

    def weights(e, k):
        sides = ((wg_ref, gbuf), (wu_ref, ubuf), (wd_ref, dbuf))
        return [
            pltpu.make_async_copy(src.at[e], dst.at[k], wsem.at[i, k])
            for i, (src, dst) in enumerate(sides)
        ]

    for copy in weights(0, 0):
        copy.start()
    load_dy.wait()
    greet_all(base, me, t)
    lax.fori_loop(1, 2 * LINE, lambda k, carry: (row_out(k).start(), carry)[1], 0)
    load.wait()
    for h in range(2):
        gather.event(0, h)
    acco[...] = jnp.zeros_like(acco)
    acch[...] = jnp.zeros_like(acch)
    accp[...] = jnp.zeros_like(accp)
    lanes = lax.broadcasted_iota(jnp.int32, (tokens, 128), 1)

    def one_expert(e, carry):
        k = lax.rem(e, 2)
        planned(gather, EXPERT_PLAN, e, dict(d=dy_gather.late, ds=dy_gather.sevent))

        @pl.when(e < EXPERTS - 1)
        def _():
            for copy in weights(e + 1, 1 - k):
                copy.start()

        for copy in weights(e, k):
            copy.wait()

        own = h2all[mine]
        g = dot_nn(own, gbuf[k])
        u = dot_nn(own, ubuf[k])
        p = dot_nt(dy_ref[...], dbuf[k])
        column = jnp.sum(jnp.where(lanes == e, cg_ref[...], 0.0), axis=1, keepdims=True)
        s = 1.0 / (1.0 + jnp.exp(-g))
        act = g * s
        hidden = act * u
        accp[...] += jnp.where(lanes == e, jnp.sum(hidden * p, axis=1, keepdims=True), 0.0)
        hc = (column * hidden).astype(bf16)
        hg = column * p
        dg = (hg * u * s * (1.0 + g * (1.0 - s))).astype(bf16)
        du = (hg * act).astype(bf16)
        acco[...] += dot_nn(hc, dbuf[k])
        acch[...] += dot_nt(dg, gbuf[k]) + dot_nt(du, ubuf[k])
        return carry

    def own_experts():
        copies = []
        for n in range(2):
            e = a * 4 + n * 2 + c
            half = pl.ds(n * ff, ff)
            copies.append(pltpu.make_async_copy(wd_ref.at[e], wdo.at[half], lsem.at[2 + n]))
            copies.append(pltpu.make_async_copy(wg_ref.at[e], rawg.at[n], lsem.at[4 + n]))
            copies.append(pltpu.make_async_copy(wu_ref.at[e], rawu.at[n], lsem.at[6 + n]))
        return copies

    for copy in own_experts():
        copy.start()
    lax.fori_loop(0, EXPERTS, one_expert, 0)
    other = (base + me, 1 - t)
    opart_ref[...] = acco[...].astype(bf16)
    ysend[...] = acch[...].astype(bf16)
    psend[...] = accp[...].T[:EXPERTS]
    swaps = [
        pltpu.make_async_remote_copy(
            src, dst, yss.at[i], yrs.at[i], device_id=other, device_id_type=MESH
        )
        for i, (src, dst) in enumerate(((ysend, yrecv), (psend, precv)))
    ]
    for copy in swaps:
        copy.start()
    lax.fori_loop(1, 2 * LINE, lambda k, carry: (row_out(k).wait(), carry)[1], 0)
    for copy in own_experts():
        copy.wait()
    for n in range(2):
        wgt[n * ff : (n + 1) * ff] = rawg[n].T
        wut[n * ff : (n + 1) * ff] = rawu[n].T

    def one_pair(j, carry):
        planned(gather, PAIR_PLAN, j, dict(d=dy_gather.late, ds=dy_gather.sevent))
        for h in range(2):
            gather.from_core(j, h)
        for q in range(2):
            s = near(a, j) * 2 + q
            h = h2all[s]
            span = pl.ds(pl.multiple_of(s * tokens, 128), tokens)
            glin[s] = dot_nt(wgt[...], h)
            ulin[s] = dot_nt(wut[...], h)
            for n in range(2):
                half = slice(n * ff, (n + 1) * ff)
                g, u = glin[s, half], ulin[s, half]
                row = ctall[s, n, 0:1, :]
                hidden = g * u / (1.0 + jnp.exp(-g))
                cat[0, half, span] = (row * hidden).astype(bf16)
        return carry

    def pull_back(s, carry):
        span = pl.ds(pl.multiple_of(s * tokens, 128), tokens)
        pull = dot_nt(wdo[...], dyall[s])
        for n in range(2):
            half = slice(n * ff, (n + 1) * ff)
            g, u = glin[s, half], ulin[s, half]
            row = ctall[s, n, 0:1, :]
            sig = 1.0 / (1.0 + jnp.exp(-g))
            hg = row * pull[half]
            cat[1, half, span] = (hg * u * sig * (1.0 + g * (1.0 - sig))).astype(bf16)
            cat[2, half, span] = (hg * g * sig).astype(bf16)
        return carry

    lax.fori_loop(0, LINE, one_pair, 0)
    width = h2all.shape[2]
    tile = 4 * (width // EXPERTS)

    def gradient(i, buf):
        def one_tile(n, carry):
            cols = pl.ds(pl.multiple_of(n * tile, 128), tile)
            right = buf[:, :, cols].reshape(2 * LINE * tokens, tile)
            block = dot_nn(cat[i], right).astype(bf16).T
            grads_ref[i, n] = block.reshape(grads_ref.shape[2:])
            return carry

        lax.fori_loop(0, LINE, one_tile, 0)

    for j in range(LATE, LINE):
        for h in range(2):
            dy_gather.late_from_core(j, h)
    gradient(0, dyall)
    cross = pltpu.make_async_remote_copy(
        grads_ref.at[0, :, 1 - b], down, xsem.at[0], xsem.at[1],
        device_id=(base + a * 4 + (1 - b) * 2 + c, t), device_id_type=MESH,
    )
    cross.start()
    lax.fori_loop(0, 2 * LINE, pull_back, 0)
    gradient(1, h2all)
    gradient(2, h2all)
    cross.wait()
    for z in range(LINE):
        both = grads_ref[0, z, b].astype(f32) + down[z].astype(f32)
        grads_ref[0, z, b] = both.astype(bf16)
    for copy in swaps:
        copy.wait()
    dprob_ref[...] = psend[...] + precv[...]
    dh2_ref[...] = ysend[...].astype(f32) + yrecv[...].astype(f32)
    gather.finish()
    dy_gather.finish_late(LATE)


def moe_call(h2, dy, cg, ct, wg, wu, wd, dyall):
    tokens, width = h2.shape
    ff = wg.shape[2]
    rows = width // EXPERTS
    vmem = pl.BlockSpec(memory_space=pltpu.VMEM)
    hbm = pl.BlockSpec(memory_space=pl.ANY)
    shape = jax.ShapeDtypeStruct
    dma = pltpu.SemaphoreType.DMA
    return pl.pallas_call(
        moe_kernel,
        out_shape=(
            shape((tokens, width), bf16),
            shape((tokens, width), f32),
            shape((EXPERTS, tokens), f32),
            shape((3, LINE, 2, 2, rows, 2 * ff), bf16),
        ),
        in_specs=[hbm, vmem, vmem, vmem, hbm, hbm, hbm, hbm],
        out_specs=(vmem, vmem, vmem, vmem),
        scratch_shapes=[
            pltpu.VMEM((2 * LINE, tokens, width), bf16),
            pltpu.VMEM((2 * LINE, tokens, width), bf16),
            pltpu.VMEM((2 * LINE, 2, 8, tokens), f32),
            pltpu.VMEM((2 * LINE, 2, 8, tokens), f32),
            pltpu.VMEM((2, width, ff), bf16),
            pltpu.VMEM((2, width, ff), bf16),
            pltpu.VMEM((2, ff, width), bf16),
            pltpu.VMEM((2, width, ff), bf16),
            pltpu.VMEM((2, width, ff), bf16),
            pltpu.VMEM((2 * ff, width), bf16),
            pltpu.VMEM((2 * ff, width), bf16),
            pltpu.VMEM((2 * ff, width), bf16),
            pltpu.VMEM((3, 2 * ff, 2 * LINE * tokens), bf16),
            pltpu.VMEM((2 * LINE, 2 * ff, tokens), f32),
            pltpu.VMEM((2 * LINE, 2 * ff, tokens), f32),
            pltpu.VMEM((tokens, width), f32),
            pltpu.VMEM((tokens, width), f32),
            pltpu.VMEM((tokens, 128), f32),
            pltpu.VMEM((LINE, 2, rows, 2 * ff), bf16),
            pltpu.VMEM((tokens, width), bf16),
            pltpu.VMEM((tokens, width), bf16),
            pltpu.VMEM((EXPERTS, tokens), f32),
            pltpu.VMEM((EXPERTS, tokens), f32),
            dma((3, 2)),
            dma((8,)),
            dma((2,)),
            dma((2,)),
            dma((2 * LINE,)),
            dma((2 * LINE,)),
            dma((2,)),
        ]
        + gather_sems(2)
        + gather_sems(2),
        compiler_params=pltpu.CompilerParams(
            collective_id=0, has_side_effects=True, vmem_limit_bytes=VMEM_LIMIT
        ),
        name="moe",
    )(h2, dy, cg, ct, wg, wu, wd, dyall)


class Scatter:
    def __init__(self, bufs, sems):
        self.part, self.cbuf, self.keep, self.xbuf, self.last, self.zbuf = bufs
        self.csem, self.xsem, self.zsend, self.zrecv = sems
        self.base, self.a, self.b, self.c, self.t = place()

    def target(self, a, b, c):
        return (self.base + a * 4 + b * 2 + c, self.t)

    def core(self):
        return pltpu.make_async_remote_copy(
            self.part.at[:, 1 - self.c], self.cbuf, self.csem.at[0], self.csem.at[1],
            device_id=self.target(self.a, self.b, 1 - self.c), device_id_type=MESH,
        )

    def cross(self):
        return pltpu.make_async_remote_copy(
            self.keep.at[:, 1 - self.b], self.xbuf, self.xsem.at[0], self.xsem.at[1],
            device_id=self.target(self.a, 1 - self.b, self.c), device_id_type=MESH,
        )

    def along(self, k):
        z = lax.rem(self.a + k, LINE)
        return pltpu.make_async_remote_copy(
            self.last.at[z], self.zbuf.at[k - 1], self.zsend.at[k - 1], self.zrecv.at[k - 1],
            device_id=self.target(z, self.b, self.c), device_id_type=MESH,
        )

    def start(self):
        self.core().start()

    def second(self):
        self.core().wait()

        def add(i, carry):
            for j in range(2):
                mine = self.part[2 * i + j, self.c].astype(f32)
                self.keep[i, j] = (mine + self.cbuf[2 * i + j].astype(f32)).astype(bf16)
            return carry

        lax.fori_loop(0, LINE, add, 0)
        self.cross().start()

    def third(self):
        self.cross().wait()

        def add(i, carry):
            mine = self.keep[i, self.b].astype(f32)
            self.last[i] = (mine + self.xbuf[i].astype(f32)).astype(bf16)
            return carry

        lax.fori_loop(0, LINE, add, 0)
        for k in range(1, LINE):
            self.along(k).start()

    def total(self):
        result = self.last[self.a].astype(f32)
        for k in range(1, LINE):
            self.along(k).wait_recv()
            result = result + self.zbuf[k - 1].astype(f32)
        return result

    def finish(self):
        for k in range(1, LINE):
            self.along(k).wait_send()

    def put(self, matrix, columns):
        def some(i, carry):
            block = dot_nn(matrix[i], columns).astype(bf16)
            self.part[pl.ds(2 * i, 2)] = block.reshape((2,) + self.part.shape[1:])
            return carry

        lax.fori_loop(0, 4, some, 0)


def scatter_bufs(rows, columns):
    shapes = [(8, 2), (8,), (4, 2), (4,), (4,), (3,)]
    return [pltpu.VMEM(s + (rows, columns), bf16) for s in shapes]


def scatter_sems():
    dma = pltpu.SemaphoreType.DMA
    return [dma((2,)), dma((2,)), dma((LINE - 1,)), dma((LINE - 1,))]


def back_kernel(
    grads_ref, opart_ref, dh2_ref, dprob_ref, router_ref, routes_ref, h2_ref, middle_ref, x_ref, dy_ref,
    gain1_ref, gain2_ref, wr_ref, mixed_ref, mixedt_ref, q_ref, kv_ref, lse_ref, docrow_ref,
    turns_ref, wq_ref, wk_ref, wv_ref, wo_ref,
    output_ref, dtok_ref, experts_ref, out_ref, query_ref, rest_ref,
    turns, wq, wk, wv, kheads, vheads, kt, qstack, qt, dmixt, dmixstack, delta, bias, wcat, scat, dqt,
    coresend, corerecv, pairsend, pairrecv, linesend, linerecv, parts, rowst, mgrad, ysend, yrecv, orecv, gbuf, summed, crossed,
    wsem, asend, arecv, lsem, csem, kvs, kvr, ysem, gsem, *rest,
):
    tokens, width = x_ref.shape
    reach = kv_ref.shape[0] - 1
    assert (reach, ROW_LENGTH // tokens) == (4, 8)
    row_blocks = ROW_LENGTH // tokens
    kv_width = wk_ref.shape[1]
    kv_heads = kv_width // HEAD_SIZE
    q_width = wq_ref.shape[1]
    group = q_width // kv_width
    rows = width // EXPERTS
    keys = (reach + 1) * tokens
    outs = Scatter(rest[0:6], rest[23:27])
    q_low = Scatter(rest[6:12], rest[27:31])
    q_high = Scatter(rest[6:7] + rest[12:17], rest[31:35])
    tail = Scatter(rest[17:23], rest[35:39])
    base, a, b, c, t = place()
    me = a * 4 + b * 2 + c
    dp = base + me
    at = lax.rem(dp, row_blocks)
    loads = [
        pltpu.make_async_copy(src, dst, wsem.at[i])
        for i, (src, dst) in enumerate(((wq_ref, wq), (wk_ref, wk), (wv_ref, wv)))
    ]
    for copy in loads:
        copy.start()
    load_turns = pltpu.make_async_copy(
        turns_ref.at[pl.ds(pl.multiple_of(at * tokens, tokens), tokens)], turns, wsem.at[4]
    )
    load_turns.start()
    load_dh2 = pltpu.make_async_copy(dh2_ref, mgrad, wsem.at[3])
    load_dh2.start()
    greet_all(base, me, t, [lax.rem(a + k, LINE) * 4 + b * 2 + c for k in range(1, LINE)])

    def deal(p, k, n):
        z, core = lax.rem(a + k, LINE), lax.rem(c + n, 2)
        source = grads_ref.at[0, z, b, core] if p == 0 else summed.at[p - 1, z, core]
        return pltpu.make_async_remote_copy(
            source, experts_ref.at[a * 2 + c, p], asend.at[p, 2 * k + n], arecv.at[p, 2 * k + n],
            device_id=(base + z * 4 + b * 2 + core, t), device_id_type=MESH,
        )

    def keep_own(p):
        source = grads_ref.at[0, a, b, c] if p == 0 else summed.at[p - 1, a, c]
        return pltpu.make_async_copy(source, experts_ref.at[a * 2 + c, p], lsem.at[p])

    places = [(k, n) for k in range(LINE) for n in range(2) if k or n]

    def deal_out(p):
        keep_own(p).start()
        for k, n in places:
            deal(p, k, n).start()

    def half_load(p):
        return pltpu.make_async_copy(grads_ref.at[p, :, b], summed.at[p - 1], lsem.at[2 + p])

    def cross(p):
        return pltpu.make_async_remote_copy(
            grads_ref.at[p, :, 1 - b], crossed.at[p - 1], csem.at[0, p - 1], csem.at[1, p - 1],
            device_id=(base + a * 4 + (1 - b) * 2 + c, t), device_id_type=MESH,
        )

    def merge(p):
        half_load(p).wait()
        cross(p).wait()

        def add(z, carry):
            for n in range(2):
                both = summed[p - 1, z, n].astype(f32) + crossed[p - 1, z, n].astype(f32)
                summed[p - 1, z, n] = both.astype(bf16)
            return carry

        lax.fori_loop(0, LINE, add, 0)
        deal_out(p)

    cross(1).start()
    half_load(1).start()
    half_load(2).start()
    deal_out(0)
    swap_out = pltpu.make_async_remote_copy(
        opart_ref, orecv, ysem.at[4], ysem.at[5], device_id=(dp, 1 - t), device_id_type=MESH
    )
    swap_out.start()

    router = router_ref[...]
    dprob = jnp.concatenate([dprob_ref[...], jnp.zeros((128 - EXPERTS, tokens), f32)], axis=0).T
    dprob = jnp.where(named(routes_ref), dprob, 0.0)
    dlogits = router * (dprob - jnp.sum(dprob * router, axis=1, keepdims=True))
    dlogits = dlogits.astype(bf16)
    load_dh2.wait()
    grad = mgrad[...] + dot_nn(dlogits, router_rows(wr_ref))
    middle = middle_ref[...]
    inverse = lax.rsqrt(jnp.mean(middle * middle, axis=1, keepdims=True) + norm_eps)
    scaled = grad * as_row(gain2_ref)
    inner = jnp.mean(scaled * middle, axis=1, keepdims=True)
    normed = middle * inverse
    dgain2 = jnp.sum(grad * normed, axis=0, keepdims=True)
    middle_grad = dy_ref[...].astype(f32) + (
        inverse * scaled - normed * (inverse * inverse) * inner
    )
    mgrad[...] = middle_grad
    attn_grad = middle_grad.astype(bf16)
    rowst[...] = attn_grad.T.reshape(rowst.shape)

    outs.put(rowst, mixed_ref[...])
    outs.start()
    dmix_t = dot_nt(wo_ref[...], attn_grad).astype(bf16)
    dmix = dmix_t.T
    both = (dmix_t.astype(f32) * mixedt_ref[...].astype(f32)).reshape(
        kv_heads * group, HEAD_SIZE, tokens
    )
    delta[: kv_heads * group] = jnp.sum(both, axis=1)
    small = jnp.concatenate(
        [dot_nn(dlogits.T, h2_ref[...])[:EXPERTS], dgain2, jnp.zeros((7, width), f32)], axis=0
    )

    q = (q_ref[...].astype(f32) * HEAD_SIZE**-0.5).astype(bf16)
    q_t = q.T
    for i in range(kv_heads):
        for n in range(group):
            head = i * group + n
            cols = slice(HEAD_SIZE * head, HEAD_SIZE * (head + 1))
            span = slice(n * tokens, (n + 1) * tokens)
            qstack[i, span] = q[:, cols]
            qt[head] = q_t[cols]
            dmixstack[i, span] = dmix[:, cols]
            dmixt[head] = dmix_t[cols]
    for d in range(reach, -1, -1):
        s = reach - d
        far = (
            lax.broadcasted_iota(jnp.int32, (tokens, tokens), 1)
            - lax.broadcasted_iota(jnp.int32, (tokens, tokens), 0)
            + d * tokens
        )
        tags = kv_ref[s, tokens:, :tokens].T[:, :1].astype(f32)
        allowed = (tags == docrow_ref[...].astype(f32)) & (far >= 0) & (far < WINDOW)
        allowed = allowed & (at >= d)
        span = slice(s * tokens, (s + 1) * tokens)
        bias[span] = jnp.where(allowed, 0.0, masked_score)
        k_t = kv_ref[s, :tokens, :kv_width].T
        for i in range(kv_heads):
            cols = slice(HEAD_SIZE * i, HEAD_SIZE * (i + 1))
            kheads[i, span] = kv_ref[s, :tokens, cols]
            vheads[i, span] = kv_ref[
                s, :tokens, kv_width + HEAD_SIZE * i : kv_width + HEAD_SIZE * (i + 1)
            ]
            kt[i, :, span] = k_t[cols]

    def shared(k):
        z = lax.rem(a + k, LINE)
        return pltpu.make_async_remote_copy(
            tail.last.at[z, :, pl.ds(2 * kv_width, 128)], gbuf.at[k], gsem.at[0, k], gsem.at[1, k],
            device_id=(base + z * 4 + b * 2 + c, 1 - t), device_id_type=MESH,
        )

    def by_core(n, i):
        return pltpu.make_async_remote_copy(
            coresend.at[n, i], corerecv.at[n, i], kvs.at[n, i], kvr.at[n, i],
            device_id=(base + a * 4 + b * 2 + 1 - c, t), device_id_type=MESH,
        )

    def by_pair(i):
        return pltpu.make_async_remote_copy(
            pairsend.at[i], pairrecv.at[i], kvs.at[2, i], kvr.at[2, i],
            device_id=(base + a * 4 + (1 - b) * 2 + c, t), device_id_type=MESH,
        )

    def by_line(i):
        return pltpu.make_async_remote_copy(
            linesend.at[i], linerecv.at[i], kvs.at[3, i], kvr.at[3, i],
            device_id=(dp - 4, t), device_id_type=MESH,
        )

    pair_sends = (b == 1) | (at >= 4)
    pair_takes = (b == 0) | (at >= 4)

    def after_core(i):
        for n in range(2):
            there = (c == 0) | (at >= 2 + 2 * n)
            if n:
                there = there & (at >= 2)

            @pl.when(there)
            def _():
                by_core(n, i).wait_recv()
                share = corerecv[n, i].astype(f32)

                @pl.when(c == 0)
                def _():
                    parts[n, i] = parts[n, i] + share

                @pl.when(c == 1)
                def _():
                    parts[n + 1, i] = parts[n + 1, i] + share

        @pl.when(pair_sends)
        def _():
            pairsend[i] = parts[1, i].astype(bf16)
            by_pair(i).start()

    def after_pair(i):
        @pl.when(pair_takes)
        def _():
            by_pair(i).wait_recv()
            share = pairrecv[i].astype(f32)

            @pl.when(b == 0)
            def _():
                parts[0, i] = parts[0, i] + share

            @pl.when(b == 1)
            def _():
                parts[2, i] = parts[2, i] + share

        @pl.when(at >= 4)
        def _():
            linesend[i] = parts[2, i].astype(bf16)
            by_line(i).start()

    def one_kv(i, carry):
        for n in range(group):
            head = i * group + n
            scores = dot_nn(kheads[i], qt[head]) + bias[...]
            weights = jnp.exp(scores - lse_ref[pl.ds(head, 1), :])
            pulled = dot_nn(vheads[i], dmixt[head])
            cols = slice(n * tokens, (n + 1) * tokens)
            wcat[:, cols] = weights.astype(bf16)
            scat[:, cols] = (weights * (pulled - delta[pl.ds(head, 1), :])).astype(bf16)
        dv = dot_nn(wcat[...], dmixstack[i])
        dk = dot_nn(scat[...], qstack[i])
        dq = dot_nn(kt[i], scat[...])
        for n in range(group):
            dqt[i * group + n] = dq[:, n * tokens : (n + 1) * tokens]
        dkv = jnp.concatenate([dk, dv], axis=1)
        for d in range(reach + 1):
            share = dkv[(reach - d) * tokens : (reach - d + 1) * tokens]
            if d % 2:
                coresend[d // 2, i] = share.astype(bf16)

                @pl.when(at >= d)
                def _():
                    by_core(d // 2, i).start()
            else:
                parts[d // 2, i] = share

        @pl.when(i >= 1)
        def _():
            after_core(i - 1)

        @pl.when(i == 1)
        def _():
            outs.second()

        @pl.when(i == 3)
        def _():
            q_low.second()
            merge(1)

        return carry

    load_turns.wait()
    cosine, sine = turns[:, :128], turns[:, 128:]
    x = x_ref[...].astype(f32)
    inverse1 = lax.rsqrt(jnp.mean(x * x, axis=1, keepdims=True) + norm_eps)
    normed1 = x * inverse1
    rowst[...] = (normed1 * as_row(gain1_ref)).astype(bf16).T.reshape(rowst.shape)
    half = kv_heads // 2
    half_width = q_width // 2

    def query_grad(first):
        heads = dqt[first * group : (first + half) * group]
        grad = heads.reshape(half_width, tokens).T * HEAD_SIZE**-0.5
        return rotated(grad, cosine, -sine).astype(bf16)

    lax.fori_loop(0, half, one_kv, 0)
    low = query_grad(0)
    q_low.put(rowst, low)
    q_low.start()
    lax.fori_loop(half, kv_heads, one_kv, 0)
    high = query_grad(half)
    q_high.put(rowst, high)
    q_high.start()
    after_core(kv_heads - 1)
    swap_out.wait()
    total = opart_ref[...].astype(f32) + orecv[...].astype(f32)
    output_ref[...] = (middle_ref[...] + total).astype(bf16)
    for copy in loads:
        copy.wait()
    back = dot_nt(low, wq[:, :half_width]) + dot_nt(high, wq[:, half_width:])
    q_high.second()
    cross(2).start()
    for i in range(kv_heads):
        after_pair(i)
    outs.third()
    for i in range(kv_heads):
        @pl.when(at + 4 < row_blocks)
        def _():
            by_line(i).wait_recv()
            parts[0, i] = parts[0, i] + linerecv[i].astype(f32)

    dk = jnp.concatenate([parts[0, i, :, :HEAD_SIZE] for i in range(kv_heads)], axis=1)
    dv = jnp.concatenate([parts[0, i, :, HEAD_SIZE:] for i in range(kv_heads)], axis=1)
    dkl = rotated(dk, cosine, -sine).astype(bf16)
    dvl = dv.astype(bf16)
    back = back + dot_nt(dkl, wk[...]) + dot_nt(dvl, wv[...])
    ysend[...] = back.astype(bf16)
    swap = pltpu.make_async_remote_copy(
        ysend, yrecv, ysem.at[0], ysem.at[1], device_id=(dp, 1 - t), device_id_type=MESH
    )
    swap.start()
    dgain1 = jnp.sum(back * normed1, axis=0, keepdims=True)
    row = lax.broadcasted_iota(jnp.int32, small.shape, 0)
    small = jnp.where(row == EXPERTS + 1, dgain1, small)
    small = jnp.concatenate([small, jnp.zeros((128 - small.shape[0], width), f32)], axis=0)
    small_t = small.T.astype(bf16)
    for i in range(4):
        block = jnp.concatenate(
            [dot_nn(rowst[i], dkl).astype(bf16), dot_nn(rowst[i], dvl).astype(bf16),
             small_t[i * 4 * rows : (i + 1) * 4 * rows]],
            axis=1,
        )
        tail.part[2 * i : 2 * i + 2] = block.reshape(2, 2, rows, 2 * kv_width + 128)
    tail.start()
    q_low.third()
    tail.second()
    q_high.third()
    out_ref[...] = outs.total()
    swap.wait()
    grad = ysend[...].astype(f32) + yrecv[...].astype(f32)
    scaled = grad * as_row(gain1_ref)
    inner = jnp.mean(scaled * x, axis=1, keepdims=True)
    step = inverse1 * scaled - normed1 * (inverse1 * inverse1) * inner
    dtok_ref[...] = (mgrad[...] + step).astype(bf16)
    merge(2)
    tail.third()
    for k in range(LINE):
        shared(k).start()
    query_ref[:, :half_width] = q_low.total()
    query_ref[:, half_width:] = q_high.total()
    sums = tail.total()
    rest_ref[...] = sums
    both = sums[:, 2 * kv_width :]
    for k in range(LINE):
        shared(k).wait_recv()
        both = both + gbuf[k].astype(f32)
    lane = lax.broadcasted_iota(jnp.int32, (rows, 128), 1)
    rest_ref[:, 2 * kv_width :] = jnp.where(lane == EXPERTS + 1, both, sums[:, 2 * kv_width :])
    for p in range(3):
        keep_own(p).wait()
        for k, n in places:
            deal(p, k, n).wait()
    for i in range(kv_heads):
        for n in range(2):
            @pl.when(at >= 1 + 2 * n)
            def _():
                by_core(n, i).wait_send()

        @pl.when(pair_sends)
        def _():
            by_pair(i).wait_send()

        @pl.when(at >= 4)
        def _():
            by_line(i).wait_send()

    for k in range(LINE):
        shared(k).wait_send()
    for s in (outs, q_low, q_high, tail):
        s.finish()


def back_call(grads, opart, dh2, dprob, router, routes, h2, middle, x, dy, gain1, gain2, wr, mixed, mixedt,
              q, kv, lse, docrow, turns, wq, wk, wv, wo):
    tokens, width = x.shape
    q_width, kv_width = wq.shape[1], wk.shape[1]
    heads, kv_heads = q_width // HEAD_SIZE, kv_width // HEAD_SIZE
    group = heads // kv_heads
    reach = kv.shape[0] - 1
    keys = (reach + 1) * tokens
    rows = width // EXPERTS
    ff = grads.shape[-1]
    vmem = pl.BlockSpec(memory_space=pltpu.VMEM)
    hbm = pl.BlockSpec(memory_space=pl.ANY)
    shape = jax.ShapeDtypeStruct
    dma = pltpu.SemaphoreType.DMA
    return pl.pallas_call(
        back_kernel,
        out_shape=(
            shape((tokens, width), bf16),
            shape((tokens, width), bf16),
            shape((2 * LINE, 3, rows, ff), bf16),
            shape((rows, q_width), f32),
            shape((rows, q_width), f32),
            shape((rows, 2 * kv_width + 128), f32),
        ),
        in_specs=[hbm, vmem, hbm] + [vmem] * 16 + [hbm, hbm, hbm, hbm, vmem],
        out_specs=(vmem, vmem, hbm, vmem, vmem, vmem),
        scratch_shapes=[
            pltpu.VMEM((tokens, 256), f32),
            pltpu.VMEM((width, q_width), bf16),
            pltpu.VMEM((width, kv_width), bf16),
            pltpu.VMEM((width, kv_width), bf16),
            pltpu.VMEM((kv_heads, keys, HEAD_SIZE), bf16),
            pltpu.VMEM((kv_heads, keys, HEAD_SIZE), bf16),
            pltpu.VMEM((kv_heads, HEAD_SIZE, keys), bf16),
            pltpu.VMEM((kv_heads, group * tokens, HEAD_SIZE), bf16),
            pltpu.VMEM((heads, HEAD_SIZE, tokens), bf16),
            pltpu.VMEM((heads, HEAD_SIZE, tokens), bf16),
            pltpu.VMEM((kv_heads, group * tokens, HEAD_SIZE), bf16),
            pltpu.VMEM((16, tokens), f32),
            pltpu.VMEM((keys, tokens), f32),
            pltpu.VMEM((keys, group * tokens), bf16),
            pltpu.VMEM((keys, group * tokens), bf16),
            pltpu.VMEM((heads, HEAD_SIZE, tokens), f32),
            pltpu.VMEM((2, kv_heads, tokens, 128), bf16),
            pltpu.VMEM((2, kv_heads, tokens, 128), bf16),
            pltpu.VMEM((kv_heads, tokens, 128), bf16),
            pltpu.VMEM((kv_heads, tokens, 128), bf16),
            pltpu.VMEM((kv_heads, tokens, 128), bf16),
            pltpu.VMEM((kv_heads, tokens, 128), bf16),
            pltpu.VMEM((3, kv_heads, tokens, 128), f32),
            pltpu.VMEM((4, width // 4, tokens), bf16),
            pltpu.VMEM((tokens, width), f32),
            pltpu.VMEM((tokens, width), bf16),
            pltpu.VMEM((tokens, width), bf16),
            pltpu.VMEM((tokens, width), bf16),
            pltpu.VMEM((LINE, rows, 128), bf16),
            pltpu.VMEM((2, LINE, 2, rows, ff), bf16),
            pltpu.VMEM((2, LINE, 2, rows, ff), bf16),
            dma((5,)),
            dma((3, 2 * LINE)),
            dma((3, 2 * LINE)),
            dma((5,)),
            dma((2, 2)),
            dma((reach, kv_heads)),
            dma((reach, kv_heads)),
            dma((6,)),
            dma((2, LINE)),
        ]
        + scatter_bufs(rows, q_width)
        + scatter_bufs(rows, q_width // 2)
        + scatter_bufs(rows, q_width // 2)[1:]
        + scatter_bufs(rows, 2 * kv_width + 128)
        + scatter_sems() * 4,
        compiler_params=pltpu.CompilerParams(
            collective_id=2, has_side_effects=True, vmem_limit_bytes=VMEM_LIMIT
        ),
        name="backward",
    )(grads, opart, dh2, dprob, router, routes, h2, middle, x, dy, gain1, gain2, wr, mixed, mixedt,
      q, kv, lse, docrow, turns, wq, wk, wv, wo)


def rope_table():
    half = HEAD_SIZE // 2
    freqs = rope_base ** (-2.0 * np.arange(half) / HEAD_SIZE)
    angle = np.arange(ROW_LENGTH)[:, None] * freqs[None, :]
    cosine, sine = np.cos(angle), np.sin(angle)
    table = np.concatenate([cosine] * 4 + [-sine, sine] * 2, axis=1)
    return jnp.asarray(table, dtype=f32)


def final_kernel(
    output_ref, dtok_ref, experts_ref, dout_ref, query_ref, rest_ref,
    o_output, o_dtok, o_gain1, o_gain2, o_query, o_key, o_value, o_out, o_router, o_gate, o_up,
    o_down,
):
    o_output[...] = output_ref[...]
    o_dtok[...] = dtok_ref[...]
    ff = o_gate.shape[-1]
    for n in range(2):
        cols = slice(n * ff, (n + 1) * ff)
        o_down[0, n, 0] = experts_ref[0, 0, :, cols].astype(f32)
        o_gate[0, n, 0] = experts_ref[0, 1, :, cols].astype(f32)
        o_up[0, n, 0] = experts_ref[0, 2, :, cols].astype(f32)

    @pl.when((pl.program_id(0) == 0) & (pl.program_id(1) == 0))
    def _():
        kv_width = o_key.shape[1]
        o_query[...] = query_ref[...]
        o_out[...] = dout_ref[...]
        rest = rest_ref[...]
        o_key[...] = rest[:, :kv_width]
        o_value[...] = rest[:, kv_width : 2 * kv_width]
        small = rest[:, 2 * kv_width :]
        small = small.T
        o_router[...] = small[:EXPERTS]
        o_gain2[...] = small[EXPERTS : EXPERTS + 1]
        o_gain1[...] = small[EXPERTS + 1 : EXPERTS + 2]


def final_call(output, dtok, experts, dout, query, rest):
    tokens, width = output.shape
    rows, q_width = query.shape
    kv_width = (rest.shape[1] - 128) // 2
    ff = experts.shape[3] // 2
    piece = tokens // (2 * LINE)
    shape = jax.ShapeDtypeStruct
    whole = lambda *dims: pl.BlockSpec(dims, lambda z, c: (0,) * len(dims))
    strip = pl.BlockSpec((piece, width), lambda z, c: (2 * z + c, 0))
    each = lambda *dims: pl.BlockSpec((1, 2, 1) + dims, lambda z, c: (z, 0, c, 0, 0))
    outs = pl.pallas_call(
        final_kernel,
        grid=(LINE, 2),
        out_shape=(
            shape((tokens, width), bf16),
            shape((tokens, width), bf16),
            shape((1, rows), f32),
            shape((1, rows), f32),
            shape((rows, q_width), f32),
            shape((rows, kv_width), f32),
            shape((rows, kv_width), f32),
            shape((rows, q_width), f32),
            shape((EXPERTS, rows), f32),
            shape((LINE, 2, 2, rows, ff), f32),
            shape((LINE, 2, 2, rows, ff), f32),
            shape((LINE, 2, 2, rows, ff), f32),
        ),
        in_specs=[
            strip,
            strip,
            pl.BlockSpec((1, 3, rows, 2 * ff), lambda z, c: (2 * z + c, 0, 0, 0)),
            whole(rows, q_width),
            whole(rows, q_width),
            whole(rows, 2 * kv_width + 128),
        ],
        out_specs=(
            strip,
            strip,
            whole(1, rows),
            whole(1, rows),
            whole(rows, q_width),
            whole(rows, kv_width),
            whole(rows, kv_width),
            whole(rows, q_width),
            whole(EXPERTS, rows),
            each(rows, ff),
            each(rows, ff),
            each(rows, ff),
        ),
        compiler_params=pltpu.CompilerParams(vmem_limit_bytes=VMEM_LIMIT),
        name="final",
    )(output, dtok, experts, dout, query, rest)
    outs = list(outs)
    outs[2], outs[3] = outs[2].reshape(rows), outs[3].reshape(rows)
    for i in range(9, 12):
        outs[i] = outs[i].reshape((EXPERTS,) + outs[i].shape[3:])
    outs[7], outs[8], outs[11] = outs[7].T, outs[8].T, jnp.swapaxes(outs[11], 1, 2)
    return tuple(outs)


def own_rows(block, axis):
    size = lax.axis_size("dp")
    groups = size // EXPERTS
    if groups == 1:
        return block
    members = [[r * EXPERTS + m for m in range(EXPERTS)] for r in range(groups)]
    across = [[r * EXPERTS + m for r in range(groups)] for m in range(EXPERTS)]
    block = jnp.moveaxis(block, axis, 0).astype(bf16)
    full = lax.all_gather(block, "dp", axis=0, tiled=True, axis_index_groups=members)
    full = full.reshape((groups, EXPERTS, full.shape[0] // size) + full.shape[1:])
    member = lax.rem(lax.axis_index("dp"), EXPERTS)
    mine = lax.dynamic_index_in_dim(full, member, 1, keepdims=False).astype(f32)
    mine = lax.psum_scatter(
        mine, "dp", scatter_dimension=0, tiled=False, axis_index_groups=across
    )
    return jnp.moveaxis(mine, 0, axis)


def per_device(
    tokens,
    cotangent,
    document_numbers,
    valid,
    routes,
    gain_attn,
    gain_moe,
    w_query,
    key_weight,
    value_weight,
    w_out,
    w_router,
    w_gate,
    w_up,
    w_down,
):
    turns = rope_table()
    router_w = w_router.T
    tags = document_numbers[None, :]
    names = routes.T
    (
        h2, middle, router, gates, gates_t, query_rows, kv, lse, mixed, mixed_t, dy, all_dy
    ) = attn_call(
        tokens, cotangent, valid[None, :], tags, names, gain_attn, gain_moe,
        w_query, key_weight, value_weight, w_out, router_w, turns,
    )
    opart, dh2, dprob, grads = moe_call(
        h2, dy, gates, gates_t, w_gate, w_up, w_down,
        all_dy,
    )
    output, d_tokens, experts, d_out, d_query, rest = back_call(
        grads, opart, dh2, dprob, router, names, h2, middle, tokens, dy, gain_attn, gain_moe,
        router_w, mixed, mixed_t, query_rows, kv, lse, tags, turns,
        w_query, key_weight, value_weight, w_out,
    )
    return final_call(
        output, d_tokens, own_rows(experts, 2), own_rows(d_out, 0), own_rows(d_query, 0),
        own_rows(rest, 0),
    )


def solution(mesh):
    in_specs = (
        P("dp", None),
        P("dp", None),
        P("dp"),
        P("dp"),
        P("dp", None),
        P(),
        P(),
        P(None, "tensor"),
        P(None, "tensor"),
        P(None, "tensor"),
        P("tensor", None),
        P(),
        P(None, None, "tensor"),
        P(None, None, "tensor"),
        P(None, "tensor", None),
    )
    out_specs = (
        P("dp", None),
        P("dp", None),
        P("dp"),
        P("dp"),
        P("dp", "tensor"),
        P("dp", "tensor"),
        P("dp", "tensor"),
        P("tensor", "dp"),
        P("dp", None),
        P(None, "dp", "tensor"),
        P(None, "dp", "tensor"),
        P(None, "tensor", "dp"),
    )
    return jax.shard_map(
        per_device, mesh=mesh, in_specs=in_specs, out_specs=out_specs, check_vma=False
    )
```

```python
import jax
import jax.numpy as jnp
import numpy as np
from jax import lax
from jax.experimental import pallas as pl
from jax.experimental.pallas import tpu as pltpu
from jax.sharding import PartitionSpec as P

HEAD_SIZE = 64
EXPERTS = 16
ROW_LENGTH = 2048
WINDOW = 1024
norm_eps = 1e-06
rope_base = 10000.0
masked_score = -1e30
MESH = pl.DeviceIdType.MESH
f32 = jnp.float32
bf16 = jnp.bfloat16
LINE = 4
VMEM_LIMIT = 63 * 2**20


def dot_nn(a,b): return lax.dot_general(a,b,(((1,),(0,)),((),())),preferred_element_type=f32)
def dot_nt(a,b): return lax.dot_general(a,b,(((1,),(1,)),((),())),preferred_element_type=f32)

def place():
    dp=lax.axis_index("dp"); t=lax.axis_index("tensor")
    m=lax.rem(dp,EXPERTS); base=dp-m
    a=m//4; b=lax.rem(m//2,2); c=lax.rem(m,2)
    return base,a,b,c,t

def near(a,j):
    low=(a<2).astype(jnp.int32)
    z=a*low+(3-a)*(1-low)
    o=j+z*((j==0)*1-(j==1)*1)
    return o*low+(3-o)*(1-low)

class Gather:
    def __init__(self, buf, sems, halves, sides):
        self.buf = buf
        self.sides = sides
        self.recv, self.srecv, self.up, self.dn, self.cx, self.sy, self.sc = sems
        self.halves = halves
        self.rows = buf.shape[1] // halves
        self.cols = buf.shape[2] // 2
        self.base, self.a, self.b, self.c, self.t = place()

    def slot(self, j):
        return near(self.a, j) * 2 + self.c

    def send(self, s, h, side, done, sem, a, c, t):
        first = pl.multiple_of(side * self.cols, 128)
        ref = self.buf.at[s, pl.ds(h * self.rows, self.rows), pl.ds(first, self.cols)]
        return pltpu.make_async_remote_copy(
            src_ref=ref, dst_ref=ref, send_sem=sem, recv_sem=done.at[s, h],
            device_id=(self.base + a * 4 + self.b * 2 + c, t), device_id_type=MESH,
        )

    def main(self, s, h, sem, a, c):
        return self.send(s, h, self.t, self.recv, sem, a, c, self.t)

    def over(self, s, h, sem):
        return self.send(s, h, self.t, self.srecv, sem, self.a, self.c, 1 - self.t)

    def aside(self, s, h, sem):
        return self.send(s, h, 1 - self.t, self.srecv, sem, self.a, 1 - self.c, self.t)

    def event(self, j, h):
        a, c = self.a, self.c
        z, s = near(a, j), self.slot(j)
        if j:
            self.main(s, h, self.cx.at[j, h], a, 1 - c).wait_recv()

        @pl.when((z <= a) & (a < LINE - 1))
        def _():
            self.main(s, h, self.up.at[j, h], a + 1, c).start()

        @pl.when((z >= a) & (a > 0))
        def _():
            self.main(s, h, self.dn.at[j, h], a - 1, c).start()

        self.main(s, h, self.cx.at[j, h], a, 1 - c).start()
        if j == 0:
            self.aside(s, h, self.sc.at[j, h]).start()
        elif j < self.sides:
            self.over(s, h, self.sy.at[j, h]).start()

    def late(self, j, h):
        self.over(self.slot(j), h, self.sy.at[j, h]).start()

    def hop(self, k, h):
        middle = (self.a > 0) & (self.a < LINE - 1)

        @pl.when(jnp.logical_not(middle))
        def _():
            self.event(k, h)

        if k < LINE - 1:
            @pl.when(middle)
            def _():
                if k == 1:
                    self.event(1, h)
                self.event(k + 1, h)

    def sevent(self, j, h):
        s = self.slot(j)
        self.aside(s, h, self.sc.at[j, h]).wait_recv()
        self.aside(s, h, self.sc.at[j, h]).start()

    def from_core(self, j, h):
        s = near(self.a, j) * 2 + 1 - self.c
        self.main(s, h, self.cx.at[0, h], self.a, 1 - self.c).wait_recv()
        if isinstance(j, int) and j >= self.sides:
            return
        self.aside(s, h, self.sc.at[0, h]).wait_recv()

    def late_from_core(self, j, h):
        s = near(self.a, j) * 2 + 1 - self.c
        self.aside(s, h, self.sc.at[0, h]).wait_recv()

    def finish_late(self, first):
        for j in range(first, LINE):
            for h in range(self.halves):
                self.over(self.slot(j), h, self.sy.at[j, h]).wait_send()
                self.aside(self.slot(j), h, self.sc.at[j, h]).wait_send()

    def finish(self):
        a, c = self.a, self.c
        for j in range(LINE):
            z, s = near(a, j), self.slot(j)
            for h in range(self.halves):
                @pl.when((z <= a) & (a < LINE - 1))
                def _():
                    self.main(s, h, self.up.at[j, h], a + 1, c).wait_send()

                @pl.when((z >= a) & (a > 0))
                def _():
                    self.main(s, h, self.dn.at[j, h], a - 1, c).wait_send()

                self.main(s, h, self.cx.at[j, h], a, 1 - c).wait_send()
                if 0 < j < self.sides:
                    self.over(s, h, self.sy.at[j, h]).wait_send()
                if j < self.sides:
                    self.aside(s, h, self.sc.at[j, h]).wait_send()


def gather_sems(halves):
    dma = pltpu.SemaphoreType.DMA
    return [dma((2 * LINE, halves))] * 2 + [dma((LINE, halves))] * 5


def planned(gather, plan, tick, more=None):
    todo = dict(hop=gather.hop, s=gather.sevent)
    todo.update(more or {})
    for at, names in plan.items():
        @pl.when(tick == at)
        def _():
            for name, j, h in names:
                todo[name](j, h)


def enter():
    base, a, b, c, t = place()
    barrier = pltpu.get_barrier_semaphore()

    def greet(a, b, c, t):
        peer = (base + a * 4 + b * 2 + c, t)
        pl.semaphore_signal(barrier, inc=1, device_id=peer, device_id_type=MESH)

    @pl.when(a < LINE - 1)
    def _():
        greet(a + 1, b, c, t)

    @pl.when(a > 0)
    def _():
        greet(a - 1, b, c, t)

    greet(a, 1 - b, c, t)
    greet(a, b, 1 - c, t)
    greet(a, b, c, 1 - t)
    ends = (a == 0).astype(jnp.int32) + (a == LINE - 1).astype(jnp.int32)
    pl.semaphore_wait(barrier, 5 - ends)


def as_column(row):
    return jnp.broadcast_to(row.astype(f32), (8, row.shape[1])).T[:, :1]


def as_row(vector_ref):
    return vector_ref[...].reshape(1, vector_ref.shape[0])


def router_rows(wr_ref):
    blank = jnp.zeros((128 - EXPERTS, wr_ref.shape[1]), bf16)
    return jnp.concatenate([wr_ref[...], blank], axis=0)


def named(routes_ref):
    routes = routes_ref[...].astype(f32).T
    lanes = lax.broadcasted_iota(jnp.int32, (routes.shape[0], 128), 1).astype(f32)
    picked = lanes < 0
    for i in range(routes.shape[1]):
        picked = picked | (routes[:, i : i + 1] == lanes)
    return picked


LATE = 3
HEAD_PLAN = {
    0: (("hop", 1, 1),),
    1: (("hop", 2, 0),),
    2: (("hop", 2, 1), ("s", 1, 0)),
    3: (("s", 1, 1),),
}
STEP_PLAN = dict(
    queries=(("hop", 1, 0),),
    keys=(),
    project=(),
    exchange=(("hop", 3, 0), ("hop", 3, 1), ("s", 2, 0), ("s", 2, 1)),
    middle=(),
    late=(),
)


def steps(gather, name):
    todo = dict(hop=gather.hop, s=gather.sevent)
    for step, j, h in STEP_PLAN[name]:
        todo[step](j, h)


def swapped(block):
    lane = lax.broadcasted_iota(jnp.int32, block.shape, 1)
    low = lax.rem(lane, HEAD_SIZE) < HEAD_SIZE // 2
    return jnp.where(low, pltpu.roll(block, 128 - HEAD_SIZE // 2, 1), pltpu.roll(block, HEAD_SIZE // 2, 1))


def rotated(rows, cosine, sine):
    pieces = []
    for i in range(rows.shape[1] // 128):
        block = rows[:, 128 * i : 128 * (i + 1)]
        pieces.append(block * cosine + swapped(block) * sine)
    return jnp.concatenate(pieces, axis=1)


def attn_kernel(
    x_ref, cot_ref, valid_ref, docrow_ref, routes_ref, gain1_ref, gain2_ref,
    wq_ref, wk_ref, wv_ref, wo_ref, wr_ref, turns_ref,
    h2_ref, middle_ref, router_ref, gates_ref, gatest_ref, q_ref, kv_ref, lse_ref, mixed_ref, mixedt_ref,
    dy_ref, dyall_ref,
    turns, dyall, kvbuf, wq, wo, kheads, vt, qheads, bias, mixedt, ysend, yrecv,
    wsem, osem, dsem, kvs, kvr, yss, yrs, *sems,
):
    tokens, width = x_ref.shape
    reach = kvbuf.shape[0] - 1
    row_blocks = ROW_LENGTH // tokens
    assert (reach, row_blocks) == (4, 8)
    kv_width = wk_ref.shape[1]
    kv_heads = kv_width // HEAD_SIZE
    group = wq.shape[1] // kv_width
    gather = Gather(dyall, sems, 2, LATE)
    base, a, b, c, t = place()
    me = a * 4 + b * 2 + c
    dp = base + me
    at = lax.rem(dp, row_blocks)
    load_turns = pltpu.make_async_copy(
        turns_ref.at[pl.ds(pl.multiple_of(at * tokens, tokens), tokens)], turns, wsem.at[2]
    )
    load_turns.start()
    loads = [
        pltpu.make_async_copy(wq_ref, wq, wsem.at[0]),
        pltpu.make_async_copy(wo_ref, wo, wsem.at[1]),
    ]
    for copy in loads:
        copy.start()
    dy = (cot_ref[...].astype(f32) * as_column(valid_ref[...])).astype(bf16)
    dyall[a * 2 + c] = dy
    dy_ref[...] = dy

    enter()
    gather.event(0, 0)

    x = x_ref[...].astype(f32)
    inverse = lax.rsqrt(jnp.mean(x * x, axis=1, keepdims=True) + norm_eps)
    h1 = (x * inverse * as_row(gain1_ref)).astype(bf16)
    load_turns.wait()
    cosine, sine = turns[:, :128], turns[:, 128:]
    kvbuf[reach, :tokens, :kv_width] = rotated(dot_nn(h1, wk_ref[...]), cosine, sine).astype(bf16)
    kvbuf[reach, :tokens, kv_width:] = dot_nn(h1, wv_ref[...]).astype(bf16)
    kvbuf[reach, tokens:, :tokens] = jnp.broadcast_to(
        docrow_ref[...].astype(f32), (16, tokens)
    ).astype(bf16)
    kvbuf[reach, tokens:, tokens:] = jnp.zeros((16, kvbuf.shape[2] - tokens), bf16)

    own, two, four = reach, reach - 2, reach - 4

    def pass_on(source, target, step, peer):
        return pltpu.make_async_remote_copy(
            kvbuf.at[source], kvbuf.at[target], kvs.at[step], kvr.at[target],
            device_id=(peer, t), device_id_type=MESH,
        )

    def arrived(target):
        pass_on(own, target, 0, dp).wait_recv()

    halo = [
        (at + 4 < row_blocks, own, four, 0, dp + 4),
        (b == 0, own, two, 1, dp + 2),
        ((b == 1) & (at >= 4), four, two, 1, dp - 2),
        (c == 0, own, reach - 1, 2, dp + 1),
        ((c == 0) & (at >= 2), two, reach - 3, 3, dp + 1),
        ((c == 1) & (at >= 2), two, reach - 1, 2, dp - 1),
        ((c == 1) & (at >= 4), four, reach - 3, 3, dp - 1),
    ]

    def halo_send(source):
        for there, first, *way in halo:
            if first == source:
                @pl.when(there)
                def _():
                    pass_on(first, *way).start()

    halo_send(own)
    for d in range(1, reach + 1):
        @pl.when(at < d)
        def _():
            kvbuf[reach - d] = jnp.zeros(kvbuf.shape[1:], bf16)

    gather.event(0, 1)
    steps(gather, "queries")
    loads[0].wait()
    q = rotated(dot_nn(h1, wq[...]), cosine, sine)
    q_ref[...] = q.astype(bf16)
    q = (q * HEAD_SIZE**-0.5).astype(bf16)
    for i in range(group * kv_heads):
        qheads[i] = q[:, HEAD_SIZE * i : HEAD_SIZE * (i + 1)]

    steps(gather, "keys")

    @pl.when(at >= 4)
    def _():
        arrived(four)

    halo_send(four)

    @pl.when(at >= 2)
    def _():
        arrived(two)

    halo_send(two)
    for d in range(reach, -1, -1):
        s = reach - d
        if d % 2:
            @pl.when(at >= d)
            def _():
                arrived(s)

        far = (
            lax.broadcasted_iota(jnp.int32, (tokens, tokens), 1)
            - lax.broadcasted_iota(jnp.int32, (tokens, tokens), 0)
            + d * tokens
        )
        tags = kvbuf[s, tokens:, :tokens].T[:, :1].astype(f32)
        allowed = (tags == docrow_ref[...].astype(f32)) & (far >= 0) & (far < WINDOW)
        allowed = allowed & (at >= d)
        rows = slice(s * tokens, (s + 1) * tokens)
        bias[rows] = jnp.where(allowed, 0.0, masked_score)
        for i in range(kv_heads):
            cols = slice(HEAD_SIZE * i, HEAD_SIZE * (i + 1))
            kheads[i, rows] = kvbuf[s, :tokens, cols]
        v = kvbuf[s, :tokens, kv_width:].T
        for i in range(kv_heads):
            vt[i, :, rows] = v[HEAD_SIZE * i : HEAD_SIZE * (i + 1)]


    def one_kv(i, carry):
        planned(gather, HEAD_PLAN, i)
        for n in range(group):
            head = i * group + n
            scores = dot_nt(kheads[i], qheads[head]) + bias[...]
            top = jnp.max(scores, axis=0, keepdims=True)
            weights = jnp.exp(scores - top)
            total = jnp.sum(weights, axis=0, keepdims=True)
            mixedt[head] = (dot_nn(vt[i], weights.astype(bf16)) / total).astype(bf16)
            lse_ref[pl.ds(head, 1), :] = top + jnp.log(total)
        return carry

    lax.fori_loop(0, kv_heads, one_kv, 0)
    mixed_t = mixedt[...].reshape(group * kv_width, tokens)
    mixedt_ref[...] = mixed_t
    mixed = mixed_t.T
    mixed_ref[...] = mixed
    loads[1].wait()
    ysend[...] = dot_nn(mixed, wo[...]).astype(bf16)
    swap = pltpu.make_async_remote_copy(
        ysend, yrecv, yss, yrs, device_id=(dp, 1 - t), device_id_type=MESH
    )
    steps(gather, "project")
    swap.start()
    steps(gather, "exchange")
    swap.wait()
    steps(gather, "middle")
    middle = x + (ysend[...].astype(f32) + yrecv[...].astype(f32))
    middle_ref[...] = middle
    inverse = lax.rsqrt(jnp.mean(middle * middle, axis=1, keepdims=True) + norm_eps)
    h2 = (middle * inverse * as_row(gain2_ref)).astype(bf16)
    h2_ref[...] = h2
    logits = dot_nt(h2, router_rows(wr_ref))
    lanes = lax.broadcasted_iota(jnp.int32, (tokens, 128), 1)
    logits = jnp.where(lanes < EXPERTS, logits, masked_score)
    raised = jnp.exp(logits - jnp.max(logits, axis=1, keepdims=True))
    router = raised / jnp.sum(raised, axis=1, keepdims=True)
    router_ref[...] = router
    gates = jnp.where(named(routes_ref), router, 0.0)
    gates_ref[...] = gates
    gatest_ref[...] = gates.T[:EXPERTS]

    def write(j):
        span = pl.ds(2 * near(a, j), 2)
        return pltpu.make_async_copy(dyall.at[span], dyall_ref.at[span], osem.at[j])

    kv_out = pltpu.make_async_copy(kvbuf, kv_ref, osem.at[LINE])
    kv_out.start()
    steps(gather, "late")
    for j in range(LINE):
        for h in range(2):
            gather.from_core(j, h)
        write(j).start()
    for there, *way in halo:
        @pl.when(there)
        def _():
            pass_on(*way).wait_send()

    for j in range(LINE):
        write(j).wait()
    kv_out.wait()
    gather.finish()


def attn_call(x, cot, valid, docrow, routes, gain1, gain2, wq, wk, wv, wo, wr, turns):
    tokens, width = x.shape
    q_width, kv_width = wq.shape[1], wk.shape[1]
    heads, kv_heads = q_width // HEAD_SIZE, kv_width // HEAD_SIZE
    reach = (WINDOW + tokens - 1) // tokens
    keys = (reach + 1) * tokens
    vmem = pl.BlockSpec(memory_space=pltpu.VMEM)
    hbm = pl.BlockSpec(memory_space=pl.ANY)
    shape = jax.ShapeDtypeStruct
    dma = pltpu.SemaphoreType.DMA
    return pl.pallas_call(
        attn_kernel,
        out_shape=(
            shape((tokens, width), bf16),
            shape((tokens, width), f32),
            shape((tokens, 128), f32),
            shape((tokens, 128), f32),
            shape((EXPERTS, tokens), f32),
            shape((tokens, q_width), bf16),
            shape((reach + 1, tokens + 16, 2 * kv_width), bf16),
            shape((16, tokens), f32),
            shape((tokens, q_width), bf16),
            shape((q_width, tokens), bf16),
            shape((tokens, width), bf16),
            shape((2 * LINE, tokens, width), bf16),
        ),
        in_specs=[vmem] * 7 + [hbm, vmem, vmem, hbm, vmem, hbm],
        out_specs=(vmem,) * 6 + (hbm, vmem, vmem, vmem, vmem, hbm),
        scratch_shapes=[
            pltpu.VMEM((tokens, 256), f32),
            pltpu.VMEM((2 * LINE, tokens, width), bf16),
            pltpu.VMEM((reach + 1, tokens + 16, 2 * kv_width), bf16),
            pltpu.VMEM((width, q_width), bf16),
            pltpu.VMEM((q_width, width), bf16),
            pltpu.VMEM((kv_heads, keys, HEAD_SIZE), bf16),
            pltpu.VMEM((kv_heads, HEAD_SIZE, keys), bf16),
            pltpu.VMEM((heads, tokens, HEAD_SIZE), bf16),
            pltpu.VMEM((keys, tokens), f32),
            pltpu.VMEM((heads, HEAD_SIZE, tokens), bf16),
            pltpu.VMEM((tokens, width), bf16),
            pltpu.VMEM((tokens, width), bf16),
            dma((3,)),
            dma((LINE + 1,)),
            dma((2,)),
            dma((reach,)),
            dma((reach,)),
            dma,
            dma,
        ]
        + gather_sems(2),
        compiler_params=pltpu.CompilerParams(
            collective_id=1, has_side_effects=True, vmem_limit_bytes=VMEM_LIMIT
        ),
        name="attention",
    )(x, cot, valid, docrow, routes, gain1, gain2, wq, wk, wv, wo, wr, turns)


def greet_all(base, me, t, beyond=()):
    barrier = pltpu.get_barrier_semaphore()

    def greet(k, carry):
        peer = base + lax.rem(me + k, EXPERTS)
        pl.semaphore_signal(barrier, inc=1, device_id=(peer, t), device_id_type=MESH)
        return carry

    lax.fori_loop(1, EXPERTS, greet, 0)
    for peer in [me, *beyond]:
        pl.semaphore_signal(barrier, inc=1, device_id=(base + peer, 1 - t), device_id_type=MESH)
    pl.semaphore_wait(barrier, EXPERTS + len(beyond))


EXPERT_PLAN = {
    1: (("d", 3, 0), ("d", 3, 1)),
    3: (("hop", 1, 0),),
    5: (("hop", 1, 1),),
    8: (("hop", 2, 0),),
    10: (("hop", 2, 1), ("ds", 3, 0), ("ds", 3, 1)),
    12: (("hop", 3, 0), ("s", 1, 0), ("s", 1, 1)),
    15: (("hop", 3, 1),),
}
PAIR_PLAN = {
    1: (("s", 2, 0), ("s", 2, 1)),
    3: (("s", 3, 0), ("s", 3, 1)),
}


def moe_kernel(
    h2_ref, dy_ref, cg_ref, ct_ref, wg_ref, wu_ref, wd_ref, dyall_ref,
    opart_ref, dh2_ref, dprob_ref, grads_ref,
    h2all, dyall, ctsend, ctall, gbuf, ubuf, dbuf, rawg, rawu, wgt, wut, wdo, cat, glin, ulin, acco, acch, accp, down,
    ysend, yrecv, psend, precv, wsem, lsem, yss, yrs, cts, ctr, xsem, dsem, *sems,
):
    tokens = h2_ref.shape[0]
    ff = wdo.shape[0] // 2
    gather = Gather(h2all, sems[:7], 2, LINE)
    dy_gather = Gather(dyall, sems[7:], 2, LINE)
    base, a, b, c, t = place()
    me = a * 4 + b * 2 + c
    mine = a * 2 + c
    load = pltpu.make_async_copy(h2_ref, h2all.at[mine], lsem.at[0])
    load.start()

    def load_dy(j):
        span = pl.ds(2 * near(a, j), 2)
        return pltpu.make_async_copy(dyall_ref.at[span], dyall.at[span], dsem.at[j])

    for j in range(LINE - 1, -1, -1):
        load_dy(j).start()
    rows = jnp.broadcast_to(ct_ref[...][:, None, :], (EXPERTS, 8, tokens))
    for i in range(2 * LINE):
        for n in range(2):
            ctsend[i, n] = rows[(i // 2) * 4 + n * 2 + i % 2]
    ctall[mine] = ctsend[mine]

    def row_out(k):
        peer = lax.rem(mine + k, 2 * LINE)
        return pltpu.make_async_remote_copy(
            ctsend.at[peer], ctall.at[mine], cts.at[k], ctr.at[k],
            device_id=(base + (peer // 2) * 4 + b * 2 + lax.rem(peer, 2), t), device_id_type=MESH,
        )

    def weights(e, k):
        sides = ((wg_ref, gbuf), (wu_ref, ubuf), (wd_ref, dbuf))
        return [
            pltpu.make_async_copy(src.at[e], dst.at[k], wsem.at[i, k])
            for i, (src, dst) in enumerate(sides)
        ]

    for copy in weights(0, 0):
        copy.start()
    for j in range(LATE, LINE):
        load_dy(j).wait()
    greet_all(base, me, t)
    lax.fori_loop(1, 2 * LINE, lambda k, carry: (row_out(k).start(), carry)[1], 0)
    load.wait()
    for h in range(2):
        gather.event(0, h)
    acco[...] = jnp.zeros_like(acco)
    acch[...] = jnp.zeros_like(acch)
    accp[...] = jnp.zeros_like(accp)
    lanes = lax.broadcasted_iota(jnp.int32, (tokens, 128), 1)

    def one_expert(e, carry):
        k = lax.rem(e, 2)
        planned(gather, EXPERT_PLAN, e, dict(d=dy_gather.late, ds=dy_gather.sevent))

        @pl.when(e < EXPERTS - 1)
        def _():
            for copy in weights(e + 1, 1 - k):
                copy.start()

        for copy in weights(e, k):
            copy.wait()

        own = h2all[mine]
        g = dot_nn(own, gbuf[k])
        u = dot_nn(own, ubuf[k])
        p = dot_nt(dy_ref[...], dbuf[k])
        column = jnp.sum(jnp.where(lanes == e, cg_ref[...], 0.0), axis=1, keepdims=True)
        s = 1.0 / (1.0 + jnp.exp(-g))
        act = g * s
        hidden = act * u
        accp[...] += jnp.where(lanes == e, jnp.sum(hidden * p, axis=1, keepdims=True), 0.0)
        hc = (column * hidden).astype(bf16)
        hg = column * p
        dg = (hg * u * s * (1.0 + g * (1.0 - s))).astype(bf16)
        du = (hg * act).astype(bf16)
        acco[...] += dot_nn(hc, dbuf[k])
        acch[...] += dot_nt(dg, gbuf[k]) + dot_nt(du, ubuf[k])
        return carry

    def own_experts():
        copies = []
        for n in range(2):
            e = a * 4 + n * 2 + c
            half = pl.ds(n * ff, ff)
            copies.append(pltpu.make_async_copy(wd_ref.at[e], wdo.at[half], lsem.at[2 + n]))
            copies.append(pltpu.make_async_copy(wg_ref.at[e], rawg.at[n], lsem.at[4 + n]))
            copies.append(pltpu.make_async_copy(wu_ref.at[e], rawu.at[n], lsem.at[6 + n]))
        return copies

    for copy in own_experts():
        copy.start()
    lax.fori_loop(0, EXPERTS, one_expert, 0)
    other = (base + me, 1 - t)
    opart_ref[...] = acco[...].astype(bf16)
    ysend[...] = acch[...].astype(bf16)
    psend[...] = accp[...].T[:EXPERTS]
    swaps = [
        pltpu.make_async_remote_copy(
            src, dst, yss.at[i], yrs.at[i], device_id=other, device_id_type=MESH
        )
        for i, (src, dst) in enumerate(((ysend, yrecv), (psend, precv)))
    ]
    for copy in swaps:
        copy.start()
    lax.fori_loop(1, 2 * LINE, lambda k, carry: (row_out(k).wait(), carry)[1], 0)
    for copy in own_experts():
        copy.wait()
    for n in range(2):
        wgt[n * ff : (n + 1) * ff] = rawg[n].T
        wut[n * ff : (n + 1) * ff] = rawu[n].T

    def one_pair(j, carry):
        planned(gather, PAIR_PLAN, j, dict(d=dy_gather.late, ds=dy_gather.sevent))
        for h in range(2):
            gather.from_core(j, h)
        for q in range(2):
            s = near(a, j) * 2 + q
            h = h2all[s]
            span = pl.ds(pl.multiple_of(s * tokens, 128), tokens)
            glin[s] = dot_nt(wgt[...], h)
            ulin[s] = dot_nt(wut[...], h)
            for n in range(2):
                half = slice(n * ff, (n + 1) * ff)
                g, u = glin[s, half], ulin[s, half]
                row = ctall[s, n, 0:1, :]
                hidden = g * u / (1.0 + jnp.exp(-g))
                cat[0, half, span] = (row * hidden).astype(bf16)
        return carry

    def pull_back(s, carry):
        span = pl.ds(pl.multiple_of(s * tokens, 128), tokens)
        pull = dot_nt(wdo[...], dyall[s])
        for n in range(2):
            half = slice(n * ff, (n + 1) * ff)
            g, u = glin[s, half], ulin[s, half]
            row = ctall[s, n, 0:1, :]
            sig = 1.0 / (1.0 + jnp.exp(-g))
            hg = row * pull[half]
            cat[1, half, span] = (hg * u * sig * (1.0 + g * (1.0 - sig))).astype(bf16)
            cat[2, half, span] = (hg * g * sig).astype(bf16)
        return carry

    lax.fori_loop(0, LINE, one_pair, 0)
    width = h2all.shape[2]
    tile = 4 * (width // EXPERTS)

    def gradient(i, buf):
        def one_tile(n, carry):
            cols = pl.ds(pl.multiple_of(n * tile, 128), tile)
            right = buf[:, :, cols].reshape(2 * LINE * tokens, tile)
            block = dot_nn(cat[i], right).astype(bf16).T
            grads_ref[i, n] = block.reshape(grads_ref.shape[2:])
            return carry

        lax.fori_loop(0, LINE, one_tile, 0)

    for j in range(LATE):
        load_dy(j).wait()
    for j in range(LATE, LINE):
        for h in range(2):
            dy_gather.late_from_core(j, h)
    gradient(0, dyall)
    cross = pltpu.make_async_remote_copy(
        grads_ref.at[0, :, 1 - b], down, xsem.at[0], xsem.at[1],
        device_id=(base + a * 4 + (1 - b) * 2 + c, t), device_id_type=MESH,
    )
    cross.start()
    lax.fori_loop(0, 2 * LINE, pull_back, 0)
    gradient(1, h2all)
    gradient(2, h2all)
    cross.wait()
    for z in range(LINE):
        both = grads_ref[0, z, b].astype(f32) + down[z].astype(f32)
        grads_ref[0, z, b] = both.astype(bf16)
    for copy in swaps:
        copy.wait()
    dprob_ref[...] = psend[...] + precv[...]
    dh2_ref[...] = ysend[...].astype(f32) + yrecv[...].astype(f32)
    gather.finish()
    dy_gather.finish_late(LATE)


def moe_call(h2, dy, cg, ct, wg, wu, wd, dyall):
    tokens, width = h2.shape
    ff = wg.shape[2]
    rows = width // EXPERTS
    vmem = pl.BlockSpec(memory_space=pltpu.VMEM)
    hbm = pl.BlockSpec(memory_space=pl.ANY)
    shape = jax.ShapeDtypeStruct
    dma = pltpu.SemaphoreType.DMA
    return pl.pallas_call(
        moe_kernel,
        out_shape=(
            shape((tokens, width), bf16),
            shape((tokens, width), f32),
            shape((EXPERTS, tokens), f32),
            shape((3, LINE, 2, 2, rows, 2 * ff), bf16),
        ),
        in_specs=[hbm, vmem, vmem, vmem, hbm, hbm, hbm, hbm],
        out_specs=(vmem, vmem, vmem, vmem),
        scratch_shapes=[
            pltpu.VMEM((2 * LINE, tokens, width), bf16),
            pltpu.VMEM((2 * LINE, tokens, width), bf16),
            pltpu.VMEM((2 * LINE, 2, 8, tokens), f32),
            pltpu.VMEM((2 * LINE, 2, 8, tokens), f32),
            pltpu.VMEM((2, width, ff), bf16),
            pltpu.VMEM((2, width, ff), bf16),
            pltpu.VMEM((2, ff, width), bf16),
            pltpu.VMEM((2, width, ff), bf16),
            pltpu.VMEM((2, width, ff), bf16),
            pltpu.VMEM((2 * ff, width), bf16),
            pltpu.VMEM((2 * ff, width), bf16),
            pltpu.VMEM((2 * ff, width), bf16),
            pltpu.VMEM((3, 2 * ff, 2 * LINE * tokens), bf16),
            pltpu.VMEM((2 * LINE, 2 * ff, tokens), f32),
            pltpu.VMEM((2 * LINE, 2 * ff, tokens), f32),
            pltpu.VMEM((tokens, width), f32),
            pltpu.VMEM((tokens, width), f32),
            pltpu.VMEM((tokens, 128), f32),
            pltpu.VMEM((LINE, 2, rows, 2 * ff), bf16),
            pltpu.VMEM((tokens, width), bf16),
            pltpu.VMEM((tokens, width), bf16),
            pltpu.VMEM((EXPERTS, tokens), f32),
            pltpu.VMEM((EXPERTS, tokens), f32),
            dma((3, 2)),
            dma((8,)),
            dma((2,)),
            dma((2,)),
            dma((2 * LINE,)),
            dma((2 * LINE,)),
            dma((2,)),
            dma((LINE,)),
        ]
        + gather_sems(2)
        + gather_sems(2),
        compiler_params=pltpu.CompilerParams(
            collective_id=0, has_side_effects=True, vmem_limit_bytes=VMEM_LIMIT
        ),
        name="moe",
    )(h2, dy, cg, ct, wg, wu, wd, dyall)


class Scatter:
    def __init__(self, bufs, sems):
        self.part, self.cbuf, self.keep, self.xbuf, self.last, self.zbuf = bufs
        self.csem, self.xsem, self.zsend, self.zrecv = sems
        self.base, self.a, self.b, self.c, self.t = place()

    def target(self, a, b, c):
        return (self.base + a * 4 + b * 2 + c, self.t)

    def core(self):
        return pltpu.make_async_remote_copy(
            self.part.at[:, 1 - self.c], self.cbuf, self.csem.at[0], self.csem.at[1],
            device_id=self.target(self.a, self.b, 1 - self.c), device_id_type=MESH,
        )

    def cross(self):
        return pltpu.make_async_remote_copy(
            self.keep.at[:, 1 - self.b], self.xbuf, self.xsem.at[0], self.xsem.at[1],
            device_id=self.target(self.a, 1 - self.b, self.c), device_id_type=MESH,
        )

    def along(self, k):
        z = lax.rem(self.a + k, LINE)
        return pltpu.make_async_remote_copy(
            self.last.at[z], self.zbuf.at[k - 1], self.zsend.at[k - 1], self.zrecv.at[k - 1],
            device_id=self.target(z, self.b, self.c), device_id_type=MESH,
        )

    def start(self):
        self.core().start()

    def second(self):
        self.core().wait()

        def add(i, carry):
            for j in range(2):
                mine = self.part[2 * i + j, self.c].astype(f32)
                self.keep[i, j] = (mine + self.cbuf[2 * i + j].astype(f32)).astype(bf16)
            return carry

        lax.fori_loop(0, LINE, add, 0)
        self.cross().start()

    def third(self):
        self.cross().wait()

        def add(i, carry):
            mine = self.keep[i, self.b].astype(f32)
            self.last[i] = (mine + self.xbuf[i].astype(f32)).astype(bf16)
            return carry

        lax.fori_loop(0, LINE, add, 0)
        for k in range(1, LINE):
            self.along(k).start()

    def total(self):
        result = self.last[self.a].astype(f32)
        for k in range(1, LINE):
            self.along(k).wait_recv()
            result = result + self.zbuf[k - 1].astype(f32)
        return result

    def finish(self):
        for k in range(1, LINE):
            self.along(k).wait_send()

    def put(self, matrix, columns):
        def some(i, carry):
            block = dot_nn(matrix[i], columns).astype(bf16)
            self.part[pl.ds(2 * i, 2)] = block.reshape((2,) + self.part.shape[1:])
            return carry

        lax.fori_loop(0, 4, some, 0)


def scatter_bufs(rows, columns):
    shapes = [(8, 2), (8,), (4, 2), (4,), (4,), (3,)]
    return [pltpu.VMEM(s + (rows, columns), bf16) for s in shapes]


def scatter_sems():
    dma = pltpu.SemaphoreType.DMA
    return [dma((2,)), dma((2,)), dma((LINE - 1,)), dma((LINE - 1,))]


def back_kernel(
    grads_ref, opart_ref, dh2_ref, dprob_ref, router_ref, routes_ref, h2_ref, middle_ref, x_ref, dy_ref,
    gain1_ref, gain2_ref, wr_ref, mixed_ref, mixedt_ref, q_ref, kv_ref, lse_ref, docrow_ref,
    turns_ref, wq_ref, wk_ref, wv_ref, wo_ref,
    output_ref, dtok_ref, experts_ref, out_ref, query_ref, rest_ref,
    turns, wq, wk, wv, kheads, vheads, kt, qstack, qt, dmixt, dmixstack, delta, bias, wcat, scat, dqt,
    coresend, corerecv, pairsend, pairrecv, linesend, linerecv, parts, rowst, mgrad, ysend, yrecv, orecv, gbuf, summed, crossed,
    wsem, asend, arecv, lsem, csem, kvs, kvr, ysem, gsem, *rest,
):
    tokens, width = x_ref.shape
    reach = kv_ref.shape[0] - 1
    assert (reach, ROW_LENGTH // tokens) == (4, 8)
    row_blocks = ROW_LENGTH // tokens
    kv_width = wk_ref.shape[1]
    kv_heads = kv_width // HEAD_SIZE
    q_width = wq_ref.shape[1]
    group = q_width // kv_width
    rows = width // EXPERTS
    keys = (reach + 1) * tokens
    outs = Scatter(rest[0:6], rest[23:27])
    q_low = Scatter(rest[6:12], rest[27:31])
    q_high = Scatter(rest[6:7] + rest[12:17], rest[31:35])
    tail = Scatter(rest[17:23], rest[35:39])
    base, a, b, c, t = place()
    me = a * 4 + b * 2 + c
    dp = base + me
    at = lax.rem(dp, row_blocks)
    loads = [
        pltpu.make_async_copy(src, dst, wsem.at[i])
        for i, (src, dst) in enumerate(((wq_ref, wq), (wk_ref, wk), (wv_ref, wv)))
    ]
    for copy in loads:
        copy.start()
    load_turns = pltpu.make_async_copy(
        turns_ref.at[pl.ds(pl.multiple_of(at * tokens, tokens), tokens)], turns, wsem.at[4]
    )
    load_turns.start()
    load_dh2 = pltpu.make_async_copy(dh2_ref, mgrad, wsem.at[3])
    load_dh2.start()
    greet_all(base, me, t, [lax.rem(a + k, LINE) * 4 + b * 2 + c for k in range(1, LINE)])

    def deal(p, k, n):
        z, core = lax.rem(a + k, LINE), lax.rem(c + n, 2)
        source = grads_ref.at[0, z, b, core] if p == 0 else summed.at[p - 1, z, core]
        return pltpu.make_async_remote_copy(
            source, experts_ref.at[a * 2 + c, p], asend.at[p, 2 * k + n], arecv.at[p, 2 * k + n],
            device_id=(base + z * 4 + b * 2 + core, t), device_id_type=MESH,
        )

    def keep_own(p):
        source = grads_ref.at[0, a, b, c] if p == 0 else summed.at[p - 1, a, c]
        return pltpu.make_async_copy(source, experts_ref.at[a * 2 + c, p], lsem.at[p])

    places = [(k, n) for k in range(LINE) for n in range(2) if k or n]

    def deal_out(p):
        keep_own(p).start()
        for k, n in places:
            deal(p, k, n).start()

    def half_load(p):
        return pltpu.make_async_copy(grads_ref.at[p, :, b], summed.at[p - 1], lsem.at[2 + p])

    def cross(p):
        return pltpu.make_async_remote_copy(
            grads_ref.at[p, :, 1 - b], crossed.at[p - 1], csem.at[0, p - 1], csem.at[1, p - 1],
            device_id=(base + a * 4 + (1 - b) * 2 + c, t), device_id_type=MESH,
        )

    def merge(p):
        half_load(p).wait()
        cross(p).wait()

        def add(z, carry):
            for n in range(2):
                both = summed[p - 1, z, n].astype(f32) + crossed[p - 1, z, n].astype(f32)
                summed[p - 1, z, n] = both.astype(bf16)
            return carry

        lax.fori_loop(0, LINE, add, 0)
        deal_out(p)

    cross(1).start()
    half_load(1).start()
    half_load(2).start()
    deal_out(0)
    swap_out = pltpu.make_async_remote_copy(
        opart_ref, orecv, ysem.at[4], ysem.at[5], device_id=(dp, 1 - t), device_id_type=MESH
    )
    swap_out.start()

    router = router_ref[...]
    dprob = jnp.concatenate([dprob_ref[...], jnp.zeros((128 - EXPERTS, tokens), f32)], axis=0).T
    dprob = jnp.where(named(routes_ref), dprob, 0.0)
    dlogits = router * (dprob - jnp.sum(dprob * router, axis=1, keepdims=True))
    dlogits = dlogits.astype(bf16)
    load_dh2.wait()
    grad = mgrad[...] + dot_nn(dlogits, router_rows(wr_ref))
    middle = middle_ref[...]
    inverse = lax.rsqrt(jnp.mean(middle * middle, axis=1, keepdims=True) + norm_eps)
    scaled = grad * as_row(gain2_ref)
    inner = jnp.mean(scaled * middle, axis=1, keepdims=True)
    normed = middle * inverse
    dgain2 = jnp.sum(grad * normed, axis=0, keepdims=True)
    middle_grad = dy_ref[...].astype(f32) + (
        inverse * scaled - normed * (inverse * inverse) * inner
    )
    mgrad[...] = middle_grad
    attn_grad = middle_grad.astype(bf16)
    rowst[...] = attn_grad.T.reshape(rowst.shape)

    outs.put(rowst, mixed_ref[...])
    outs.start()
    dmix_t = dot_nt(wo_ref[...], attn_grad).astype(bf16)
    dmix = dmix_t.T
    both = (dmix_t.astype(f32) * mixedt_ref[...].astype(f32)).reshape(
        kv_heads * group, HEAD_SIZE, tokens
    )
    delta[: kv_heads * group] = jnp.sum(both, axis=1)
    small = jnp.concatenate(
        [dot_nn(dlogits.T, h2_ref[...])[:EXPERTS], dgain2, jnp.zeros((7, width), f32)], axis=0
    )

    q = (q_ref[...].astype(f32) * HEAD_SIZE**-0.5).astype(bf16)
    q_t = q.T
    for i in range(kv_heads):
        for n in range(group):
            head = i * group + n
            cols = slice(HEAD_SIZE * head, HEAD_SIZE * (head + 1))
            span = slice(n * tokens, (n + 1) * tokens)
            qstack[i, span] = q[:, cols]
            qt[head] = q_t[cols]
            dmixstack[i, span] = dmix[:, cols]
            dmixt[head] = dmix_t[cols]
    for d in range(reach, -1, -1):
        s = reach - d
        far = (
            lax.broadcasted_iota(jnp.int32, (tokens, tokens), 1)
            - lax.broadcasted_iota(jnp.int32, (tokens, tokens), 0)
            + d * tokens
        )
        tags = kv_ref[s, tokens:, :tokens].T[:, :1].astype(f32)
        allowed = (tags == docrow_ref[...].astype(f32)) & (far >= 0) & (far < WINDOW)
        allowed = allowed & (at >= d)
        span = slice(s * tokens, (s + 1) * tokens)
        bias[span] = jnp.where(allowed, 0.0, masked_score)
        k_t = kv_ref[s, :tokens, :kv_width].T
        for i in range(kv_heads):
            cols = slice(HEAD_SIZE * i, HEAD_SIZE * (i + 1))
            kheads[i, span] = kv_ref[s, :tokens, cols]
            vheads[i, span] = kv_ref[
                s, :tokens, kv_width + HEAD_SIZE * i : kv_width + HEAD_SIZE * (i + 1)
            ]
            kt[i, :, span] = k_t[cols]

    def shared(k):
        z = lax.rem(a + k, LINE)
        return pltpu.make_async_remote_copy(
            tail.last.at[z, :, pl.ds(2 * kv_width, 128)], gbuf.at[k], gsem.at[0, k], gsem.at[1, k],
            device_id=(base + z * 4 + b * 2 + c, 1 - t), device_id_type=MESH,
        )

    def by_core(n, i):
        return pltpu.make_async_remote_copy(
            coresend.at[n, i], corerecv.at[n, i], kvs.at[n, i], kvr.at[n, i],
            device_id=(base + a * 4 + b * 2 + 1 - c, t), device_id_type=MESH,
        )

    def by_pair(i):
        return pltpu.make_async_remote_copy(
            pairsend.at[i], pairrecv.at[i], kvs.at[2, i], kvr.at[2, i],
            device_id=(base + a * 4 + (1 - b) * 2 + c, t), device_id_type=MESH,
        )

    def by_line(i):
        return pltpu.make_async_remote_copy(
            linesend.at[i], linerecv.at[i], kvs.at[3, i], kvr.at[3, i],
            device_id=(dp - 4, t), device_id_type=MESH,
        )

    pair_sends = (b == 1) | (at >= 4)
    pair_takes = (b == 0) | (at >= 4)

    def after_core(i):
        for n in range(2):
            there = (c == 0) | (at >= 2 + 2 * n)
            if n:
                there = there & (at >= 2)

            @pl.when(there)
            def _():
                by_core(n, i).wait_recv()
                share = corerecv[n, i].astype(f32)

                @pl.when(c == 0)
                def _():
                    parts[n, i] = parts[n, i] + share

                @pl.when(c == 1)
                def _():
                    parts[n + 1, i] = parts[n + 1, i] + share

        @pl.when(pair_sends)
        def _():
            pairsend[i] = parts[1, i].astype(bf16)
            by_pair(i).start()

    def after_pair(i):
        @pl.when(pair_takes)
        def _():
            by_pair(i).wait_recv()
            share = pairrecv[i].astype(f32)

            @pl.when(b == 0)
            def _():
                parts[0, i] = parts[0, i] + share

            @pl.when(b == 1)
            def _():
                parts[2, i] = parts[2, i] + share

        @pl.when(at >= 4)
        def _():
            linesend[i] = parts[2, i].astype(bf16)
            by_line(i).start()

    def one_kv(i, carry):
        for n in range(group):
            head = i * group + n
            scores = dot_nn(kheads[i], qt[head]) + bias[...]
            weights = jnp.exp(scores - lse_ref[pl.ds(head, 1), :])
            pulled = dot_nn(vheads[i], dmixt[head])
            cols = slice(n * tokens, (n + 1) * tokens)
            wcat[:, cols] = weights.astype(bf16)
            scat[:, cols] = (weights * (pulled - delta[pl.ds(head, 1), :])).astype(bf16)
        dv = dot_nn(wcat[...], dmixstack[i])
        dk = dot_nn(scat[...], qstack[i])
        dq = dot_nn(kt[i], scat[...])
        for n in range(group):
            dqt[i * group + n] = dq[:, n * tokens : (n + 1) * tokens]
        dkv = jnp.concatenate([dk, dv], axis=1)
        for d in range(reach + 1):
            share = dkv[(reach - d) * tokens : (reach - d + 1) * tokens]
            if d % 2:
                coresend[d // 2, i] = share.astype(bf16)

                @pl.when(at >= d)
                def _():
                    by_core(d // 2, i).start()
            else:
                parts[d // 2, i] = share

        @pl.when(i >= 1)
        def _():
            after_core(i - 1)

        @pl.when(i == 1)
        def _():
            outs.second()

        @pl.when(i == 3)
        def _():
            q_low.second()
            merge(1)

        return carry

    load_turns.wait()
    cosine, sine = turns[:, :128], turns[:, 128:]
    x = x_ref[...].astype(f32)
    inverse1 = lax.rsqrt(jnp.mean(x * x, axis=1, keepdims=True) + norm_eps)
    normed1 = x * inverse1
    rowst[...] = (normed1 * as_row(gain1_ref)).astype(bf16).T.reshape(rowst.shape)
    half = kv_heads // 2
    half_width = q_width // 2

    def query_grad(first):
        heads = dqt[first * group : (first + half) * group]
        grad = heads.reshape(half_width, tokens).T * HEAD_SIZE**-0.5
        return rotated(grad, cosine, -sine).astype(bf16)

    lax.fori_loop(0, half, one_kv, 0)
    low = query_grad(0)
    q_low.put(rowst, low)
    q_low.start()
    lax.fori_loop(half, kv_heads, one_kv, 0)
    high = query_grad(half)
    q_high.put(rowst, high)
    q_high.start()
    after_core(kv_heads - 1)
    swap_out.wait()
    total = opart_ref[...].astype(f32) + orecv[...].astype(f32)
    output_ref[...] = (middle_ref[...] + total).astype(bf16)
    for copy in loads:
        copy.wait()
    back = dot_nt(low, wq[:, :half_width]) + dot_nt(high, wq[:, half_width:])
    q_high.second()
    cross(2).start()
    for i in range(kv_heads):
        after_pair(i)
    outs.third()
    for i in range(kv_heads):
        @pl.when(at + 4 < row_blocks)
        def _():
            by_line(i).wait_recv()
            parts[0, i] = parts[0, i] + linerecv[i].astype(f32)

    dk = jnp.concatenate([parts[0, i, :, :HEAD_SIZE] for i in range(kv_heads)], axis=1)
    dv = jnp.concatenate([parts[0, i, :, HEAD_SIZE:] for i in range(kv_heads)], axis=1)
    dkl = rotated(dk, cosine, -sine).astype(bf16)
    dvl = dv.astype(bf16)
    back = back + dot_nt(dkl, wk[...]) + dot_nt(dvl, wv[...])
    ysend[...] = back.astype(bf16)
    swap = pltpu.make_async_remote_copy(
        ysend, yrecv, ysem.at[0], ysem.at[1], device_id=(dp, 1 - t), device_id_type=MESH
    )
    swap.start()
    dgain1 = jnp.sum(back * normed1, axis=0, keepdims=True)
    row = lax.broadcasted_iota(jnp.int32, small.shape, 0)
    small = jnp.where(row == EXPERTS + 1, dgain1, small)
    small = jnp.concatenate([small, jnp.zeros((128 - small.shape[0], width), f32)], axis=0)
    small_t = small.T.astype(bf16)
    for i in range(4):
        block = jnp.concatenate(
            [dot_nn(rowst[i], dkl).astype(bf16), dot_nn(rowst[i], dvl).astype(bf16),
             small_t[i * 4 * rows : (i + 1) * 4 * rows]],
            axis=1,
        )
        tail.part[2 * i : 2 * i + 2] = block.reshape(2, 2, rows, 2 * kv_width + 128)
    tail.start()
    q_low.third()
    tail.second()
    q_high.third()
    out_ref[...] = outs.total()
    swap.wait()
    grad = ysend[...].astype(f32) + yrecv[...].astype(f32)
    scaled = grad * as_row(gain1_ref)
    inner = jnp.mean(scaled * x, axis=1, keepdims=True)
    step = inverse1 * scaled - normed1 * (inverse1 * inverse1) * inner
    dtok_ref[...] = (mgrad[...] + step).astype(bf16)
    merge(2)
    tail.third()
    for k in range(LINE):
        shared(k).start()
    query_ref[:, :half_width] = q_low.total()
    query_ref[:, half_width:] = q_high.total()
    sums = tail.total()
    rest_ref[...] = sums
    both = sums[:, 2 * kv_width :]
    for k in range(LINE):
        shared(k).wait_recv()
        both = both + gbuf[k].astype(f32)
    lane = lax.broadcasted_iota(jnp.int32, (rows, 128), 1)
    rest_ref[:, 2 * kv_width :] = jnp.where(lane == EXPERTS + 1, both, sums[:, 2 * kv_width :])
    for p in range(3):
        keep_own(p).wait()
        for k, n in places:
            deal(p, k, n).wait()
    for i in range(kv_heads):
        for n in range(2):
            @pl.when(at >= 1 + 2 * n)
            def _():
                by_core(n, i).wait_send()

        @pl.when(pair_sends)
        def _():
            by_pair(i).wait_send()

        @pl.when(at >= 4)
        def _():
            by_line(i).wait_send()

    for k in range(LINE):
        shared(k).wait_send()
    for s in (outs, q_low, q_high, tail):
        s.finish()


def back_call(grads, opart, dh2, dprob, router, routes, h2, middle, x, dy, gain1, gain2, wr, mixed, mixedt,
              q, kv, lse, docrow, turns, wq, wk, wv, wo):
    tokens, width = x.shape
    q_width, kv_width = wq.shape[1], wk.shape[1]
    heads, kv_heads = q_width // HEAD_SIZE, kv_width // HEAD_SIZE
    group = heads // kv_heads
    reach = kv.shape[0] - 1
    keys = (reach + 1) * tokens
    rows = width // EXPERTS
    ff = grads.shape[-1]
    vmem = pl.BlockSpec(memory_space=pltpu.VMEM)
    hbm = pl.BlockSpec(memory_space=pl.ANY)
    shape = jax.ShapeDtypeStruct
    dma = pltpu.SemaphoreType.DMA
    return pl.pallas_call(
        back_kernel,
        out_shape=(
            shape((tokens, width), bf16),
            shape((tokens, width), bf16),
            shape((2 * LINE, 3, rows, ff), bf16),
            shape((rows, q_width), f32),
            shape((rows, q_width), f32),
            shape((rows, 2 * kv_width + 128), f32),
        ),
        in_specs=[hbm, vmem, hbm] + [vmem] * 16 + [hbm, hbm, hbm, hbm, vmem],
        out_specs=(vmem, vmem, hbm, vmem, vmem, vmem),
        scratch_shapes=[
            pltpu.VMEM((tokens, 256), f32),
            pltpu.VMEM((width, q_width), bf16),
            pltpu.VMEM((width, kv_width), bf16),
            pltpu.VMEM((width, kv_width), bf16),
            pltpu.VMEM((kv_heads, keys, HEAD_SIZE), bf16),
            pltpu.VMEM((kv_heads, keys, HEAD_SIZE), bf16),
            pltpu.VMEM((kv_heads, HEAD_SIZE, keys), bf16),
            pltpu.VMEM((kv_heads, group * tokens, HEAD_SIZE), bf16),
            pltpu.VMEM((heads, HEAD_SIZE, tokens), bf16),
            pltpu.VMEM((heads, HEAD_SIZE, tokens), bf16),
            pltpu.VMEM((kv_heads, group * tokens, HEAD_SIZE), bf16),
            pltpu.VMEM((16, tokens), f32),
            pltpu.VMEM((keys, tokens), f32),
            pltpu.VMEM((keys, group * tokens), bf16),
            pltpu.VMEM((keys, group * tokens), bf16),
            pltpu.VMEM((heads, HEAD_SIZE, tokens), f32),
            pltpu.VMEM((2, kv_heads, tokens, 128), bf16),
            pltpu.VMEM((2, kv_heads, tokens, 128), bf16),
            pltpu.VMEM((kv_heads, tokens, 128), bf16),
            pltpu.VMEM((kv_heads, tokens, 128), bf16),
            pltpu.VMEM((kv_heads, tokens, 128), bf16),
            pltpu.VMEM((kv_heads, tokens, 128), bf16),
            pltpu.VMEM((3, kv_heads, tokens, 128), f32),
            pltpu.VMEM((4, width // 4, tokens), bf16),
            pltpu.VMEM((tokens, width), f32),
            pltpu.VMEM((tokens, width), bf16),
            pltpu.VMEM((tokens, width), bf16),
            pltpu.VMEM((tokens, width), bf16),
            pltpu.VMEM((LINE, rows, 128), bf16),
            pltpu.VMEM((2, LINE, 2, rows, ff), bf16),
            pltpu.VMEM((2, LINE, 2, rows, ff), bf16),
            dma((5,)),
            dma((3, 2 * LINE)),
            dma((3, 2 * LINE)),
            dma((5,)),
            dma((2, 2)),
            dma((reach, kv_heads)),
            dma((reach, kv_heads)),
            dma((6,)),
            dma((2, LINE)),
        ]
        + scatter_bufs(rows, q_width)
        + scatter_bufs(rows, q_width // 2)
        + scatter_bufs(rows, q_width // 2)[1:]
        + scatter_bufs(rows, 2 * kv_width + 128)
        + scatter_sems() * 4,
        compiler_params=pltpu.CompilerParams(
            collective_id=2, has_side_effects=True, vmem_limit_bytes=VMEM_LIMIT
        ),
        name="backward",
    )(grads, opart, dh2, dprob, router, routes, h2, middle, x, dy, gain1, gain2, wr, mixed, mixedt,
      q, kv, lse, docrow, turns, wq, wk, wv, wo)


def rope_table():
    half = HEAD_SIZE // 2
    freqs = rope_base ** (-2.0 * np.arange(half) / HEAD_SIZE)
    angle = np.arange(ROW_LENGTH)[:, None] * freqs[None, :]
    cosine, sine = np.cos(angle), np.sin(angle)
    table = np.concatenate([cosine] * 4 + [-sine, sine] * 2, axis=1)
    return jnp.asarray(table, dtype=f32)


def final_kernel(
    output_ref, dtok_ref, experts_ref, dout_ref, query_ref, rest_ref,
    o_output, o_dtok, o_gain1, o_gain2, o_query, o_key, o_value, o_out, o_router, o_gate, o_up,
    o_down,
):
    o_output[...] = output_ref[...]
    o_dtok[...] = dtok_ref[...]
    ff = o_gate.shape[-1]
    for n in range(2):
        cols = slice(n * ff, (n + 1) * ff)
        o_down[0, n, 0] = experts_ref[0, 0, :, cols].astype(f32)
        o_gate[0, n, 0] = experts_ref[0, 1, :, cols].astype(f32)
        o_up[0, n, 0] = experts_ref[0, 2, :, cols].astype(f32)

    @pl.when((pl.program_id(0) == 0) & (pl.program_id(1) == 0))
    def _():
        kv_width = o_key.shape[1]
        o_query[...] = query_ref[...]
        o_out[...] = dout_ref[...]
        rest = rest_ref[...]
        o_key[...] = rest[:, :kv_width]
        o_value[...] = rest[:, kv_width : 2 * kv_width]
        small = rest[:, 2 * kv_width :]
        small = small.T
        o_router[...] = small[:EXPERTS]
        o_gain2[...] = small[EXPERTS : EXPERTS + 1]
        o_gain1[...] = small[EXPERTS + 1 : EXPERTS + 2]


def final_call(output, dtok, experts, dout, query, rest):
    tokens, width = output.shape
    rows, q_width = query.shape
    kv_width = (rest.shape[1] - 128) // 2
    ff = experts.shape[3] // 2
    piece = tokens // (2 * LINE)
    shape = jax.ShapeDtypeStruct
    whole = lambda *dims: pl.BlockSpec(dims, lambda z, c: (0,) * len(dims))
    strip = pl.BlockSpec((piece, width), lambda z, c: (2 * z + c, 0))
    each = lambda *dims: pl.BlockSpec((1, 2, 1) + dims, lambda z, c: (z, 0, c, 0, 0))
    outs = pl.pallas_call(
        final_kernel,
        grid=(LINE, 2),
        out_shape=(
            shape((tokens, width), bf16),
            shape((tokens, width), bf16),
            shape((1, rows), f32),
            shape((1, rows), f32),
            shape((rows, q_width), f32),
            shape((rows, kv_width), f32),
            shape((rows, kv_width), f32),
            shape((rows, q_width), f32),
            shape((EXPERTS, rows), f32),
            shape((LINE, 2, 2, rows, ff), f32),
            shape((LINE, 2, 2, rows, ff), f32),
            shape((LINE, 2, 2, rows, ff), f32),
        ),
        in_specs=[
            strip,
            strip,
            pl.BlockSpec((1, 3, rows, 2 * ff), lambda z, c: (2 * z + c, 0, 0, 0)),
            whole(rows, q_width),
            whole(rows, q_width),
            whole(rows, 2 * kv_width + 128),
        ],
        out_specs=(
            strip,
            strip,
            whole(1, rows),
            whole(1, rows),
            whole(rows, q_width),
            whole(rows, kv_width),
            whole(rows, kv_width),
            whole(rows, q_width),
            whole(EXPERTS, rows),
            each(rows, ff),
            each(rows, ff),
            each(rows, ff),
        ),
        compiler_params=pltpu.CompilerParams(vmem_limit_bytes=VMEM_LIMIT),
        name="final",
    )(output, dtok, experts, dout, query, rest)
    outs = list(outs)
    outs[2], outs[3] = outs[2].reshape(rows), outs[3].reshape(rows)
    for i in range(9, 12):
        outs[i] = outs[i].reshape((EXPERTS,) + outs[i].shape[3:])
    outs[7], outs[8], outs[11] = outs[7].T, outs[8].T, jnp.swapaxes(outs[11], 1, 2)
    return tuple(outs)


def own_rows(block, axis):
    size = lax.axis_size("dp")
    groups = size // EXPERTS
    if groups == 1:
        return block
    members = [[r * EXPERTS + m for m in range(EXPERTS)] for r in range(groups)]
    across = [[r * EXPERTS + m for r in range(groups)] for m in range(EXPERTS)]
    block = jnp.moveaxis(block, axis, 0).astype(bf16)
    full = lax.all_gather(block, "dp", axis=0, tiled=True, axis_index_groups=members)
    full = full.reshape((groups, EXPERTS, full.shape[0] // size) + full.shape[1:])
    member = lax.rem(lax.axis_index("dp"), EXPERTS)
    mine = lax.dynamic_index_in_dim(full, member, 1, keepdims=False).astype(f32)
    mine = lax.psum_scatter(
        mine, "dp", scatter_dimension=0, tiled=False, axis_index_groups=across
    )
    return jnp.moveaxis(mine, 0, axis)


def per_device(
    tokens,
    cotangent,
    document_numbers,
    valid,
    routes,
    gain_attn,
    gain_moe,
    w_query,
    key_weight,
    value_weight,
    w_out,
    w_router,
    w_gate,
    w_up,
    w_down,
):
    turns = rope_table()
    router_w = w_router.T
    tags = document_numbers[None, :]
    names = routes.T
    (
        h2, middle, router, gates, gates_t, query_rows, kv, lse, mixed, mixed_t, dy, all_dy
    ) = attn_call(
        tokens, cotangent, valid[None, :], tags, names, gain_attn, gain_moe,
        w_query, key_weight, value_weight, w_out, router_w, turns,
    )
    opart, dh2, dprob, grads = moe_call(
        h2, dy, gates, gates_t, w_gate, w_up, w_down,
        all_dy,
    )
    output, d_tokens, experts, d_out, d_query, rest = back_call(
        grads, opart, dh2, dprob, router, names, h2, middle, tokens, dy, gain_attn, gain_moe,
        router_w, mixed, mixed_t, query_rows, kv, lse, tags, turns,
        w_query, key_weight, value_weight, w_out,
    )
    return final_call(
        output, d_tokens, own_rows(experts, 2), own_rows(d_out, 0), own_rows(d_query, 0),
        own_rows(rest, 0),
    )


def solution(mesh):
    in_specs = (
        P("dp", None),
        P("dp", None),
        P("dp"),
        P("dp"),
        P("dp", None),
        P(),
        P(),
        P(None, "tensor"),
        P(None, "tensor"),
        P(None, "tensor"),
        P("tensor", None),
        P(),
        P(None, None, "tensor"),
        P(None, None, "tensor"),
        P(None, "tensor", None),
    )
    out_specs = (
        P("dp", None),
        P("dp", None),
        P("dp"),
        P("dp"),
        P("dp", "tensor"),
        P("dp", "tensor"),
        P("dp", "tensor"),
        P("tensor", "dp"),
        P("dp", None),
        P(None, "dp", "tensor"),
        P(None, "dp", "tensor"),
        P(None, "tensor", "dp"),
    )
    return jax.shard_map(
        per_device, mesh=mesh, in_specs=in_specs, out_specs=out_specs, check_vma=False
    )
```
